128 devices in a mesh: dp: 32 (over x, z, core), mp: 4 (over y).
Axes of the slice: x: 4, y: 4, z: 4, core: 2. Of those that a mesh axis runs over, the one named last changes fastest.
Arguments:
- states: bfloat16 [8192, 2048], P('dp'), may hold values from -6 to 6
- w_query: bfloat16 [2048, 2048], P(None, 'mp'), may hold values from -0.125 to 0.125
- w_key: bfloat16 [2048, 2048], P(None, 'mp'), may hold values from -0.125 to 0.125
- w_value: bfloat16 [2048, 2048], P(None, 'mp'), may hold values from -0.125 to 0.125
- w_out: bfloat16 [2048, 2048], P('mp'), may hold values from -0.125 to 0.125
- w_gate: bfloat16 [2048, 8192], P(None, 'mp'), may hold values from -0.125 to 0.125
- w_up: bfloat16 [2048, 8192], P(None, 'mp'), may hold values from -0.125 to 0.125
- w_down: bfloat16 [8192, 2048], P('mp'), may hold values from -0.0625 to 0.0625
- q_gain: float32 [2048], P('mp'), may hold values from 0.1 to 1.9
- k_gain: float32 [2048], P('mp'), may hold values from 0.1 to 1.9
- attn_gain: float32 [2048], replicated, may hold values from 0.1 to 1.9
- mlp_gain: float32 [2048], replicated, may hold values from 0.1 to 1.9
- cotangent: bfloat16 [8192, 2048], P('dp'), may hold values from -6 to 6
- segments: int32 [8192], replicated, may hold values from 0 to 13, as said below
- sources: int32 [8192], P('dp'), may hold values from 0 to 7
- group_weights: int32 [8], replicated, may hold values from 4 to 32
Outputs:
- output: bfloat16 [8192, 2048], P('dp')
- grad_states: float32 [8192, 2048], P('dp')
- grad_query: float32 [2048, 2048], P('dp', 'mp')
- grad_key: float32 [2048, 2048], P('dp', 'mp')
- grad_value: float32 [2048, 2048], P('dp', 'mp')
- grad_out: float32 [2048, 2048], P('mp', 'dp')
- grad_gate: float32 [2048, 8192], P('dp', 'mp')
- grad_up: float32 [2048, 8192], P('dp', 'mp')
- grad_down: float32 [8192, 2048], P('mp', 'dp')
- grad_q_gain: float32 [2048], P('mp')
- grad_k_gain: float32 [2048], P('mp')
- grad_attn_gain: float32 [2048], replicated
- grad_mlp_gain: float32 [2048], replicated
The draws below stay inside these ranges and needn't reach their ends.
Inputs may be any that keep to these rules, and one draw needn't show every extreme that they name: `segments`: document ids never fall along the tokens; a new document begins at every multiple of 4096; a sequence holds at most seven documents; in each sequence one document runs from its first 256 tokens into its last 256.
All inputs are finite; a program needn't handle non-finite values.
Results may differ from the reference program's by a relative error of at most 0.035.
Values may be sent and summed in bfloat16 or wider, within the bound.
No kernel may reach another device: no remote copies, remote signals or barrier semaphores. Data moves between devices by JAX's collectives and lax.ppermute only.
A program may use at most 320 MiB of HBM per device.

```python
import math
import jax
import jax.numpy as jnp
import numpy as np
from jax import lax

D = 2048
HEADS = 16
HD = 128
FF = 8192
TOK_DEV = 256
SOURCES = 8
TOKENS = 8192
SEQ = 4096


def draw_segments(key, part):
    key = jax.random.fold_in(key, 7)
    subkeys = jax.random.split(key, 6)
    count = TOKENS // SEQ
    long_start = jax.random.randint(subkeys[0], (count,), 1, TOK_DEV)
    front_one = jax.random.randint(subkeys[1], (count,), 1, long_start + 1)
    front_two = jax.random.randint(subkeys[2], (count,), 1, long_start + 1)
    finish = SEQ - jax.random.randint(subkeys[3], (count,), 1, TOK_DEV)
    back_one = jax.random.randint(subkeys[4], (count,), finish, SEQ)
    back_two = jax.random.randint(subkeys[5], (count,), finish, SEQ)
    positions = jnp.arange(TOKENS, dtype=jnp.int32)
    which = positions // SEQ
    local = positions % SEQ
    segment_ids = 7 * which + (local >= front_one[which]).astype(jnp.int32) + (local >= front_two[which]).astype(jnp.int32)
    segment_ids = segment_ids + (local >= long_start[which]).astype(jnp.int32) + (local >= finish[which]).astype(jnp.int32)
    segment_ids = segment_ids + (local >= back_one[which]).astype(jnp.int32) + (local >= back_two[which]).astype(jnp.int32)
    return segment_ids.astype(jnp.int32)


def with_ends(drawn, rng, smallest, largest):
    extent = drawn.shape
    index_at = [jax.random.randint(jax.random.fold_in(rng, axis), (), 0, extent[axis]) for axis in range(len(extent))]
    drawn = drawn.at[tuple(index_at)].set(smallest)
    longest = extent.index(max(extent))
    index_at[longest] = (index_at[longest] + 1) % extent[longest]
    return drawn.at[tuple(index_at)].set(largest)


def strengthened(entries, stream_key, source, target, blocks, factor):
    owner, partner = [(jnp.arange(entries.shape[dim]) // (entries.shape[dim] // blocks)).reshape([-1 if axis == dim else 1 for axis in range(entries.ndim)]) for dim in (source, target)]
    chosen = jax.random.permutation(stream_key, blocks)[partner]
    strong = (owner == chosen) | (owner == (partner + blocks // 2) % blocks)
    return jnp.where(strong, factor * entries, entries)


def block_levels(rng, shape, cuts, least, top_value):
    def one(dim, shards_of):
        draws = jax.random.uniform(jax.random.fold_in(jax.random.fold_in(rng, 6), dim), (shards_of,), jnp.float32, least / len(cuts), top_value / len(cuts))
        return jnp.repeat(jnp.exp(draws), shape[dim] // shards_of).reshape((-1,) + (1,) * (len(shape) - dim - 1))

    level = one(*cuts[0])
    for cut in cuts[1:]:
        level = level * one(*cut)
    return level


def cumulative_ranks(amount, lean):
    loads = [(1 << 20) // math.isqrt(rank ** lean) + 1 for rank in range(1, amount + 1)]
    spread = 1 + sum(loads) // (1 << 30)
    return np.cumsum(np.array([max(1, weight // spread) for weight in loads]))


def ranked_ids(own_key, shape, number_of, slope):
    grid = cumulative_ranks(number_of, slope)
    lot = jax.random.randint(jax.random.fold_in(own_key, 1), shape, 0, int(grid[number_of - 1]))
    rank = jnp.searchsorted(jnp.asarray(grid, jnp.int32), lot, side="right")
    return jax.random.permutation(jax.random.fold_in(own_key, 2), number_of)[rank].astype(jnp.int32)


def scatter_about(key, dims, scale, reach, cuts=(), kind=jnp.bfloat16):
    drawn = scale * jax.random.normal(key, dims, jnp.float32)
    if cuts:
        drawn = drawn * block_levels(key, dims, cuts, -0.22, 0.18)
    return jnp.clip(drawn, -reach, reach).astype(kind)


def gaussian_with(stream_key, dims, scale, reach, pieces, heavy, kind=jnp.bfloat16):
    values = scale * jax.random.normal(stream_key, dims, jnp.float32)
    if pieces:
        values = values * block_levels(stream_key, dims, pieces, -0.22, 0.18)
    return jnp.clip(strengthened(values, jax.random.fold_in(stream_key, 3), *heavy), -reach, reach).astype(kind)


def setup_inputs(seed: int = 0) -> dict:
    keys = jax.random.split(jax.random.key(seed), 17)
    states = gaussian_with(keys[0], (TOKENS, D), 1.0, 6.0, ((0, 32),), (0, 1, 32, 2.75))
    w_query = scatter_about(keys[1], (D, D), D ** -0.5, 0.125, ((1, 4),))
    w_key = scatter_about(keys[2], (D, D), D ** -0.5, 0.125, ((1, 4),))
    w_value = scatter_about(keys[3], (D, D), D ** -0.5, 0.125, ((1, 4),))
    w_out = scatter_about(keys[4], (D, D), D ** -0.5, 0.125, ((0, 4),))
    w_gate = scatter_about(keys[5], (D, FF), D ** -0.5, 0.125, ((1, 4),))
    w_up = scatter_about(keys[6], (D, FF), D ** -0.5, 0.125, ((1, 4),))
    w_down = scatter_about(keys[7], (FF, D), FF ** -0.5, 0.0625, ((0, 4),))
    q_gain = jnp.clip(1.0 + 0.18 * jax.random.normal(keys[8], (D,), jnp.float32), 0.1, 1.9)
    k_gain = jnp.clip(1.0 + 0.18 * jax.random.normal(keys[9], (D,), jnp.float32), 0.1, 1.9)
    attn_gain = jnp.clip(1.0 + 0.18 * jax.random.normal(keys[10], (D,), jnp.float32), 0.1, 1.9)
    mlp_gain = jnp.clip(1.0 + 0.18 * jax.random.normal(keys[11], (D,), jnp.float32), 0.1, 1.9)
    cotangent = gaussian_with(keys[12], (TOKENS, D), 1.0, 6.0, ((0, 32),), (0, 1, 32, 2.75))
    segments = draw_segments(jax.random.fold_in(keys[16], 71), 0)
    sources = with_ends(ranked_ids(keys[14], (TOKENS,), SOURCES, 2), jax.random.fold_in(keys[14], 3), 0, SOURCES - 1).astype(jnp.int32)
    group_weights = with_ends(jax.random.randint(keys[15], (SOURCES,), 4, 33), jax.random.fold_in(keys[15], 1), 4, 32).astype(jnp.int32)
    return dict(states=states, w_query=w_query, w_key=w_key, w_value=w_value, w_out=w_out, w_gate=w_gate, w_up=w_up, w_down=w_down, q_gain=q_gain, k_gain=k_gain, attn_gain=attn_gain, mlp_gain=mlp_gain, cotangent=cotangent, segments=segments, sources=sources, group_weights=group_weights)


@jax.custom_vjp
def low(v):
    return lax.optimization_barrier(v.astype(jnp.bfloat16)).astype(jnp.float32)

@jax.custom_vjp
def low_back(v):
    return v

def low_keep(v):
    return (low(v), None)

def low_pass(kept, grad):
    return (grad,)

def back_keep(v):
    return (v, None)

def back_low(kept, grad):
    return (low(grad),)
low.defvjp(low_keep, low_pass)
low_back.defvjp(back_keep, back_low)
epsilon = 1e-06
theta_base = 500000.0
weight_unit = 16.0
far_below = -1e+30

def product(left, right):
    return jnp.dot(left, right, precision=lax.Precision.HIGHEST, preferred_element_type=jnp.float32)

def normalize(values, gain):
    return values * lax.rsqrt(lax.optimization_barrier(jnp.mean(values * values, axis=-1, keepdims=True)) + epsilon) * gain

def tables(positions, head_width):
    inverse = 1.0 / theta_base ** (jnp.arange(0, head_width, 2, dtype=jnp.float32) / head_width)
    angles = positions.astype(jnp.float32)[:, None] * inverse[None, :]
    angles = jnp.concatenate([angles, angles], axis=-1)
    return (jnp.cos(angles), jnp.sin(angles))

def rotate(values, cosine_table, sine_table):
    half_width = values.shape[-1] // 2
    turned = jnp.concatenate([-values[..., half_width:], values[..., :half_width]], axis=-1)
    return values * cosine_table[:, None, :] + turned * sine_table[:, None, :]

def decoder(states, w_query, w_key, w_value, w_out, w_gate, w_up, w_down, q_gain, k_gain, attn_gain, mlp_gain, allowed, cosine_table, sine_table):
    token_count = states.shape[0]
    query_raw = low_back(product(states, w_query))
    key_raw = low_back(product(states, w_key))
    value_low = low_back(low(product(states, w_value)))
    q_norm = normalize(query_raw, q_gain).reshape(token_count, HEADS, HD)
    k_norm = normalize(key_raw, k_gain).reshape(token_count, HEADS, HD)
    q_rot = low(rotate(q_norm, cosine_table, sine_table))
    k_rot = low(rotate(k_norm, cosine_table, sine_table))
    value_heads = value_low.reshape(token_count, HEADS, HD)

    def head_attention(operands):
        query_head, key_head, value_head = operands
        scores = low_back(product(query_head, key_head.T) * HD ** (-0.5))
        scores = jnp.where(allowed, scores, far_below)
        probs = jax.nn.softmax(scores, axis=-1)
        return product(low(probs), value_head)
    mixed = lax.map(jax.checkpoint(head_attention), (jnp.transpose(q_rot, (1, 0, 2)), jnp.transpose(k_rot, (1, 0, 2)), jnp.transpose(value_heads, (1, 0, 2))))
    mixed_low = low_back(low(jnp.transpose(mixed, (1, 0, 2)).reshape(token_count, D)))
    branch = low_back(product(mixed_low, w_out))
    hidden = states + normalize(branch, attn_gain)
    hidden_low = low(hidden)
    gate_proj = low_back(product(hidden_low, w_gate))
    up_proj = low_back(product(hidden_low, w_up))
    act_low = low(jax.nn.silu(gate_proj) * up_proj)
    down_proj = low_back(product(act_low, w_down))
    return hidden + normalize(down_proj, mlp_gain)

def reference(states, w_query, w_key, w_value, w_out, w_gate, w_up, w_down, q_gain, k_gain, attn_gain, mlp_gain, cotangent, segments, sources, group_weights):
    floats = tuple((operand.astype(jnp.float32) for operand in (states, w_query, w_key, w_value, w_out, w_gate, w_up, w_down, q_gain, k_gain, attn_gain, mlp_gain)))
    position = jnp.arange(TOKENS, dtype=jnp.int32)
    same_sequence = position[:, None] // SEQ == position[None, :] // SEQ
    allowed = same_sequence & (segments[:, None] == segments[None, :]) & (position[:, None] >= position[None, :])
    cosine_table, sine_table = tables(position % SEQ, HD)

    def forward(*params):
        return decoder(*params, allowed, cosine_table, sine_table)
    result, pullback = jax.vjp(forward, *floats)
    chosen = sources[:, None] == jnp.arange(SOURCES, dtype=jnp.int32)[None, :]
    token_share = lax.optimization_barrier(jnp.sum(jnp.where(chosen, group_weights[None, :], 0), axis=1)).astype(jnp.float32) / weight_unit
    grads = pullback(cotangent.astype(jnp.float32) * token_share[:, None])
    return (result.astype(jnp.bfloat16), grads[0], grads[1], grads[2], grads[3], grads[4], grads[5], grads[6], grads[7], grads[8], grads[9], grads[10], grads[11])
```

```python
import functools

import jax
import jax.numpy as jnp
from jax import lax
from jax.experimental import pallas as pl
from jax.experimental.pallas import tpu as pltpu
from jax.sharding import Mesh
from jax.sharding import PartitionSpec as P

HD = 128
HEADS = 4
TOK = 256
ROWS = 64
BLOCKS = 16
SEQ = 4096
WIDTH = 2048
epsilon = 1e-06
theta_base = 500000.0
weight_unit = 16.0
far_below = -1e30
score_scale = HD ** (-0.5)
LOG2E = 1.4426950408889634
F32 = jnp.float32
BF16 = jnp.bfloat16

FIRST = (1, 0, 3, 2)
SECOND = (3, 2, 1, 0)
VMEM_LIMIT = 48 * 1024 * 1024


def product(left, right):
    return jnp.dot(left, right, preferred_element_type=F32)


def product_right(left, right):
    return lax.dot_general(left, right, (((1,), (1,)), ((), ())), preferred_element_type=F32)


def product_left(left, right):
    return lax.dot_general(left, right, (((0,), (0,)), ((), ())), preferred_element_type=F32)


def swap(value, axis, pairing):
    return lax.ppermute(value, axis, [(i, pairing[i]) for i in range(4)])


def swap_core(value):
    return lax.ppermute(value, "c", [(0, 1), (1, 0)])


def swap_xz(value, x_pairing, z_pairing):
    pairs = [(i * 4 + j, x_pairing[i] * 4 + z_pairing[j]) for i in range(4) for j in range(4)]
    return lax.ppermute(value, ("x", "z"), pairs)


def shift_y(value, step):
    return lax.ppermute(value, "y", [(i, (i + step) % 4) for i in range(4)])


def scatter_y(partial):
    total = partial[:ROWS].astype(F32)
    for k in (1, 3, 2):
        total = total + shift_y(partial[k * ROWS : (k + 1) * ROWS], k).astype(F32)
    return total


def gather_y(own):
    received = {k: shift_y(own, -k) for k in (1, 3, 2)}
    return jnp.concatenate([own, received[1], received[2], received[3]], axis=0)


def sum_y(value):
    total = value
    for k in (1, 3, 2):
        total = total + jnp.roll(shift_y(value, k), -ROWS * k, axis=1)
    return total


def call(body, outs, operands, smem=1, scratch=(), cost=None):
    in_specs = [pl.BlockSpec(memory_space=pltpu.SMEM)] * smem
    in_specs += [pl.BlockSpec(memory_space=pltpu.VMEM)] * (len(operands) - smem)
    return pl.pallas_call(
        body,
        out_shape=[jax.ShapeDtypeStruct(s, d) for s, d in outs],
        in_specs=in_specs,
        out_specs=[pl.BlockSpec(memory_space=pltpu.VMEM)] * len(outs),
        scratch_shapes=list(scratch),
        compiler_params=pltpu.CompilerParams(vmem_limit_bytes=VMEM_LIMIT),
        cost_estimate=cost,
    )(*operands)


def attend_body(info, q_ref, kv0, kv1, kv2, kv3, qpos_ref, qstart_ref, o_ref, ot_ref, lse_ref, m_ref, l_ref, acc_ref):
    own_x = info[0]
    roll = info[1]
    kvs = (kv0, kv1, kv2, kv3)

    @pl.loop(0, 4)
    def _(a):
        block = info[2 + a]
        q = q_ref[a]
        qpos = qpos_ref[a]
        qstart = qstart_ref[a]
        m_ref[...] = jnp.full_like(m_ref, far_below)
        l_ref[...] = jnp.zeros_like(l_ref)
        acc_ref[...] = jnp.zeros_like(acc_ref)
        for xb in range(2):
            for group in range(4):
                at = 6 + (group * 2 + xb) * 2
                first, second = info[at], info[at + 1]

                @pl.when(jnp.minimum(first, second) <= block)
                def _(group=group, xb=xb, first=first, second=second):
                    start = (own_x ^ xb) * 2
                    k = kvs[group][0, pl.ds(start, 2)].reshape(2 * TOK, HD)
                    v = kvs[group][1, pl.ds(start, 2)].reshape(2 * TOK, HD)
                    s = product_right(k, q)
                    row = lax.broadcasted_iota(jnp.int32, (2 * TOK, TOK), 0)
                    place = ((row + roll) & (TOK - 1)) + jnp.where(row < TOK, first, second) * TOK
                    s = jnp.where((place <= qpos) & (place >= qstart), s, far_below)
                    m_old = m_ref[...]
                    m_new = jnp.maximum(m_old, jnp.max(s, axis=0, keepdims=True))
                    p = jnp.exp2((s - m_new) * (score_scale * LOG2E))
                    alpha = jnp.exp2((m_old - m_new) * (score_scale * LOG2E))
                    l_ref[...] = alpha * l_ref[...] + jnp.sum(p, axis=0, keepdims=True)
                    acc_ref[...] = alpha * acc_ref[...] + product_left(v, p.astype(BF16))
                    m_ref[...] = m_new

        out = acc_ref[...] / l_ref[...]
        ot_ref[a] = out
        o_ref[a] = out.T.astype(BF16)
        lse_ref[a] = m_ref[...] * (score_scale * LOG2E) + jnp.log2(l_ref[...])


def attend(info, q, kvs, qpos, qstart):
    return call(
        attend_body,
        [((4, TOK, HD), BF16), ((4, HD, TOK), F32), ((4, 1, TOK), F32)],
        [info, q, *kvs, qpos, qstart],
        scratch=[pltpu.VMEM((1, TOK), F32), pltpu.VMEM((1, TOK), F32), pltpu.VMEM((HD, TOK), F32)],
        cost=pl.CostEstimate(flops=36 * 4 * TOK * TOK * HD, bytes_accessed=4 << 20, transcendentals=36 * TOK * TOK),
    )


def attend_back_body(info, q_ref, kv0, kv1, kv2, kv3, qpos_ref, qstart_ref, do_ref, ot_ref, lse_ref, dq_ref, keep0_ref, keep2_ref, send_ref, acc_ref, dqt_ref):
    own_x = info[0]
    roll = info[1]
    kvs = (kv0, kv1, kv2, kv3)
    acc_ref[...] = jnp.zeros_like(acc_ref)

    @pl.loop(0, 4)
    def _(a):
        block = info[2 + a]
        q = q_ref[a]
        do = do_ref[a]
        delta = jnp.sum(do.astype(F32).T * ot_ref[a], axis=0, keepdims=True)
        lse = lse_ref[a]
        qpos = qpos_ref[a]
        qstart = qstart_ref[a]
        dqt_ref[...] = jnp.zeros_like(dqt_ref)
        for xb in range(2):
            for group in range(4):
                at = 6 + (group * 2 + xb) * 2
                first, second = info[at], info[at + 1]

                @pl.when(jnp.minimum(first, second) <= block)
                def _(group=group, xb=xb, first=first, second=second):
                    start = (own_x ^ xb) * 2
                    k = kvs[group][0, pl.ds(start, 2)].reshape(2 * TOK, HD)
                    v = kvs[group][1, pl.ds(start, 2)].reshape(2 * TOK, HD)
                    s = product_right(k, q)
                    dp = product_right(v, do)
                    row = lax.broadcasted_iota(jnp.int32, (2 * TOK, TOK), 0)
                    place = ((row + roll) & (TOK - 1)) + jnp.where(row < TOK, first, second) * TOK
                    keep = (place <= qpos) & (place >= qstart)
                    p = jnp.where(keep, jnp.exp2(s * (score_scale * LOG2E) - lse), 0.0)
                    ds = (p * (dp - delta)).astype(BF16)
                    dqt_ref[...] += product_left(k, ds)
                    acc_ref[group, 0, pl.ds(start, 2)] += product(ds, q).reshape(2, TOK, HD)
                    acc_ref[group, 1, pl.ds(start, 2)] += product(p.astype(BF16), do).reshape(2, TOK, HD)

        dq_ref[a] = (dqt_ref[...] * score_scale).T.astype(BF16)

    for group, out in ((0, keep0_ref), (2, keep2_ref), (1, send_ref.at[0]), (3, send_ref.at[1])):
        out[0] = (acc_ref[group, 0] * score_scale).astype(BF16)
        out[1] = acc_ref[group, 1].astype(BF16)


def attend_back(info, q, kvs, qpos, qstart, do, ot, lse):
    piece = (2, 4, TOK, HD)
    return call(
        attend_back_body,
        [((4, TOK, HD), BF16), (piece, BF16), (piece, BF16), ((2, *piece), BF16)],
        [info, q, *kvs, qpos, qstart, do, ot, lse],
        scratch=[pltpu.VMEM((4, *piece), F32), pltpu.VMEM((HD, TOK), F32)],
        cost=pl.CostEstimate(flops=36 * 10 * TOK * TOK * HD, bytes_accessed=8 << 20, transcendentals=36 * TOK * TOK),
    )


def enter_body(info, q_ref, k_ref, v_ref, rate_ref, gain_ref, cos_ref, sin_ref, *outs):
    head = info[0]
    cos, sin = cos_ref[...], sin_ref[...]
    for r in range(4):
        at = pl.ds(pl.multiple_of((head ^ r) * HD, HD), HD)
        for j, raw_ref in enumerate((q_ref, k_ref)):
            value = raw_ref[:, at] * rate_ref[j] * gain_ref[j, :, at]
            turned = pltpu.roll(value, HD // 2, 1)
            outs[r][j] = (value * cos + turned * sin).astype(BF16)
        outs[r][2] = v_ref[:, at]


def enter(info, q_raw, k_raw, v_low, rates, gains, cos, sin):
    return call(enter_body, [((3, TOK, HD), BF16)] * 4, [info, q_raw, k_raw, v_low, rates, gains, cos, sin])


def leave_body(info, q_ref, k_ref, rate_ref, gain_ref, cos_ref, sin_ref, *refs):
    head = info[0]
    dqs, dkvs = refs[:4], refs[4:8]
    q_scaled, k_scaled, v_low, gains_out, inner_out = refs[8:]
    cos, sin = cos_ref[...], sin_ref[...]
    inner = [jnp.zeros((TOK, 1), F32), jnp.zeros((TOK, 1), F32)]
    for r in range(4):
        at = pl.ds(pl.multiple_of((head ^ r) * HD, HD), HD)
        v_low[:, at] = dkvs[r][1]
        for j, (raw_ref, out) in enumerate(((q_ref, q_scaled), (k_ref, k_scaled))):
            grad = (dqs[r][...] if j == 0 else dkvs[r][0]).astype(F32)
            grad = grad * cos - pltpu.roll(grad, HD // 2, 1) * sin
            raw = raw_ref[:, at]
            gains_out[j, :, at] = jnp.sum(grad * raw * rate_ref[j], axis=0, keepdims=True)
            scaled = grad * gain_ref[j, :, at]
            out[:, at] = scaled
            inner[j] = inner[j] + jnp.sum(raw * scaled, axis=1, keepdims=True)
    for j in range(2):
        inner_out[j] = inner[j]


def leave(info, q_raw, k_raw, rates, gains, cos, sin, dqs, dkvs):
    outs = [((TOK, 512), F32), ((TOK, 512), F32), ((TOK, 512), BF16), ((2, 1, 512), F32), ((2, TOK, 1), F32)]
    return call(leave_body, outs, [info, q_raw, k_raw, rates, gains, cos, sin, *dqs, *dkvs])


def columns_body(info, x_ref, own_ref, other_ref):
    core = info[0]
    for k in range(BLOCKS):
        at = pl.ds(pl.multiple_of(info[1 + k] * 128, 128), 128)
        turned = x_ref[:, at].astype(F32).T
        low, high = turned[:ROWS], turned[ROWS:]
        own_ref[pl.ds(k * ROWS, ROWS)] = jnp.where(core == 0, low, high).astype(BF16)
        other_ref[pl.ds(k * ROWS, ROWS)] = jnp.where(core == 0, high, low).astype(BF16)


def columns(order, value):
    return call(columns_body, [((BLOCKS * ROWS, TOK), BF16)] * 2, [order, value])


def halves_body(bit, a0, a1, b0, b1, send_ref, keep_ref):
    rows = 256
    for i in range(BLOCKS * ROWS // rows):
        at = pl.ds(i * rows, rows)
        c = (product(a0[at], b0[...]) + product(a1[at], b1[...])).astype(BF16)
        for n in range(rows // ROWS):
            k = i * (rows // ROWS) + n
            upper = (k >> (3 - bit)) & 1
            low = k & ((1 << (3 - bit)) - 1)
            to = ((k >> (4 - bit)) << (3 - bit)) | low
            out = send_ref if upper else keep_ref
            out[pl.ds(to * ROWS, ROWS)] = c[n * ROWS : (n + 1) * ROWS]


def halves(bit, index, width, left, right):
    whole = pl.BlockSpec((BLOCKS * ROWS, TOK), lambda j: (0, 0))
    part = pl.BlockSpec((TOK, width), lambda j: (0, index))
    half = jax.ShapeDtypeStruct((BLOCKS * ROWS // 2, width), BF16)
    return pl.pallas_call(
        functools.partial(halves_body, bit),
        grid=(1,),
        out_shape=[half, half],
        in_specs=[whole, whole, part, part],
        out_specs=[pl.BlockSpec((BLOCKS * ROWS // 2, width), lambda j: (0, 0))] * 2,
        compiler_params=pltpu.CompilerParams(vmem_limit_bytes=VMEM_LIMIT),
        cost_estimate=pl.CostEstimate(flops=4 * BLOCKS * ROWS * TOK * width, bytes_accessed=BLOCKS * ROWS * width * 2, transcendentals=0),
    )(*left, *right)


STEPS = (("x", FIRST), ("x", SECOND), ("z", FIRST), ("z", SECOND))


def scatter_parts(pairs):
    bits = [[b for b in range(4) if b != p] for p in range(4)]
    sends = [s for s, _ in pairs]
    keeps = [k for _, k in pairs]
    for t in range(4):
        received = [swap(sends[p], *STEPS[(p + t) % 4]) for p in range(4)]
        if t == 3:
            return [(keeps[p].astype(F32) + received[p].astype(F32)) for p in range(4)]
        for p in range(4):
            bit = (p + t + 1) % 4
            at = bits[p].index(bit)
            bits[p].pop(at)
            width = keeps[p].shape[-1]
            shape = (1 << at, 2, (1 << (2 - t)) >> at, ROWS, width)
            kept, came = keeps[p].reshape(shape), received[p].reshape(shape)
            halves_now = [
                (kept[:, i].astype(F32) + came[:, i].astype(F32)).astype(BF16).reshape(-1, width) for i in (1, 0)
            ]
            sends[p], keeps[p] = halves_now


def plain_body(a0, a1, b0, b1, out):
    out[...] = (product(a0[...], b0[...]) + product(a1[...], b1[...])).astype(BF16)


def plain(left, right):
    columns_now = right[0].shape[1]
    width = min(512, columns_now)
    whole = pl.BlockSpec((BLOCKS * ROWS, TOK), lambda j: (0, 0))
    part = pl.BlockSpec((TOK, width), lambda j: (0, j))
    return pl.pallas_call(
        plain_body,
        grid=(columns_now // width,),
        out_shape=jax.ShapeDtypeStruct((BLOCKS * ROWS, columns_now), BF16),
        in_specs=[whole, whole, part, part],
        out_specs=pl.BlockSpec((BLOCKS * ROWS, width), lambda j: (0, j)),
        compiler_params=pltpu.CompilerParams(vmem_limit_bytes=VMEM_LIMIT),
        cost_estimate=pl.CostEstimate(flops=4 * BLOCKS * ROWS * TOK * columns_now, bytes_accessed=BLOCKS * ROWS * columns_now * 2, transcendentals=0),
    )(*left, *right)


def sum_all(value):
    for axis, pairing in STEPS:
        value = value + swap(value, axis, pairing)
    return value + swap_core(value)


def local(
    states,
    w_query,
    w_key,
    w_value,
    w_out,
    w_gate,
    w_up,
    w_down,
    q_gain,
    k_gain,
    attn_gain,
    mlp_gain,
    cotangent,
    segments,
    sources,
    group_weights,
):
    x, z, c, y = (lax.axis_index(n) for n in ("x", "z", "c", "y"))
    own_x = x & 1
    z_low, z_high = (z ^ (z >> 1)) & 1, z >> 1
    head = own_x * 2 + z_high
    roll = y * ROWS
    head_info = head.reshape(1)

    def rolled(value):
        return lax.dynamic_slice_in_dim(jnp.concatenate([value, value], axis=0), roll, TOK, 0)

    def own_rows(value):
        return lax.dynamic_slice_in_dim(value, roll, ROWS, 0)

    here = (jnp.arange(TOK, dtype=jnp.int32) + roll) & (TOK - 1)
    own_block = own_x * 8 + z * 2 + c

    def z_of(high, low):
        return high * 2 + (low ^ high)

    q_blocks = jnp.stack([(own_x ^ (a >> 1)) * 8 + z_of(z_high ^ (a & 1), z_low) * 2 + c for a in range(4)])
    tiles = []
    for group in range(4):
        for xb in range(2):
            for a in range(2):
                tiles.append(xb * 8 + z_of(z_high ^ a, z_low ^ (group >> 1)) * 2 + (c ^ (group & 1)))
    info = jnp.stack([own_x, roll, *q_blocks, *tiles]).astype(jnp.int32)
    q_pos = q_blocks[:, None] * TOK + here[None]
    seq_segments = lax.dynamic_slice_in_dim(segments, (x >> 1) * SEQ, SEQ)
    q_segments = seq_segments[q_pos.reshape(-1)]
    q_start = jnp.sum((seq_segments[None, :] < q_segments[:, None]).astype(jnp.int32), axis=1)
    q_start = q_start.reshape(4, 1, TOK)
    q_pos = q_pos.reshape(4, 1, TOK)

    inverse = 1.0 / theta_base ** (jnp.arange(0, HD, 2, dtype=F32) / HD)
    angles = (own_block * TOK + here).astype(F32)[:, None] * inverse[None, :]
    cosine, sine = jnp.cos(angles), jnp.sin(angles)
    cos_table = jnp.concatenate([cosine, cosine], axis=-1)
    sin_table = jnp.concatenate([-sine, sine], axis=-1)
    gains = jnp.stack([q_gain, k_gain]).reshape(2, 1, 512)

    states_here = rolled(states)
    query_raw = product(states_here, w_query)
    key_raw = product(states_here, w_key)
    value_low = product(states_here, w_value).astype(BF16)
    squares = jnp.stack([jnp.sum(query_raw * query_raw, axis=1), jnp.sum(key_raw * key_raw, axis=1)])
    squares = sum_y(squares)
    rates = lax.rsqrt(squares / WIDTH + epsilon)
    rates_column = rates.reshape(2, TOK, 1)
    mine, to_z, to_x, to_xz = enter(head_info, query_raw, key_raw, value_low, rates_column, gains, cos_table, sin_table)

    def exchange(to_z, to_x, to_xz):
        return swap(to_z, "z", SECOND), swap(to_x, "x", FIRST), swap_xz(to_xz, FIRST, SECOND)

    pieces = jnp.stack([mine, *exchange(to_z, to_x, to_xz)], axis=1)
    q_here, kv_own = pieces[0], pieces[1:]
    kv_z = swap(kv_own, "z", FIRST)
    kv_c = swap_core(kv_own)
    kv_zc = swap_core(kv_z)
    kvs = (kv_own, kv_c, kv_z, kv_zc)
    mixed, mixed_turned, log_total = attend(info, q_here, kvs, q_pos, q_start)
    back = jnp.stack([mixed[0], *exchange(mixed[1], mixed[2], mixed[3])])
    mixed_low = jnp.concatenate([lax.dynamic_index_in_dim(back, head ^ k, 0, False) for k in range(4)], axis=1)

    branch = scatter_y(product(mixed_low, w_out).astype(BF16))
    b_rate = lax.rsqrt(jnp.mean(branch * branch, axis=1, keepdims=True) + epsilon)
    b_norm = branch * b_rate
    hidden = own_rows(states).astype(F32) + attn_gain * b_norm
    hidden_low = gather_y(hidden.astype(BF16))
    gate_proj = product(hidden_low, w_gate)
    up_proj = product(hidden_low, w_up)
    sigmoid_gate = jax.nn.sigmoid(gate_proj)
    silu_gate = gate_proj * sigmoid_gate
    act_low = (silu_gate * up_proj).astype(BF16)
    down_proj = scatter_y(product(act_low, w_down).astype(BF16))
    d_rate = lax.rsqrt(jnp.mean(down_proj * down_proj, axis=1, keepdims=True) + epsilon)
    d_norm = down_proj * d_rate
    output_own = (hidden + mlp_gain * d_norm).astype(BF16)

    chosen = own_rows(sources)[:, None] == jnp.arange(group_weights.shape[0], dtype=jnp.int32)[None, :]
    token_share = jnp.sum(jnp.where(chosen, group_weights[None, :], 0), axis=1).astype(F32) / weight_unit
    grad_top = own_rows(cotangent).astype(F32) * token_share[:, None]
    local_mlp_gain = jnp.sum(grad_top * d_norm, axis=0)
    scaled_top = mlp_gain * grad_top
    grad_down_own = (
        d_rate * (scaled_top - d_norm * jnp.mean(scaled_top * d_norm, axis=1, keepdims=True))
    ).astype(BF16)
    grad_down_proj = gather_y(grad_down_own)

    x_order = [x, jnp.bitwise_xor(x, 1), 3 - x, 3 - jnp.bitwise_xor(x, 1)]
    z_order = [z, jnp.bitwise_xor(z, 1), 3 - z, 3 - jnp.bitwise_xor(z, 1)]
    by_bits = (0, 2, 1, 3)
    order = jnp.stack([c] + [x_order[by_bits[i]] * 4 + z_order[by_bits[j]] for i in range(4) for j in range(4)])
    plain_order = jnp.concatenate([c.reshape(1), jnp.arange(BLOCKS, dtype=jnp.int32)])

    def shared(order_now, left, rights):
        own, other = columns(order_now, left)
        return (own, swap_core(other)), [(r, swap_core(r)) for r in rights]

    down_left, (down_right,) = shared(plain_order, grad_down_proj, [act_low])
    grad_down = lax.psum_scatter(plain(down_left, down_right), ("x", "z"), scatter_dimension=0, tiled=True)

    grad_act = product_right(grad_down_proj, w_down)
    grad_gate_proj = (grad_act * up_proj * sigmoid_gate * (1.0 + gate_proj * (1.0 - sigmoid_gate))).astype(BF16)
    grad_up_proj = (grad_act * silu_gate).astype(BF16)
    hidden_part = product_right(grad_gate_proj, w_gate) + product_right(grad_up_proj, w_up)
    hidden_sum = scatter_y(hidden_part.astype(BF16))

    gate_left, (gate_right, up_right) = shared(order, hidden_low, [grad_gate_proj, grad_up_proj])
    gate_up = scatter_parts(
        [
            halves(0, 0, 1024, gate_left, gate_right),
            halves(1, 1, 1024, gate_left, gate_right),
            halves(2, 0, 1024, gate_left, up_right),
            halves(3, 1, 1024, gate_left, up_right),
        ]
    )
    output = gather_y(output_own)

    grad_hidden = grad_top + hidden_sum
    local_attn_gain = jnp.sum(grad_hidden * b_norm, axis=0)
    scaled_hidden = attn_gain * grad_hidden
    grad_branch = gather_y(
        (b_rate * (scaled_hidden - b_norm * jnp.mean(scaled_hidden * b_norm, axis=1, keepdims=True))).astype(BF16)
    )
    grad_mixed = product_right(grad_branch, w_out).astype(BF16)
    to = [lax.dynamic_slice_in_dim(grad_mixed, (head ^ r) * HD, HD, 1) for r in range(4)]
    grad_mixed_here = jnp.stack([to[0], *exchange(to[1], to[2], to[3])])

    out_left, (out_right,) = shared(plain_order, grad_branch, [mixed_low])
    grad_out = lax.psum_scatter(plain(out_left, out_right), ("x", "z"), scatter_dimension=0, tiled=True)

    dq, keep_own, keep_z, send_c = attend_back(
        info, q_here, kvs, q_pos, q_start, grad_mixed_here, mixed_turned, log_total
    )
    dqs = [dq[0], *exchange(dq[1], dq[2], dq[3])]
    came = swap_core(send_c)
    keep_z = (keep_z.astype(F32) + came[1].astype(F32)).astype(BF16)
    keep_own = keep_own.astype(F32) + came[0].astype(F32)
    keep_own = (keep_own + swap(keep_z, "z", FIRST).astype(F32)).astype(BF16)
    dkvs = [keep_own[:, 0], *exchange(keep_own[:, 1], keep_own[:, 2], keep_own[:, 3])]
    q_scaled, k_scaled, grad_value_low, local_qk_gain, inner = leave(
        head_info, query_raw, key_raw, rates_column, gains, cos_table, sin_table, dqs, dkvs
    )
    inner = inner.reshape(2, TOK)
    inner = sum_y(inner)
    factor = rates * rates * rates * inner / WIDTH
    grad_query_raw = (rates[0][:, None] * q_scaled - query_raw * factor[0][:, None]).astype(BF16)
    grad_key_raw = (rates[1][:, None] * k_scaled - key_raw * factor[1][:, None]).astype(BF16)
    input_part = (
        product_right(grad_query_raw, w_query)
        + product_right(grad_key_raw, w_key)
        + product_right(grad_value_low, w_value)
    )
    grad_states_own = grad_hidden + scatter_y(input_part.astype(BF16))
    grad_states = gather_y(grad_states_own.astype(BF16))

    together = jnp.concatenate([grad_query_raw, grad_key_raw, grad_value_low], axis=1)
    qkv_left, (qkv_right,) = shared(order, states_here, [together])
    qkv = jnp.concatenate(scatter_parts([halves(p, p, 384, qkv_left, qkv_right) for p in range(4)]), axis=1)

    wide_gains = sum_all(jnp.stack([local_attn_gain, local_mlp_gain]))
    wide_gains = wide_gains + swap(wide_gains, "y", FIRST)
    wide_gains = wide_gains + swap(wide_gains, "y", SECOND)
    qk_gains = sum_all(local_qk_gain.reshape(2, 512))

    def unrolled(value):
        return lax.dynamic_slice_in_dim(jnp.concatenate([value, value], axis=0), (TOK - roll) & (TOK - 1), TOK, 0)

    return (
        unrolled(output),
        unrolled(grad_states).astype(F32),
        qkv[:, :512],
        qkv[:, 512:1024],
        qkv[:, 1024:],
        jnp.transpose(grad_out.astype(F32)),
        jnp.concatenate(gate_up[:2], axis=1),
        jnp.concatenate(gate_up[2:], axis=1),
        jnp.transpose(grad_down.astype(F32)),
        qk_gains[0],
        qk_gains[1],
        wide_gains[0],
        wide_gains[1],
    )


def solution(mesh):
    split = Mesh(mesh.devices.reshape(4, 4, 2, 4), ("x", "z", "c", "y"))
    dp, mp = ("x", "z", "c"), "y"
    placed = (
        P(dp, None),
        P(None, mp),
        P(None, mp),
        P(None, mp),
        P(mp, None),
        P(None, mp),
        P(None, mp),
        P(mp, None),
        P(mp),
        P(mp),
        P(),
        P(),
        P(dp, None),
        P(),
        P(dp),
        P(),
    )
    return jax.shard_map(
        local,
        mesh=split,
        in_specs=placed,
        out_specs=(
            P(dp, None),
            P(dp, None),
            P(dp, mp),
            P(dp, mp),
            P(dp, mp),
            P(mp, dp),
            P(dp, mp),
            P(dp, mp),
            P(mp, dp),
            P(mp),
            P(mp),
            P(),
            P(),
        ),
        check_vma=False,
    )
```

```python
import functools

import jax
import jax.numpy as jnp
from jax import lax
from jax.experimental import pallas as pl
from jax.experimental.pallas import tpu as pltpu
from jax.sharding import Mesh
from jax.sharding import PartitionSpec as P

HD = 128
HEADS = 4
TOK = 256
ROWS = 64
BLOCKS = 16
SEQ = 4096
WIDTH = 2048
epsilon = 1e-06
theta_base = 500000.0
weight_unit = 16.0
far_below = -1e30
score_scale = HD ** (-0.5)
LOG2E = 1.4426950408889634
F32 = jnp.float32
BF16 = jnp.bfloat16

FIRST = (1, 0, 3, 2)
SECOND = (3, 2, 1, 0)
BOTH = (2, 3, 0, 1)
HERE = (0, 1, 2, 3)
PAIRINGS = (HERE, FIRST, SECOND, BOTH)
VMEM_LIMIT = 10 * 1024 * 1024
COST = pl.CostEstimate(flops=1, bytes_accessed=1, transcendentals=0)
LONG = pl.CostEstimate(flops=10**12, bytes_accessed=1, transcendentals=0)


def product(left, right):
    return jnp.dot(left, right, preferred_element_type=F32)


def product_right(left, right):
    return lax.dot_general(left, right, (((1,), (1,)), ((), ())), preferred_element_type=F32)


def product_left(left, right):
    return lax.dot_general(left, right, (((0,), (0,)), ((), ())), preferred_element_type=F32)


def swap(value, axis, pairing):
    return lax.ppermute(value, axis, [(i, pairing[i]) for i in range(4)])


def swap_core(value):
    return lax.ppermute(value, "c", [(0, 1), (1, 0)])


def swap_xz(value, x_pairing, z_pairing):
    pairs = [(i * 4 + j, x_pairing[i] * 4 + z_pairing[j]) for i in range(4) for j in range(4)]
    return lax.ppermute(value, ("x", "z"), pairs)


def shift_y(value, step):
    return lax.ppermute(value, "y", [(i, (i + step) % 4) for i in range(4)])


def scatter_y(pieces):
    return [pieces[0]] + [shift_y(pieces[k], k) for k in (1, 2, 3)]


def gather_y(own):
    return [own] + [shift_y(own, -k) for k in (1, 2, 3)]


def rows_of(value):
    return [value[k * ROWS : (k + 1) * ROWS] for k in range(4)]


def fetching(body, far, *refs):
    held, sems = refs[-1 - len(far) : -1], refs[-1]
    refs = list(refs[: -1 - len(far)])
    copies = [pltpu.make_async_copy(refs[at], held[n], sems.at[n]) for n, at in enumerate(far)]
    for copy in copies:
        copy.start()
    for n, at in enumerate(far):
        copies[n].wait()
        refs[at] = held[n]
    body(*refs)


def hbm(value):
    return pltpu.with_memory_space_constraint(value, pltpu.HBM)


def call(body, outs, operands, scratch=(), limit=VMEM_LIMIT, far=(), cost=COST):
    in_specs = [pl.BlockSpec(memory_space=pltpu.VMEM)] * len(operands)
    scratch = list(scratch)
    if far:
        body = functools.partial(fetching, body, far)
        operands = list(operands)
        for at in far:
            operands[at] = hbm(operands[at])
            in_specs[at] = pl.BlockSpec(memory_space=pltpu.HBM)
            scratch.append(pltpu.VMEM(operands[at].shape, operands[at].dtype))
        scratch.append(pltpu.SemaphoreType.DMA((len(far),)))
    return pl.pallas_call(
        body,
        out_shape=[jax.ShapeDtypeStruct(s, d) for s, d in outs],
        in_specs=in_specs,
        out_specs=[pl.BlockSpec(memory_space=pltpu.VMEM)] * len(outs),
        scratch_shapes=scratch,
        compiler_params=pltpu.CompilerParams(vmem_limit_bytes=limit),
        cost_estimate=cost,
    )(*operands)


def place():
    x, z, core, y = (lax.axis_index(n) for n in ("x", "z", "c", "y"))
    own_x, high, low = x & 1, z >> 1, (z ^ (z >> 1)) & 1
    return own_x, high, low, own_x * 2 + high, core, y * ROWS


def block_of(x_bit, high, low, core):
    return x_bit * 8 + (high * 2 + (low ^ high)) * 2 + core


def key_tile(group, xb, own_x, high, low, core, kv):
    start = (own_x ^ xb) * 2
    k = kv[0, pl.ds(start, 2)].reshape(2 * TOK, HD)
    v = kv[1, pl.ds(start, 2)].reshape(2 * TOK, HD)
    return start, k, v


def tile_blocks(group, xb, high, low, core):
    return [block_of(xb, high ^ n, low ^ (group >> 1), core ^ (group & 1)) for n in (0, 1)]


def allowed(first, second, roll, qpos, qstart):
    row = lax.broadcasted_iota(jnp.int32, (2 * TOK, TOK), 0)
    at = ((row + roll) & (TOK - 1)) + jnp.where(row < TOK, first, second) * TOK
    return (at <= qpos) & (at >= qstart)


def attend_body(groups, q_ref, kva, kvb, qpos_ref, qstart_ref, *refs):
    own_x, high, low, _, core, roll = place()
    last = groups == (2, 3)
    if last:
        m_in, l_in, acc_in, o0, o1, o2, o3, ot_ref, lse_ref, m_ref, l_ref, acc_ref = refs
        m_ref[...] = m_in[...]
        l_ref[...] = l_in[...]
        acc_ref[...] = acc_in[...]
    else:
        m_ref, l_ref, acc_ref = refs
        m_ref[...] = jnp.full_like(m_ref, far_below)
        l_ref[...] = jnp.zeros_like(l_ref)
        acc_ref[...] = jnp.zeros_like(acc_ref)

    @pl.loop(0, 4)
    def _(a):
        block = block_of(own_x ^ (a >> 1), high ^ (a & 1), low, core)
        q = q_ref[a]
        qpos = qpos_ref[a]
        qstart = qstart_ref[a]
        for xb in range(2):
            for group, kv in zip(groups, (kva, kvb)):
                first, second = tile_blocks(group, xb, high, low, core)

                @pl.when(jnp.minimum(first, second) <= block)
                def _(group=group, kv=kv, xb=xb, first=first, second=second):
                    _, k, v = key_tile(group, xb, own_x, high, low, core, kv)
                    s = product_right(k, q)
                    s = jnp.where(allowed(first, second, roll, qpos, qstart), s, far_below)
                    m_old = m_ref[a]
                    m_new = jnp.maximum(m_old, jnp.max(s, axis=0, keepdims=True))
                    p = jnp.exp2((s - m_new) * (score_scale * LOG2E))
                    alpha = jnp.exp2((m_old - m_new) * (score_scale * LOG2E))
                    l_ref[a] = alpha * l_ref[a] + jnp.sum(p, axis=0, keepdims=True)
                    acc_ref[a] = alpha * acc_ref[a] + product_left(v, p.astype(BF16))
                    m_ref[a] = m_new

    if last:
        for a, out in enumerate((o0, o1, o2, o3)):
            mixed = acc_ref[a] / l_ref[a]
            ot_ref[a] = mixed
            out[...] = mixed.T.astype(BF16)
            lse_ref[a] = m_ref[a] * (score_scale * LOG2E) + jnp.log2(l_ref[a])


STATE = [((4, 1, TOK), F32), ((4, 1, TOK), F32), ((4, HD, TOK), F32)]


def attend_first(q, kvs, qpos, qstart):
    return call(functools.partial(attend_body, (0, 1)), STATE, [q, *kvs, qpos, qstart])


def attend_last(q, kvs, qpos, qstart, state):
    outs = [((TOK, HD), BF16)] * 4 + [((4, HD, TOK), F32), ((4, 1, TOK), F32)]
    scratch = [pltpu.VMEM(shape, kind) for shape, kind in STATE]
    return call(functools.partial(attend_body, (2, 3)), outs, [q, *kvs, qpos, qstart, *state], scratch=scratch)


def attend_back_body(groups, q_ref, kva, kvb, qpos_ref, qstart_ref, do0, do1, do2, do3, ot_ref, lse_ref, *refs):
    own_x, high, low, _, core, roll = place()
    last = groups == (0, 1)
    if last:
        dq_in, d0, d1, d2, d3, keep_ref, send_ref, acc_ref, dqt_ref, do_ref = refs
        dqt_ref[...] = dq_in[...]
    else:
        dqt_ref, keep_ref, send_ref, acc_ref, do_ref = refs
        dqt_ref[...] = jnp.zeros_like(dqt_ref)
    acc_ref[...] = jnp.zeros_like(acc_ref)
    for a, ref in enumerate((do0, do1, do2, do3)):
        do_ref[a] = ref[...]

    @pl.loop(0, 4)
    def _(a):
        block = block_of(own_x ^ (a >> 1), high ^ (a & 1), low, core)
        q = q_ref[a]
        do = do_ref[a]
        delta = jnp.sum(do.astype(F32).T * ot_ref[a], axis=0, keepdims=True)
        lse = lse_ref[a]
        qpos = qpos_ref[a]
        qstart = qstart_ref[a]
        for xb in range(2):
            for n, (group, kv) in enumerate(zip(groups, (kva, kvb))):
                first, second = tile_blocks(group, xb, high, low, core)

                @pl.when(jnp.minimum(first, second) <= block)
                def _(n=n, group=group, kv=kv, xb=xb, first=first, second=second):
                    start, k, v = key_tile(group, xb, own_x, high, low, core, kv)
                    s = product_right(k, q)
                    dp = product_right(v, do)
                    keep = allowed(first, second, roll, qpos, qstart)
                    p = jnp.where(keep, jnp.exp2(s * (score_scale * LOG2E) - lse), 0.0)
                    ds = (p * (dp - delta)).astype(BF16)
                    dqt_ref[a] += product_left(k, ds)
                    acc_ref[n, 0, pl.ds(start, 2)] += product(ds, q).reshape(2, TOK, HD)
                    acc_ref[n, 1, pl.ds(start, 2)] += product(p.astype(BF16), do).reshape(2, TOK, HD)

    if last:
        for a, out in enumerate((d0, d1, d2, d3)):
            out[...] = (dqt_ref[a] * score_scale).T.astype(BF16)
    for n, out in enumerate((keep_ref, send_ref)):
        for at in range(4):
            for j in range(2):
                factor = score_scale if j == 0 else 1.0
                out[pl.ds((at * 2 + j) * TOK, TOK)] = (acc_ref[n, j, at] * factor).astype(BF16)


PIECES = ((8 * TOK, HD), BF16)


def attend_back(first, q, kvs, qpos, qstart, do, ot, lse, dq=None):
    scratch = [pltpu.VMEM((2, 2, 4, TOK, HD), F32)]
    operands = [q, *kvs, qpos, qstart, *do, ot, lse]
    if first:
        outs = [((4, HD, TOK), F32), PIECES, PIECES]
    else:
        outs = [((TOK, HD), BF16)] * 4 + [PIECES, PIECES]
        operands.append(dq)
        scratch.append(pltpu.VMEM((4, HD, TOK), F32))
    scratch.append(pltpu.VMEM((4, TOK, HD), BF16))
    body = functools.partial(attend_back_body, (2, 3) if first else (0, 1))
    far = (0, 1, 2, 3, 4, 9, 10) if first else ()
    return call(body, outs, operands, scratch=scratch, limit=16 * 1024 * 1024, far=far)


def merge_body(*refs):
    *ins, out = refs
    total = ins[0][...].astype(F32)
    for ref in ins[1:]:
        total = total + ref[...].astype(F32)
    out[...] = total.astype(BF16)


def merge(*values):
    return call(merge_body, [PIECES], list(values))[0]


def merge_own_body(keep_ref, came_ref, from_ref, q0, q1, q2, q3, *outs):
    for a, (out, q) in enumerate(zip(outs, (q0, q1, q2, q3))):
        at = pl.ds(a * 2 * TOK, 2 * TOK)
        out[:TOK] = q[...]
        out[TOK:] = (keep_ref[at].astype(F32) + came_ref[at].astype(F32) + from_ref[at].astype(F32)).astype(BF16)


def merge_own(keep, came, from_z, dq):
    return call(merge_own_body, [((3 * TOK, HD), BF16)] * 4, [keep, came, from_z, *dq])


def enter_body(q_ref, k_ref, v_ref, s0, s1, gain_ref, cos_ref, sin_ref, o0, o1, o2, o3, rates_ref):
    _, _, _, head, _, roll = place()
    cos, sin = cos_ref[...], sin_ref[...]
    total = pltpu.roll(s0[...] + s1[...], (TOK - roll) & (TOK - 1), 1)
    rates = lax.rsqrt(total / WIDTH + epsilon)
    rates_ref[...] = rates
    turned_rates = rates.T
    for r, out in enumerate((o0, o1, o2, o3)):
        at = pl.ds(pl.multiple_of((head ^ r) * HD, HD), HD)
        for j, raw_ref in enumerate((q_ref, k_ref)):
            value = raw_ref[:, at] * turned_rates[:, j : j + 1] * gain_ref[j, :, at]
            turned = pltpu.roll(value, HD // 2, 1)
            out[j] = (value * cos + turned * sin).astype(BF16)
        out[2] = v_ref[:, at]


def enter(q_raw, k_raw, v_low, squares, gains, cos, sin):
    outs = [((3, TOK, HD), BF16)] * 4 + [((8, TOK), F32)]
    return call(enter_body, outs, [q_raw, k_raw, v_low, *squares, gains, cos, sin])


def leave_body(q_raw, k_raw, rates_ref, gain_ref, cos_ref, sin_ref, g0, g1, g2, g3, q_out, k_out, gains_out, inner_out, low):
    _, _, _, head, _, roll = place()
    cos, sin = cos_ref[...], sin_ref[...]
    rates = rates_ref[...].T
    inner = [jnp.zeros((TOK, 1), F32), jnp.zeros((TOK, 1), F32)]
    for r, ref in enumerate((g0, g1, g2, g3)):
        at = pl.ds(pl.multiple_of((head ^ r) * HD, HD), HD)
        low[:, at] = ref[2 * TOK :]
        for j, (raw_ref, out) in enumerate(((q_raw, q_out), (k_raw, k_out))):
            grad = ref[j * TOK : (j + 1) * TOK].astype(F32)
            grad = grad * cos - pltpu.roll(grad, HD // 2, 1) * sin
            raw = raw_ref[:, at]
            gains_out[j, :, at] = jnp.sum(grad * raw * rates[:, j : j + 1], axis=0, keepdims=True)
            scaled = grad * gain_ref[j, :, at]
            out[:, at] = scaled
            inner[j] = inner[j] + jnp.sum(raw * scaled, axis=1, keepdims=True)
    lane = lax.broadcasted_iota(jnp.int32, (TOK, 8), 1)
    both = jnp.where(lane == 0, inner[0], jnp.where(lane == 1, inner[1], 0.0))
    inner_out[...] = pltpu.roll(both.T, roll, 1)


def leave(q_raw, k_raw, rates, gains, cos, sin, pieces):
    outs = [((TOK, 512), F32), ((TOK, 512), F32), ((2, 1, 512), F32), ((8, TOK), F32), ((TOK, 512), BF16)]
    return call(leave_body, outs, [q_raw, k_raw, rates, gains, cos, sin, *pieces], far=(0, 1, 3, 4, 5))


def finish_body(q_raw, k_raw, q_scaled, k_scaled, rates_ref, i0, i1, v_ref, mixed_ref, q_out, k_out, mine_ref, send_ref):
    core, roll = place()[4:]
    rates = rates_ref[...]
    inner = pltpu.roll(i0[...] + i1[...], (TOK - roll) & (TOK - 1), 1)
    factor = (rates * rates * rates * inner / WIDTH).T
    rates = rates.T
    for j, raw, scaled, out in ((0, q_raw, q_scaled, q_out), (1, k_raw, k_scaled, k_out)):
        out[...] = (rates[:, j : j + 1] * scaled[...] - raw[...] * factor[:, j : j + 1]).astype(BF16)
    for own, with_query, with_key in ((0, mine_ref, send_ref), (1, send_ref, mine_ref)):

        @pl.when(core == own)
        def _(with_query=with_query, with_key=with_key):
            with_query[:, :512] = q_out[...]
            with_query[:, 512:] = v_ref[...]
            with_key[:, :512] = k_out[...]
            with_key[:, 512:] = mixed_ref[...]


def finish(q_raw, k_raw, q_scaled, k_scaled, rates, inner, v_low, mixed_low):
    outs = [((TOK, 512), BF16)] * 2 + [((TOK, 1024), BF16)] * 2
    operands = [q_raw, k_raw, q_scaled, k_scaled, rates, *inner, v_low, mixed_low]
    return call(finish_body, outs, operands, far=(0, 1))


def mean_row(value):
    return jnp.sum(value, axis=1, keepdims=True) / WIDTH


def total_of(refs):
    return (refs[0][...].astype(F32) + refs[1][...].astype(F32)) + (refs[2][...].astype(F32) + refs[3][...].astype(F32))


def branch_body(p0, p1, p2, p3, states_ref, gain_ref, hidden_ref, low_ref, norm_ref, rate_ref):
    branch = total_of((p0, p1, p2, p3))
    rate = lax.rsqrt(mean_row(branch * branch) + epsilon)
    norm = branch * rate
    hidden = states_ref[...].astype(F32) + gain_ref[...] * norm
    hidden_ref[...] = hidden
    low_ref[...] = hidden.astype(BF16)
    norm_ref[...] = norm
    rate_ref[...] = rate


def branch_norm(pieces, states, gain):
    wide = (ROWS, WIDTH)
    outs = [(wide, F32), (wide, BF16), (wide, F32), ((ROWS, 1), F32)]
    return call(branch_body, outs, [*pieces, states, gain], far=(4, 5))


def top_body(p0, p1, p2, p3, hidden_ref, gain_ref, cotangent_ref, share_ref, out_ref, low_ref, top_ref, sum_ref):
    down = total_of((p0, p1, p2, p3))
    rate = lax.rsqrt(mean_row(down * down) + epsilon)
    norm = down * rate
    gain = gain_ref[...]
    out_ref[...] = (hidden_ref[...] + gain * norm).astype(BF16)
    top = cotangent_ref[...].astype(F32) * share_ref[...]
    top_ref[...] = top
    sum_ref[...] = jnp.sum(top * norm, axis=0, keepdims=True)
    scaled = gain * top
    low_ref[...] = (rate * (scaled - norm * mean_row(scaled * norm))).astype(BF16)


def top_norm(pieces, hidden, gain, cotangent, share):
    wide = (ROWS, WIDTH)
    outs = [(wide, BF16), (wide, BF16), (wide, F32), ((1, WIDTH), F32)]
    return call(top_body, outs, [*pieces, hidden, gain, cotangent, share], far=(5, 6))


def split_rows(value):
    high = value.astype(BF16).astype(F32)
    filler = jnp.zeros((16 - 2 * value.shape[0], value.shape[1]), F32)
    return jnp.concatenate([high, value - high, filler], axis=0).astype(BF16)


def joined_rows(value, count):
    return value[:count].astype(F32) + value[count : 2 * count].astype(F32)


def hidden_body(p0, p1, p2, p3, top_ref, norm_ref, rate_ref, gain_ref, mlp_ref, mark_ref, grad_ref, low_ref):
    grad = top_ref[...] + total_of((p0, p1, p2, p3))
    grad_ref[...] = grad
    norm = norm_ref[...]
    scaled = gain_ref[...] * grad
    low_ref[:ROWS] = (rate_ref[...] * (scaled - norm * mean_row(scaled * norm))).astype(BF16)
    sums = jnp.concatenate([jnp.sum(grad * norm, axis=0, keepdims=True), mlp_ref[...]], axis=0)
    low_ref[ROWS:] = split_rows(sums)


def hidden_norm(pieces, top, norm, rate, gain, mlp_gain_sum, mark):
    outs = [((ROWS, WIDTH), F32), ((ROWS + 16, WIDTH), BF16)]
    return call(hidden_body, outs, [*pieces, top, norm, rate, gain, mlp_gain_sum, mark], far=(7,), cost=LONG)


TILE = 512
DEPTH = 4


class Weights:
    def __init__(self, weights, held, sems, turned):
        self.copies = []
        for t in range(WIDTH // TILE):
            at = pl.ds(t * TILE, TILE)
            at = (at, slice(None)) if turned else (slice(None), at)
            self.copies.append(
                [pltpu.make_async_copy(w.at[at], to.at[at], sems.at[n, t]) for n, (w, to) in enumerate(zip(weights, held))]
            )
        for t in range(DEPTH):
            self.start(t)

    def start(self, t):
        if t < len(self.copies):
            for copy in self.copies[t]:
                copy.start()

    def wait(self, t):
        for copy in self.copies[t]:
            copy.wait()
        self.start(t + DEPTH)


def rows_body(count, turned, *refs):
    lefts, weights, sems = refs[:count], refs[count : 2 * count], refs[-1]
    outs, held = refs[2 * count : -1 - count], refs[-1 - count : -1]
    arriving = Weights(weights, held, sems, turned)
    for t in range(WIDTH // TILE):
        at = pl.ds(t * TILE, TILE)
        total = None
        arriving.wait(t)
        for n in range(count):
            if turned:
                now = product_right(lefts[n][...], held[n][at])
            else:
                now = product(lefts[n][...], held[n][:, at])
            total = now if total is None else total + now
        for k in range(4):
            value = total[k * ROWS : (k + 1) * ROWS].astype(BF16)
            if len(outs) == 4:
                outs[k][:, at] = value
            else:
                row = pl.multiple_of(((k + lax.axis_index("y")) & 3) * ROWS, ROWS)
                outs[0][pl.ds(row, ROWS), at] = value


def streamed(body, outs, operands, weights, cost=COST):
    scratch = [pltpu.VMEM(w.shape, w.dtype) for w in weights]
    scratch.append(pltpu.SemaphoreType.DMA((len(weights), WIDTH // TILE)))
    return pl.pallas_call(
        body,
        out_shape=[jax.ShapeDtypeStruct(shape, kind) for shape, kind in outs],
        in_specs=[pl.BlockSpec(memory_space=pltpu.VMEM)] * len(operands)
        + [pl.BlockSpec(memory_space=pltpu.HBM)] * len(weights),
        out_specs=[pl.BlockSpec(memory_space=pltpu.VMEM)] * len(outs),
        scratch_shapes=scratch,
        compiler_params=pltpu.CompilerParams(vmem_limit_bytes=20 * 1024 * 1024),
        cost_estimate=cost,
    )(*operands, *[hbm(w) for w in weights])


def rows_product(pairs, turned=True, whole=False):
    body = functools.partial(rows_body, len(pairs), turned)
    outs = [((TOK, WIDTH), BF16)] if whole else [((ROWS, WIDTH), BF16)] * 4
    return streamed(body, outs, [left for left, _ in pairs], [right for _, right in pairs])


def rolled_rows_body(x_ref, out_ref, sems):
    y = lax.axis_index("y")
    copies = [
        pltpu.make_async_copy(x_ref.at[pl.ds(((k + y) & 3) * ROWS, ROWS)], out_ref.at[pl.ds(k * ROWS, ROWS)], sems.at[k])
        for k in range(4)
    ]
    for copy in copies:
        copy.start()
    for copy in copies:
        copy.wait()


def rolled_rows(value):
    return pl.pallas_call(
        rolled_rows_body,
        out_shape=jax.ShapeDtypeStruct(value.shape, value.dtype),
        in_specs=[pl.BlockSpec(memory_space=pltpu.HBM)],
        out_specs=pl.BlockSpec(memory_space=pltpu.VMEM),
        scratch_shapes=[pltpu.SemaphoreType.DMA((4,))],
        compiler_params=pltpu.CompilerParams(vmem_limit_bytes=VMEM_LIMIT),
        cost_estimate=COST,
    )(hbm(value))


def states_body(part_ref, grad_ref, out_ref):
    out_ref[...] = (part_ref[...].astype(F32) + grad_ref[...]).astype(BF16)


def states_sum(part, grad):
    return call(states_body, [((ROWS, WIDTH), BF16)], [part, grad], far=(1,))[0]


def act_body(h0, h1, h2, h3, gate_w, up_w, act_ref, gate_factor_ref, up_factor_ref, gate_held, up_held, sems):
    arriving = Weights((gate_w, up_w), (gate_held, up_held), sems, False)
    rows = jnp.concatenate([h0[...], h1[...], h2[...], h3[...]], axis=0)
    for t in range(WIDTH // TILE):
        at = pl.ds(t * TILE, TILE)
        arriving.wait(t)
        gate = product(rows, gate_held[:, at])
        up = product(rows, up_held[:, at])
        sigmoid = jax.nn.sigmoid(gate)
        silu = gate * sigmoid
        act_ref[:, at] = (silu * up).astype(BF16)
        gate_factor_ref[:, at] = (up * (sigmoid + silu * (1.0 - sigmoid))).astype(BF16)
        up_factor_ref[:, at] = silu.astype(BF16)


def act_product(pieces, w_gate, w_up):
    return streamed(act_body, [((TOK, WIDTH), BF16)] * 3, list(pieces), [w_gate, w_up])


def mixed_back_body(g0, g1, g2, g3, out_w, o0, o1, o2, o3, held, sem):
    copy = pltpu.make_async_copy(out_w, held, sem)
    copy.start()
    head = place()[3]
    rows = jnp.concatenate([ref[:ROWS] for ref in (g0, g1, g2, g3)], axis=0)
    copy.wait()
    for r, out in enumerate((o0, o1, o2, o3)):
        at = pl.ds(pl.multiple_of((head ^ r) * HD, HD), HD)
        out[...] = product_right(rows, held[at]).astype(BF16)


def mixed_back(pieces, w_out):
    return pl.pallas_call(
        mixed_back_body,
        out_shape=[jax.ShapeDtypeStruct((TOK, HD), BF16)] * 4,
        in_specs=[pl.BlockSpec(memory_space=pltpu.VMEM)] * 4 + [pl.BlockSpec(memory_space=pltpu.HBM)],
        out_specs=[pl.BlockSpec(memory_space=pltpu.VMEM)] * 4,
        scratch_shapes=[pltpu.VMEM(w_out.shape, BF16), pltpu.SemaphoreType.DMA],
        compiler_params=pltpu.CompilerParams(vmem_limit_bytes=VMEM_LIMIT),
        cost_estimate=COST,
    )(*pieces, hbm(w_out))


def act_back_body(g0, g1, g2, g3, gate_factor_ref, up_factor_ref, down_w, gate_ref, up_ref, down_held, sems):
    arriving = Weights((down_w,), (down_held,), sems, True)
    rows = jnp.concatenate([g0[...], g1[...], g2[...], g3[...]], axis=0)
    for t in range(WIDTH // TILE):
        at = pl.ds(t * TILE, TILE)
        arriving.wait(t)
        grad = product_right(rows, down_held[at])
        gate_ref[:, at] = (grad * gate_factor_ref[:, at].astype(F32)).astype(BF16)
        up_ref[:, at] = (grad * up_factor_ref[:, at].astype(F32)).astype(BF16)


def act_back(pieces, w_down, gate_factor, up_factor):
    return streamed(act_back_body, [((TOK, WIDTH), BF16)] * 2, [*pieces, gate_factor, up_factor], [w_down])


def columns_body(relative, *refs):
    *ins, own_ref, other_ref = refs
    x, z, core = (lax.axis_index(n) for n in ("x", "z", "c"))
    xs, zs = [x, x ^ 1, 3 - x, 3 - (x ^ 1)], [z, z ^ 1, 3 - z, 3 - (z ^ 1)]
    for k in range(BLOCKS):
        block = xs[k // 4] * 4 + zs[k % 4] if relative else k
        at = pl.ds(pl.multiple_of(block * 128, 128), 128)
        rows = jnp.concatenate([ref[: TOK // len(ins), at].astype(F32) for ref in ins], axis=0)
        turned = rows.T
        low, high = turned[:ROWS], turned[ROWS:]
        to = pl.ds(k * ROWS, ROWS)
        own_ref[to] = jnp.where(core == 0, low, high).astype(BF16)
        other_ref[to] = jnp.where(core == 0, high, low).astype(BF16)


def columns(relative, values, far=()):
    return call(functools.partial(columns_body, relative), [((BLOCKS * ROWS, TOK), BF16)] * 2, list(values), far=far)


def all_columns_body(*refs):
    *ins, out_ref = refs
    x, z = lax.axis_index("x"), lax.axis_index("z")
    xs, zs = [x, x ^ 1, 3 - x, 3 - (x ^ 1)], [z, z ^ 1, 3 - z, 3 - (z ^ 1)]
    for k in range(BLOCKS):
        at = pl.ds(pl.multiple_of((xs[k // 4] * 4 + zs[k % 4]) * 128, 128), 128)
        rows = jnp.concatenate([ref[: TOK // len(ins), at].astype(F32) for ref in ins], axis=0)
        out_ref[pl.ds(k * 128, 128)] = rows.T.astype(BF16)


def all_columns(values, far=()):
    return call(all_columns_body, [((WIDTH, TOK), BF16)], list(values), far=far)[0]


def spread_body(s0, s1, g0, g1, b0, b1, riders_ref, *outs):
    core = lax.axis_index("c")
    riders = split_rows(riders_ref[...])

    def part(n, left):
        at = pl.ds(n * 512, 512)
        right = jnp.concatenate([b0[:, at], b1[:, at]], axis=0)
        for p, out in enumerate(outs):
            blocks = [jnp.where(core == 0, p * 4 + i, i * 4 + p) * 128 for i in range(4)]
            rows = [pl.ds(pl.multiple_of(block, 128), 128) for block in blocks]
            now = jnp.concatenate([jnp.concatenate([ref[r] for ref in left], axis=1) for r in rows], axis=0)
            out[:512, at] = product(now, right).astype(BF16)

    part(0, (s0, s1))

    @pl.when(core == 0)
    def _():
        part(1, (s0, s1))

    @pl.when(core == 1)
    def _():
        part(1, (g0, g1))

    for out in outs:
        out[512:] = riders


def spread(states_left, branch_left, right, riders):
    return call(spread_body, [((528, 1024), BF16)] * 4, [*states_left, *branch_left, *right, riders])


def add_body(*refs):
    ins, outs = refs[:4], refs[4:]
    total = total_of([ref.at[pl.ds(0, 512)] for ref in ins])
    riders = [joined_rows(ref[512:], 5) for ref in ins]
    riders = split_rows((riders[0] + riders[1]) + (riders[2] + riders[3]))
    for n, out in enumerate(outs):
        out[:128] = total[n * 128 : (n + 1) * 128].astype(BF16)
        out[128:] = riders


def add_pieces(pieces):
    return call(add_body, [((144, 1024), BF16)] * 4, list(pieces))


def around(pieces, first):
    result = [pieces[0]]
    for k in (1, 2, 3):
        pairs = []
        for x in range(4):
            for z in range(4):
                for core in range(2):
                    along_x = (core == 0) == first
                    to = (PAIRINGS[k][x], z) if along_x else (x, PAIRINGS[k][z])
                    pairs.append(((x * 4 + z) * 2 + core, (to[0] * 4 + to[1]) * 2 + core))
        result.append(lax.ppermute(pieces[k], ("x", "z", "c"), pairs))
    return result


def last_body(p0, p1, p2, p3, mine_ref, send_ref, riders_ref):
    core = lax.axis_index("c")
    total = total_of((p0, p1, p2, p3))
    low, high = total[:ROWS], total[ROWS:128]
    mine_ref[...] = jnp.where(core == 0, low, high)
    send_ref[...] = jnp.where(core == 0, high, low).astype(BF16)
    riders_ref[...] = total[128 : 128 + 5] + total[128 + 5 : 128 + 10]


def last_sum(pieces):
    outs = [((ROWS, 1024), F32), ((ROWS, 1024), BF16), ((5, 1024), F32)]
    return call(last_body, outs, list(pieces))


def sum_four(pieces):
    return (pieces[0].astype(F32) + pieces[1].astype(F32)) + (pieces[2].astype(F32) + pieces[3].astype(F32))


def plain_body(base, count, *refs):
    width = 512
    each = WIDTH // width
    inputs, (out_ref, mark_ref, held, sems) = refs[: 4 * count], refs[-4:]
    copies = []
    for n in range(count * each):
        a0, a1, b0, b1 = inputs[4 * (n // each) : 4 * (n // each) + 4]
        at = pl.ds((n % each) * width, width)
        slot = n % 2
        if n >= 2:
            copies[n - 2].wait()
        left = jnp.concatenate([a0[...], a1[...]], axis=1)
        held[slot] = product(left, jnp.concatenate([b0[:, at], b1[:, at]], axis=0)).astype(BF16)
        to = out_ref.at[:, pl.ds((base * each + n) * width, width)]
        copies.append(pltpu.make_async_copy(held.at[slot], to, sems.at[slot]))
        copies[n].start()
    copies[-2].wait()
    copies[-1].wait()
    mark_ref[...] = jnp.zeros((8, 128), F32)


def plain(base, pairs, into=None):
    operands = [value for left, right in pairs for value in (*left, *right)]
    in_specs = [pl.BlockSpec(memory_space=pltpu.VMEM)] * len(operands)
    aliases = {}
    if into is not None:
        aliases = {len(operands): 0}
        in_specs.append(pl.BlockSpec(memory_space=pltpu.HBM))
        operands.append(hbm(into))
    return pl.pallas_call(
        functools.partial(plain_body, base, len(pairs)),
        out_shape=[pltpu.HBM((BLOCKS * ROWS, 3 * WIDTH), BF16), jax.ShapeDtypeStruct((8, 128), F32)],
        in_specs=in_specs,
        out_specs=[pl.BlockSpec(memory_space=pltpu.HBM), pl.BlockSpec(memory_space=pltpu.VMEM)],
        scratch_shapes=[pltpu.VMEM((2, BLOCKS * ROWS, 512), BF16), pltpu.SemaphoreType.DMA((2,))],
        input_output_aliases=aliases,
        compiler_params=pltpu.CompilerParams(vmem_limit_bytes=VMEM_LIMIT),
        cost_estimate=COST,
    )(*operands)


def rolled_columns(value, shift):
    return lax.dynamic_slice_in_dim(jnp.concatenate([value, value], axis=1), shift, TOK, 1)


class Line:
    def __init__(self, token):
        self.token = token

    def __call__(self, *values):
        values, self.token = lax.optimization_barrier((values, self.token))
        return values if len(values) > 1 else values[0]


def local(
    states,
    w_query,
    w_key,
    w_value,
    w_out,
    w_gate,
    w_up,
    w_down,
    q_gain,
    k_gain,
    attn_gain,
    mlp_gain,
    cotangent,
    segments,
    sources,
    group_weights,
):
    x = lax.axis_index("x")
    own_x, z_high, z_low, head, core, roll = place()

    def own_rows(value):
        return lax.dynamic_slice_in_dim(value, roll, ROWS, 0)

    here = (jnp.arange(TOK, dtype=jnp.int32) + roll) & (TOK - 1)
    own_block = block_of(own_x, z_high, z_low, core)
    q_blocks = jnp.stack([block_of(own_x ^ (a >> 1), z_high ^ (a & 1), z_low, core) for a in range(4)])
    q_pos = (q_blocks[:, None] * TOK + here[None]).reshape(4, 1, TOK)
    seq_segments = lax.dynamic_slice_in_dim(segments, (x >> 1) * SEQ, SEQ)
    by_block = seq_segments.reshape(BLOCKS, TOK)
    q_segments = jnp.stack([lax.dynamic_index_in_dim(by_block, q_blocks[a], 0, False) for a in range(4)])
    q_segments = lax.dynamic_slice_in_dim(jnp.concatenate([q_segments, q_segments], axis=1), roll, TOK, 1)
    q_start = jnp.sum((seq_segments[:, None, None] < q_segments[None]).astype(jnp.int32), axis=0).reshape(4, 1, TOK)

    inverse = 1.0 / theta_base ** (jnp.arange(0, HD, 2, dtype=F32) / HD)
    angles = (own_block * TOK + here).astype(F32)[:, None] * inverse[None, :]
    cosine, sine = jnp.cos(angles), jnp.sin(angles)
    cos_table = jnp.concatenate([cosine, cosine], axis=-1)
    sin_table = jnp.concatenate([-sine, sine], axis=-1)
    gains = jnp.stack([q_gain, k_gain]).reshape(2, 1, 512)

    states_here = rolled_rows(states)
    query_raw = product(states_here, w_query)
    key_raw = product(states_here, w_key)
    squares = jnp.concatenate(
        [jnp.sum(query_raw * query_raw, axis=1)[None], jnp.sum(key_raw * key_raw, axis=1)[None], jnp.zeros((6, TOK), F32)]
    )
    squares = rolled_columns(squares, (TOK - roll) & (TOK - 1))
    line = Line(roll)
    from_squares = swap(line(squares), "y", FIRST)
    value_low = line(product(states_here, w_value).astype(BF16))
    squares = line(squares + line(from_squares))
    from_squares = swap(squares, "y", SECOND)
    cos_table, sin_table = line(cos_table, sin_table)
    from_squares = line(from_squares)
    mine, to_z, to_x, to_xz, rates = enter(
        query_raw, key_raw, value_low, (squares, from_squares), gains, cos_table, sin_table
    )

    def exchange(to_z, to_x, to_xz):
        return swap(to_z, "z", SECOND), swap(to_x, "x", FIRST), swap_xz(to_xz, FIRST, SECOND)

    from_others = exchange(*line(to_z, to_x, to_xz))
    q_start = line(q_start)
    pieces = [mine, *line(from_others)]
    kv_own = line(jnp.stack([p[1:] for p in pieces], axis=1))
    kv_z = swap(kv_own, "z", FIRST)
    kv_c = swap_core(kv_own)
    q_here = line(jnp.stack([p[0] for p in pieces]))
    kv_c = line(kv_c)
    state = line(attend_first(q_here, (kv_own, kv_c), q_pos, q_start))
    kv_z = line(kv_z)
    kv_zc = line(swap_core(kv_z))
    *mixed, mixed_turned, log_total = line(attend_last(q_here, (kv_z, kv_zc), q_pos, q_start, state))
    back = jnp.stack([mixed[0], *exchange(*mixed[1:])])
    mixed_low = jnp.concatenate([lax.dynamic_index_in_dim(back, head ^ k, 0, False) for k in range(4)], axis=1)

    attn_gain, mlp_gain = attn_gain.reshape(1, WIDTH), mlp_gain.reshape(1, WIDTH)
    branch = scatter_y(line(rows_of(product(mixed_low, w_out).astype(BF16))))
    chosen = own_rows(sources)[:, None] == jnp.arange(group_weights.shape[0], dtype=jnp.int32)[None, :]
    token_share = jnp.sum(jnp.where(chosen, group_weights[None, :], 0), axis=1).astype(F32) / weight_unit
    token_share = token_share.reshape(ROWS, 1)
    states_own, cotangent_own = states_here[:ROWS], own_rows(cotangent)
    states_own, cotangent_own, token_share = line(states_own, cotangent_own, token_share)
    branch = line(branch)
    hidden, hidden_own, b_norm, b_rate = branch_norm(branch, states_own, attn_gain)
    hidden_pieces = line(gather_y(line(hidden_own)))
    act_low, gate_factor, up_factor = line(act_product(hidden_pieces, w_gate, w_up))
    down = scatter_y(line(rows_product([(act_low, w_down)], turned=False)))

    def shared_left(pair):
        return pair[0], swap_core(pair[1])

    def shared(right):
        return right, swap_core(right)

    act_right = shared(act_low)
    hidden_left = line(columns(False, hidden_pieces))
    down = line(down)
    output_own, grad_down_own, grad_top, local_mlp_gain = top_norm(down, hidden, mlp_gain, cotangent_own, token_share)

    hidden_left, act_right = line(shared_left(hidden_left), act_right)
    grad_down_pieces = gather_y(line(grad_down_own))
    states_left = shared(line(all_columns([states_here], far=(0,))))
    grad_down_pieces, states_left = line(grad_down_pieces, states_left)
    output = lax.all_gather(line(output_own), "y", axis=0, tiled=True)
    grad_gate_proj, grad_up_proj = line(act_back(grad_down_pieces, w_down, gate_factor, up_factor))
    gate_right, up_right = shared(grad_gate_proj), shared(grad_up_proj)
    down_left = shared_left(line(columns(False, grad_down_pieces)))
    hidden_part = line(rows_product([(grad_gate_proj, w_gate), (grad_up_proj, w_up)]))
    gate_right, up_right, down_left = line(gate_right, up_right, down_left)
    hidden_sum = scatter_y(line(hidden_part))

    wide_grads, mark = plain(
        0, line([(hidden_left, gate_right), (hidden_left, up_right), (down_left, act_right)])
    )
    mark = line(mark)
    output = line(output)
    wide_grads = lax.psum_scatter(wide_grads, ("x", "z"), scatter_dimension=0, tiled=True)
    hidden_sum = line(hidden_sum)
    grad_hidden, grad_branch_own = hidden_norm(
        hidden_sum, grad_top, b_norm, b_rate, attn_gain, local_mlp_gain, mark
    )

    grad_branch_pieces = line(gather_y(line(grad_branch_own)))
    to = line(mixed_back(grad_branch_pieces, w_out))
    grad_mixed_here = [to[0], *exchange(to[1], to[2], to[3])]

    branch_left = line(all_columns(grad_branch_pieces))
    wide_gains = sum(joined_rows(piece[ROWS:], 2) for piece in grad_branch_pieces)
    wide_gains = line(wide_gains.reshape(4, 1024))
    grad_mixed_here = line(grad_mixed_here)
    branch_left = shared(branch_left)
    dq_part, keep_z, send_z = line(
        attend_back(True, q_here, (kv_z, kv_zc), q_pos, q_start, grad_mixed_here, mixed_turned, log_total)
    )
    branch_left = line(branch_left)
    keep_z = line(merge(keep_z, line(swap_core(send_z))))
    from_z = swap(keep_z, "z", FIRST)

    *dq, keep_own, send_c = line(
        attend_back(
            False, q_here, (kv_own, kv_c), q_pos, q_start, grad_mixed_here, mixed_turned, log_total, dq_part
        )
    )
    from_z = line(from_z)
    came = line(swap_core(line(send_c)))
    pieces = line(merge_own(keep_own, came, from_z, dq))
    pieces = line([pieces[0], *exchange(*pieces[1:])])
    q_scaled, k_scaled, qk_gain_sums, inner, grad_value_low = line(
        leave(query_raw, key_raw, rates, gains, cos_table, sin_table, pieces)
    )
    from_inner = swap(inner, "y", FIRST)

    riders = jnp.concatenate([wide_gains, qk_gain_sums.reshape(1, 1024)])
    from_core = swap_core(riders)
    inner = line(inner + line(from_inner))
    from_inner = swap(inner, "y", SECOND)
    riders = line(riders + line(from_core))
    grad_query_raw, grad_key_raw, mine, send = line(
        finish(query_raw, key_raw, q_scaled, k_scaled, rates, (inner, line(from_inner)), grad_value_low, mixed_low)
    )
    from_other = swap_core(send)
    pairs = [(grad_query_raw, w_query), (grad_key_raw, w_key), (grad_value_low, w_value)]
    input_part = rows_product(pairs, whole=True)[0]
    input_part, wide_grads = line(input_part, wide_grads)
    input_sum = lax.psum_scatter(input_part, "y", scatter_dimension=0, tiled=True)

    pieces = line(spread(states_left, branch_left, (mine, line(from_other)), riders))
    pieces = around(pieces, True)
    wide_grads = wide_grads.astype(F32)
    wide_grads = line(
        wide_grads[:, :WIDTH], wide_grads[:, WIDTH : 2 * WIDTH], jnp.transpose(wide_grads[:, 2 * WIDTH :])
    )
    grad_states_own = line(states_sum(line(input_sum), grad_hidden))
    grad_states = lax.all_gather(grad_states_own, "y", axis=0, tiled=True)

    pieces = around(line(add_pieces(line(pieces))), False)
    own, to_other, riders = line(last_sum(line(pieces)))
    other = line(swap_core(to_other)).astype(F32)
    grad_states = line(grad_states)
    with_query, with_key = jnp.where(core == 0, own, other), jnp.where(core == 0, other, own)
    wide_gains = riders[:4].reshape(2, WIDTH)
    qk_gains = riders[4].reshape(2, 512)
    q_gain_last = jnp.where(line.token < TOK, qk_gains[0], 0.0)

    return (
        output,
        grad_states.astype(F32),
        with_query[:, :512],
        with_key[:, :512],
        with_query[:, 512:],
        jnp.transpose(with_key[:, 512:]),
        wide_grads[0],
        wide_grads[1],
        wide_grads[2],
        q_gain_last,
        qk_gains[1],
        wide_gains[0],
        wide_gains[1],
    )


def solution(mesh):
    split = Mesh(mesh.devices.reshape(4, 4, 2, 4), ("x", "z", "c", "y"))
    dp, mp = ("x", "z", "c"), "y"
    placed = (
        P(dp, None),
        P(None, mp),
        P(None, mp),
        P(None, mp),
        P(mp, None),
        P(None, mp),
        P(None, mp),
        P(mp, None),
        P(mp),
        P(mp),
        P(),
        P(),
        P(dp, None),
        P(),
        P(dp),
        P(),
    )
    return jax.shard_map(
        local,
        mesh=split,
        in_specs=placed,
        out_specs=(
            P(dp, None),
            P(dp, None),
            P(dp, mp),
            P(dp, mp),
            P(dp, mp),
            P(mp, dp),
            P(dp, mp),
            P(dp, mp),
            P(mp, dp),
            P(mp),
            P(mp),
            P(),
            P(),
        ),
        check_vma=False,
    )
```

```python
import functools

import jax
import jax.numpy as jnp
from jax import lax
from jax.experimental import pallas as pl
from jax.experimental.pallas import tpu as pltpu
from jax.sharding import Mesh
from jax.sharding import PartitionSpec as P

HD = 128
HEADS = 4
TOK = 256
ROWS = 64
BLOCKS = 16
SEQ = 4096
WIDTH = 2048
epsilon = 1e-06
theta_base = 500000.0
weight_unit = 16.0
far_below = -1e30
score_scale = HD ** (-0.5)
LOG2E = 1.4426950408889634
F32 = jnp.float32
BF16 = jnp.bfloat16

FIRST = (1, 0, 3, 2)
SECOND = (3, 2, 1, 0)
BOTH = (2, 3, 0, 1)
HERE = (0, 1, 2, 3)
PAIRINGS = (HERE, FIRST, SECOND, BOTH)
VMEM_LIMIT = 10 * 1024 * 1024
COST = pl.CostEstimate(flops=1, bytes_accessed=1, transcendentals=0)
LONG = pl.CostEstimate(flops=10**12, bytes_accessed=1, transcendentals=0)


def product(left, right):
    return jnp.dot(left, right, preferred_element_type=F32)


def product_right(left, right):
    return lax.dot_general(left, right, (((1,), (1,)), ((), ())), preferred_element_type=F32)


def product_left(left, right):
    return lax.dot_general(left, right, (((0,), (0,)), ((), ())), preferred_element_type=F32)


def swap(value, axis, pairing):
    return lax.ppermute(value, axis, [(i, pairing[i]) for i in range(4)])


def swap_core(value):
    return lax.ppermute(value, "c", [(0, 1), (1, 0)])


def swap_xz(value, x_pairing, z_pairing):
    pairs = [(i * 4 + j, x_pairing[i] * 4 + z_pairing[j]) for i in range(4) for j in range(4)]
    return lax.ppermute(value, ("x", "z"), pairs)


def shift_y(value, step):
    return lax.ppermute(value, "y", [(i, (i + step) % 4) for i in range(4)])


def scatter_y(pieces):
    return [pieces[0]] + [shift_y(pieces[k], k) for k in (1, 2, 3)]


def gather_y(own):
    return [own] + [shift_y(own, -k) for k in (1, 2, 3)]


def rows_of(value):
    return [value[k * ROWS : (k + 1) * ROWS] for k in range(4)]


def fetching(body, far, *refs):
    held, sems = refs[-1 - len(far) : -1], refs[-1]
    refs = list(refs[: -1 - len(far)])
    copies = [pltpu.make_async_copy(refs[at], held[n], sems.at[n]) for n, at in enumerate(far)]
    for copy in copies:
        copy.start()
    for n, at in enumerate(far):
        copies[n].wait()
        refs[at] = held[n]
    body(*refs)


def hbm(value):
    return pltpu.with_memory_space_constraint(value, pltpu.HBM)


def call(body, outs, operands, scratch=(), limit=VMEM_LIMIT, far=(), cost=COST):
    in_specs = [pl.BlockSpec(memory_space=pltpu.VMEM)] * len(operands)
    scratch = list(scratch)
    if far:
        body = functools.partial(fetching, body, far)
        operands = list(operands)
        for at in far:
            operands[at] = hbm(operands[at])
            in_specs[at] = pl.BlockSpec(memory_space=pltpu.HBM)
            scratch.append(pltpu.VMEM(operands[at].shape, operands[at].dtype))
        scratch.append(pltpu.SemaphoreType.DMA((len(far),)))
    return pl.pallas_call(
        body,
        out_shape=[jax.ShapeDtypeStruct(s, d) for s, d in outs],
        in_specs=in_specs,
        out_specs=[pl.BlockSpec(memory_space=pltpu.VMEM)] * len(outs),
        scratch_shapes=scratch,
        compiler_params=pltpu.CompilerParams(vmem_limit_bytes=limit),
        cost_estimate=cost,
    )(*operands)


def place():
    x, z, core, y = (lax.axis_index(n) for n in ("x", "z", "c", "y"))
    own_x, high, low = x & 1, z >> 1, (z ^ (z >> 1)) & 1
    return own_x, high, low, own_x * 2 + high, core, y * ROWS


def block_of(x_bit, high, low, core):
    return x_bit * 8 + (high * 2 + (low ^ high)) * 2 + core


def key_tile(group, xb, own_x, high, low, core, kv):
    start = (own_x ^ xb) * 2
    k = kv[0, pl.ds(start, 2)].reshape(2 * TOK, HD)
    v = kv[1, pl.ds(start, 2)].reshape(2 * TOK, HD)
    return start, k, v


def tile_blocks(group, xb, high, low, core):
    return [block_of(xb, high ^ n, low ^ (group >> 1), core ^ (group & 1)) for n in (0, 1)]


def allowed(first, second, roll, qpos, qstart):
    row = lax.broadcasted_iota(jnp.int32, (2 * TOK, TOK), 0)
    at = ((row + roll) & (TOK - 1)) + jnp.where(row < TOK, first, second) * TOK
    return (at <= qpos) & (at >= qstart)


def attend_body(groups, q_ref, kva, kvb, qpos_ref, qstart_ref, *refs):
    own_x, high, low, _, core, roll = place()
    last = groups == (2, 3)
    if last:
        m_in, l_in, acc_in, o0, o1, o2, o3, ot_ref, lse_ref, m_ref, l_ref, acc_ref = refs
        m_ref[...] = m_in[...]
        l_ref[...] = l_in[...]
        acc_ref[...] = acc_in[...]
    else:
        m_ref, l_ref, acc_ref = refs
        m_ref[...] = jnp.full_like(m_ref, far_below)
        l_ref[...] = jnp.zeros_like(l_ref)
        acc_ref[...] = jnp.zeros_like(acc_ref)

    @pl.loop(0, 4)
    def _(a):
        block = block_of(own_x ^ (a >> 1), high ^ (a & 1), low, core)
        q = q_ref[a]
        qpos = qpos_ref[a]
        qstart = qstart_ref[a]
        for xb in range(2):
            for group, kv in zip(groups, (kva, kvb)):
                first, second = tile_blocks(group, xb, high, low, core)

                @pl.when(jnp.minimum(first, second) <= block)
                def _(group=group, kv=kv, xb=xb, first=first, second=second):
                    _, k, v = key_tile(group, xb, own_x, high, low, core, kv)
                    s = product_right(k, q)
                    s = jnp.where(allowed(first, second, roll, qpos, qstart), s, far_below)
                    m_old = m_ref[a]
                    m_new = jnp.maximum(m_old, jnp.max(s, axis=0, keepdims=True))
                    p = jnp.exp2((s - m_new) * (score_scale * LOG2E))
                    alpha = jnp.exp2((m_old - m_new) * (score_scale * LOG2E))
                    l_ref[a] = alpha * l_ref[a] + jnp.sum(p, axis=0, keepdims=True)
                    acc_ref[a] = alpha * acc_ref[a] + product_left(v, p.astype(BF16))
                    m_ref[a] = m_new

    if last:
        for a, out in enumerate((o0, o1, o2, o3)):
            mixed = acc_ref[a] / l_ref[a]
            ot_ref[a] = mixed
            out[...] = mixed.T.astype(BF16)
            lse_ref[a] = m_ref[a] * (score_scale * LOG2E) + jnp.log2(l_ref[a])


STATE = [((4, 1, TOK), F32), ((4, 1, TOK), F32), ((4, HD, TOK), F32)]


def attend_first(q, kvs, qpos, qstart):
    return call(functools.partial(attend_body, (0, 1)), STATE, [q, *kvs, qpos, qstart])


def attend_last(q, kvs, qpos, qstart, state):
    outs = [((TOK, HD), BF16)] * 4 + [((4, HD, TOK), F32), ((4, 1, TOK), F32)]
    scratch = [pltpu.VMEM(shape, kind) for shape, kind in STATE]
    return call(functools.partial(attend_body, (2, 3)), outs, [q, *kvs, qpos, qstart, *state], scratch=scratch)


def attend_back_body(groups, q_ref, kva, kvb, qpos_ref, qstart_ref, do0, do1, do2, do3, ot_ref, lse_ref, *refs):
    own_x, high, low, _, core, roll = place()
    last = groups == (0, 1)
    if last:
        dq_in, d0, d1, d2, d3, keep_ref, send_ref, acc_ref, dqt_ref, do_ref = refs
        dqt_ref[...] = dq_in[...]
    else:
        dqt_ref, keep_ref, send_ref, acc_ref, do_ref = refs
        dqt_ref[...] = jnp.zeros_like(dqt_ref)
    acc_ref[...] = jnp.zeros_like(acc_ref)
    for a, ref in enumerate((do0, do1, do2, do3)):
        do_ref[a] = ref[...]

    @pl.loop(0, 4)
    def _(a):
        block = block_of(own_x ^ (a >> 1), high ^ (a & 1), low, core)
        q = q_ref[a]
        do = do_ref[a]
        delta = jnp.sum(do.astype(F32).T * ot_ref[a], axis=0, keepdims=True)
        lse = lse_ref[a]
        qpos = qpos_ref[a]
        qstart = qstart_ref[a]
        for xb in range(2):
            for n, (group, kv) in enumerate(zip(groups, (kva, kvb))):
                first, second = tile_blocks(group, xb, high, low, core)

                @pl.when(jnp.minimum(first, second) <= block)
                def _(n=n, group=group, kv=kv, xb=xb, first=first, second=second):
                    start, k, v = key_tile(group, xb, own_x, high, low, core, kv)
                    s = product_right(k, q)
                    dp = product_right(v, do)
                    keep = allowed(first, second, roll, qpos, qstart)
                    p = jnp.where(keep, jnp.exp2(s * (score_scale * LOG2E) - lse), 0.0)
                    ds = (p * (dp - delta)).astype(BF16)
                    dqt_ref[a] += product_left(k, ds)
                    acc_ref[n, 0, pl.ds(start, 2)] += product(ds, q).reshape(2, TOK, HD)
                    acc_ref[n, 1, pl.ds(start, 2)] += product(p.astype(BF16), do).reshape(2, TOK, HD)

    if last:
        for a, out in enumerate((d0, d1, d2, d3)):
            out[...] = (dqt_ref[a] * score_scale).T.astype(BF16)
    for n, out in enumerate((keep_ref, send_ref)):
        for at in range(4):
            for j in range(2):
                factor = score_scale if j == 0 else 1.0
                out[pl.ds((at * 2 + j) * TOK, TOK)] = (acc_ref[n, j, at] * factor).astype(BF16)


PIECES = ((8 * TOK, HD), BF16)


def attend_back(first, q, kvs, qpos, qstart, do, ot, lse, dq=None):
    scratch = [pltpu.VMEM((2, 2, 4, TOK, HD), F32)]
    operands = [q, *kvs, qpos, qstart, *do, ot, lse]
    if first:
        outs = [((4, HD, TOK), F32), PIECES, PIECES]
    else:
        outs = [((TOK, HD), BF16)] * 4 + [PIECES, PIECES]
        operands.append(dq)
        scratch.append(pltpu.VMEM((4, HD, TOK), F32))
    scratch.append(pltpu.VMEM((4, TOK, HD), BF16))
    body = functools.partial(attend_back_body, (2, 3) if first else (0, 1))
    far = (0, 1, 2, 3, 4, 9, 10) if first else ()
    return call(body, outs, operands, scratch=scratch, limit=16 * 1024 * 1024, far=far)


def merge_body(*refs):
    *ins, out = refs
    total = ins[0][...].astype(F32)
    for ref in ins[1:]:
        total = total + ref[...].astype(F32)
    out[...] = total.astype(BF16)


def merge(*values):
    return call(merge_body, [PIECES], list(values))[0]


def merge_own_body(keep_ref, came_ref, from_ref, q0, q1, q2, q3, *outs):
    for a, (out, q) in enumerate(zip(outs, (q0, q1, q2, q3))):
        at = pl.ds(a * 2 * TOK, 2 * TOK)
        out[:TOK] = q[...]
        out[TOK:] = (keep_ref[at].astype(F32) + came_ref[at].astype(F32) + from_ref[at].astype(F32)).astype(BF16)


def merge_own(keep, came, from_z, dq):
    return call(merge_own_body, [((3 * TOK, HD), BF16)] * 4, [keep, came, from_z, *dq])


def enter_body(q_ref, k_ref, v_ref, s0, s1, gain_ref, cos_ref, sin_ref, o0, o1, o2, o3, rates_ref):
    _, _, _, head, _, roll = place()
    cos, sin = cos_ref[...], sin_ref[...]
    total = pltpu.roll(s0[...] + s1[...], (TOK - roll) & (TOK - 1), 1)
    rates = lax.rsqrt(total / WIDTH + epsilon)
    rates_ref[...] = rates
    turned_rates = rates.T
    for r, out in enumerate((o0, o1, o2, o3)):
        at = pl.ds(pl.multiple_of((head ^ r) * HD, HD), HD)
        for j, raw_ref in enumerate((q_ref, k_ref)):
            value = raw_ref[:, at] * turned_rates[:, j : j + 1] * gain_ref[j, :, at]
            turned = pltpu.roll(value, HD // 2, 1)
            out[j] = (value * cos + turned * sin).astype(BF16)
        out[2] = v_ref[:, at]


def enter(q_raw, k_raw, v_low, squares, gains, cos, sin):
    outs = [((3, TOK, HD), BF16)] * 4 + [((8, TOK), F32)]
    return call(enter_body, outs, [q_raw, k_raw, v_low, *squares, gains, cos, sin])


def leave_body(
    q_raw, k_raw, rates_ref, gain_ref, cos_ref, sin_ref, mixed_ref, g0, g1, g2, g3,
    q_out, k_out, gains_out, inner_out, low, mine_ref, send_ref,
):
    _, _, _, head, core, roll = place()
    cos, sin = cos_ref[...], sin_ref[...]
    rates = rates_ref[...].T
    inner = [jnp.zeros((TOK, 1), F32), jnp.zeros((TOK, 1), F32)]
    for r, ref in enumerate((g0, g1, g2, g3)):
        at = pl.ds(pl.multiple_of((head ^ r) * HD, HD), HD)
        low[:, at] = ref[2 * TOK :]
        for j, (raw_ref, out) in enumerate(((q_raw, q_out), (k_raw, k_out))):
            grad = ref[j * TOK : (j + 1) * TOK].astype(F32)
            grad = grad * cos - pltpu.roll(grad, HD // 2, 1) * sin
            raw = raw_ref[:, at]
            gains_out[j, :, at] = jnp.sum(grad * raw * rates[:, j : j + 1], axis=0, keepdims=True)
            scaled = grad * gain_ref[j, :, at]
            out[:, at] = scaled
            inner[j] = inner[j] + jnp.sum(raw * scaled, axis=1, keepdims=True)
    lane = lax.broadcasted_iota(jnp.int32, (TOK, 8), 1)
    both = jnp.where(lane == 0, inner[0], jnp.where(lane == 1, inner[1], 0.0))
    inner_out[...] = pltpu.roll(both.T, roll, 1)
    give(core, low, mixed_ref, mine_ref, send_ref)


def give(core, first_ref, second_ref, mine_ref, send_ref):
    @pl.when(core == 0)
    def _():
        mine_ref[...] = first_ref[...]
        send_ref[...] = second_ref[...]

    @pl.when(core == 1)
    def _():
        mine_ref[...] = second_ref[...]
        send_ref[...] = first_ref[...]


def leave(q_raw, k_raw, rates, gains, cos, sin, mixed_low, pieces):
    outs = [((TOK, 512), F32), ((TOK, 512), F32), ((2, 1, 512), F32), ((8, TOK), F32)] + [((TOK, 512), BF16)] * 3
    operands = [q_raw, k_raw, rates, gains, cos, sin, mixed_low, *pieces]
    return call(leave_body, outs, operands, far=(0, 1, 3, 4, 5, 6))


def finish_body(q_raw, k_raw, q_scaled, k_scaled, rates_ref, i0, i1, q_out, k_out, mine_ref, send_ref):
    core, roll = place()[4:]
    rates = rates_ref[...]
    inner = pltpu.roll(i0[...] + i1[...], (TOK - roll) & (TOK - 1), 1)
    factor = (rates * rates * rates * inner / WIDTH).T
    rates = rates.T
    for j, raw, scaled, out in ((0, q_raw, q_scaled, q_out), (1, k_raw, k_scaled, k_out)):
        out[...] = (rates[:, j : j + 1] * scaled[...] - raw[...] * factor[:, j : j + 1]).astype(BF16)
    give(core, q_out, k_out, mine_ref, send_ref)


def finish(q_raw, k_raw, q_scaled, k_scaled, rates, inner):
    outs = [((TOK, 512), BF16)] * 4
    return call(finish_body, outs, [q_raw, k_raw, q_scaled, k_scaled, rates, *inner], far=(0, 1))


def mean_row(value):
    return jnp.sum(value, axis=1, keepdims=True) / WIDTH


def total_of(refs):
    return (refs[0][...].astype(F32) + refs[1][...].astype(F32)) + (refs[2][...].astype(F32) + refs[3][...].astype(F32))


def branch_body(p0, p1, p2, p3, states_ref, gain_ref, hidden_ref, low_ref, norm_ref, rate_ref):
    branch = total_of((p0, p1, p2, p3))
    rate = lax.rsqrt(mean_row(branch * branch) + epsilon)
    norm = branch * rate
    hidden = states_ref[...].astype(F32) + gain_ref[...] * norm
    hidden_ref[...] = hidden
    low_ref[...] = hidden.astype(BF16)
    norm_ref[...] = norm
    rate_ref[...] = rate


def branch_norm(pieces, states, gain):
    wide = (ROWS, WIDTH)
    outs = [(wide, F32), (wide, BF16), (wide, F32), ((ROWS, 1), F32)]
    return call(branch_body, outs, [*pieces, states, gain], far=(4, 5))


def top_body(p0, p1, p2, p3, hidden_ref, gain_ref, cotangent_ref, share_ref, out_ref, low_ref, top_ref, sum_ref):
    down = total_of((p0, p1, p2, p3))
    rate = lax.rsqrt(mean_row(down * down) + epsilon)
    norm = down * rate
    gain = gain_ref[...]
    out_ref[...] = (hidden_ref[...] + gain * norm).astype(BF16)
    top = cotangent_ref[...].astype(F32) * share_ref[:, :1]
    top_ref[...] = top
    sum_ref[...] = jnp.sum(top * norm, axis=0, keepdims=True)
    scaled = gain * top
    low_ref[...] = (rate * (scaled - norm * mean_row(scaled * norm))).astype(BF16)


def top_norm(pieces, hidden, gain, cotangent, share):
    wide = (ROWS, WIDTH)
    outs = [(wide, BF16), (wide, BF16), (wide, F32), ((1, WIDTH), F32)]
    return call(top_body, outs, [*pieces, hidden, gain, cotangent, share], far=(5, 6, 7))


def split_rows(value):
    high = value.astype(BF16).astype(F32)
    filler = jnp.zeros((16 - 2 * value.shape[0], value.shape[1]), F32)
    return jnp.concatenate([high, value - high, filler], axis=0).astype(BF16)


def joined_rows(value, count):
    return value[:count].astype(F32) + value[count : 2 * count].astype(F32)


def hidden_body(p0, p1, p2, p3, top_ref, norm_ref, rate_ref, gain_ref, mlp_ref, mark_ref, grad_ref, low_ref, sum_ref):
    grad = top_ref[...] + total_of((p0, p1, p2, p3))
    grad_ref[...] = grad
    norm = norm_ref[...]
    scaled = gain_ref[...] * grad
    low_ref[...] = (rate_ref[...] * (scaled - norm * mean_row(scaled * norm))).astype(BF16)
    sums = (jnp.sum(grad * norm, axis=0, keepdims=True), mlp_ref[...])
    for n in range(4):
        sum_ref[n : n + 1] = sums[n // 2][:, (n % 2) * 1024 : (n % 2 + 1) * 1024]


def hidden_norm(pieces, top, norm, rate, gain, mlp_gain_sum, mark):
    outs = [((ROWS, WIDTH), F32), ((ROWS, WIDTH), BF16), ((4, 1024), F32)]
    operands = [*pieces, top, norm, rate, gain, mlp_gain_sum, mark]
    return call(hidden_body, outs, operands, far=(7,), cost=LONG)


TILE = 512
DEPTH = 4


class Weights:
    def __init__(self, weights, held, sems, turned):
        self.copies = []
        for t in range(WIDTH // TILE):
            at = pl.ds(t * TILE, TILE)
            at = (at, slice(None)) if turned else (slice(None), at)
            self.copies.append(
                [pltpu.make_async_copy(w.at[at], to.at[at], sems.at[n, t]) for n, (w, to) in enumerate(zip(weights, held))]
            )
        for t in range(DEPTH):
            self.start(t)

    def start(self, t):
        if t < len(self.copies):
            for copy in self.copies[t]:
                copy.start()

    def wait(self, t):
        for copy in self.copies[t]:
            copy.wait()
        self.start(t + DEPTH)


def rows_body(count, turned, *refs):
    lefts, weights, sems = refs[:count], refs[count : 2 * count], refs[-1]
    outs, held = refs[2 * count : -1 - count], refs[-1 - count : -1]
    arriving = Weights(weights, held, sems, turned)
    for t in range(WIDTH // TILE):
        at = pl.ds(t * TILE, TILE)
        total = None
        arriving.wait(t)
        for n in range(count):
            if turned:
                now = product_right(lefts[n][...], held[n][at])
            else:
                now = product(lefts[n][...], held[n][:, at])
            total = now if total is None else total + now
        for k in range(4):
            value = total[k * ROWS : (k + 1) * ROWS].astype(BF16)
            if len(outs) == 4:
                outs[k][:, at] = value
            else:
                row = pl.multiple_of(((k + lax.axis_index("y")) & 3) * ROWS, ROWS)
                outs[0][pl.ds(row, ROWS), at] = value


def streamed(body, outs, operands, weights, cost=COST):
    scratch = [pltpu.VMEM(w.shape, w.dtype) for w in weights]
    scratch.append(pltpu.SemaphoreType.DMA((len(weights), WIDTH // TILE)))
    return pl.pallas_call(
        body,
        out_shape=[jax.ShapeDtypeStruct(shape, kind) for shape, kind in outs],
        in_specs=[pl.BlockSpec(memory_space=pltpu.VMEM)] * len(operands)
        + [pl.BlockSpec(memory_space=pltpu.HBM)] * len(weights),
        out_specs=[pl.BlockSpec(memory_space=pltpu.VMEM)] * len(outs),
        scratch_shapes=scratch,
        compiler_params=pltpu.CompilerParams(vmem_limit_bytes=20 * 1024 * 1024),
        cost_estimate=cost,
    )(*operands, *[hbm(w) for w in weights])


def rows_product(pairs, turned=True, whole=False):
    body = functools.partial(rows_body, len(pairs), turned)
    outs = [((TOK, WIDTH), BF16)] if whole else [((ROWS, WIDTH), BF16)] * 4
    return streamed(body, outs, [left for left, _ in pairs], [right for _, right in pairs])


def rolled_rows_body(x_ref, out_ref, sems):
    y = lax.axis_index("y")
    copies = [
        pltpu.make_async_copy(x_ref.at[pl.ds(((k + y) & 3) * ROWS, ROWS)], out_ref.at[pl.ds(k * ROWS, ROWS)], sems.at[k])
        for k in range(4)
    ]
    for copy in copies:
        copy.start()
    for copy in copies:
        copy.wait()


def rolled_rows(value):
    return pl.pallas_call(
        rolled_rows_body,
        out_shape=jax.ShapeDtypeStruct(value.shape, value.dtype),
        in_specs=[pl.BlockSpec(memory_space=pltpu.HBM)],
        out_specs=pl.BlockSpec(memory_space=pltpu.VMEM),
        scratch_shapes=[pltpu.SemaphoreType.DMA((4,))],
        compiler_params=pltpu.CompilerParams(vmem_limit_bytes=VMEM_LIMIT),
        cost_estimate=COST,
    )(hbm(value))


def states_body(p0, p1, p2, p3, grad_ref, out_ref):
    out_ref[...] = (total_of((p0, p1, p2, p3)) + grad_ref[...]).astype(BF16)


def states_sum(pieces, grad):
    return call(states_body, [((ROWS, WIDTH), BF16)], [*pieces, grad], far=(4,))[0]


def unrolled_body(p0, p1, p2, p3, out_ref):
    y = lax.axis_index("y")
    for k, ref in enumerate((p0, p1, p2, p3)):
        at = pl.multiple_of(((k + y) & 3) * ROWS, ROWS)
        out_ref[pl.ds(at, ROWS)] = ref[...]


def unrolled(pieces):
    return call(unrolled_body, [((TOK, WIDTH), BF16)], list(pieces))[0]


def act_body(h0, h1, h2, h3, gate_w, up_w, act_ref, gate_factor_ref, up_factor_ref, gate_held, up_held, sems):
    arriving = Weights((gate_w, up_w), (gate_held, up_held), sems, False)
    rows = jnp.concatenate([h0[...], h1[...], h2[...], h3[...]], axis=0)
    for t in range(WIDTH // TILE):
        at = pl.ds(t * TILE, TILE)
        arriving.wait(t)
        gate = product(rows, gate_held[:, at])
        up = product(rows, up_held[:, at])
        sigmoid = jax.nn.sigmoid(gate)
        silu = gate * sigmoid
        act_ref[:, at] = (silu * up).astype(BF16)
        gate_factor_ref[:, at] = (up * (sigmoid + silu * (1.0 - sigmoid))).astype(BF16)
        up_factor_ref[:, at] = silu.astype(BF16)


def act_product(pieces, w_gate, w_up):
    return streamed(act_body, [((TOK, WIDTH), BF16)] * 3, list(pieces), [w_gate, w_up])


def out_body(m0, m1, m2, m3, out_w, low_ref, o0, o1, o2, o3, held, sem):
    copy = pltpu.make_async_copy(out_w, held, sem)
    copy.start()
    head = place()[3]
    for r, ref in enumerate((m0, m1, m2, m3)):
        low_ref[:, pl.ds(pl.multiple_of((head ^ r) * HD, HD), HD)] = ref[...]
    copy.wait()
    branch = product(low_ref[...], held[...])
    for k, out in enumerate((o0, o1, o2, o3)):
        out[...] = branch[k * ROWS : (k + 1) * ROWS].astype(BF16)


def out_product(mixed, w_out):
    return pl.pallas_call(
        out_body,
        out_shape=[jax.ShapeDtypeStruct((TOK, 512), BF16)] + [jax.ShapeDtypeStruct((ROWS, WIDTH), BF16)] * 4,
        in_specs=[pl.BlockSpec(memory_space=pltpu.VMEM)] * 4 + [pl.BlockSpec(memory_space=pltpu.HBM)],
        out_specs=[pl.BlockSpec(memory_space=pltpu.VMEM)] * 5,
        scratch_shapes=[pltpu.VMEM(w_out.shape, BF16), pltpu.SemaphoreType.DMA],
        compiler_params=pltpu.CompilerParams(vmem_limit_bytes=VMEM_LIMIT),
        cost_estimate=COST,
    )(*mixed, hbm(w_out))


def mixed_back_body(g0, g1, g2, g3, out_w, o0, o1, o2, o3, held, sem):
    copy = pltpu.make_async_copy(out_w, held, sem)
    copy.start()
    head = place()[3]
    rows = jnp.concatenate([g0[...], g1[...], g2[...], g3[...]], axis=0)
    copy.wait()
    for r, out in enumerate((o0, o1, o2, o3)):
        at = pl.ds(pl.multiple_of((head ^ r) * HD, HD), HD)
        out[...] = product_right(rows, held[at]).astype(BF16)


def mixed_back(pieces, w_out):
    return pl.pallas_call(
        mixed_back_body,
        out_shape=[jax.ShapeDtypeStruct((TOK, HD), BF16)] * 4,
        in_specs=[pl.BlockSpec(memory_space=pltpu.VMEM)] * 4 + [pl.BlockSpec(memory_space=pltpu.HBM)],
        out_specs=[pl.BlockSpec(memory_space=pltpu.VMEM)] * 4,
        scratch_shapes=[pltpu.VMEM(w_out.shape, BF16), pltpu.SemaphoreType.DMA],
        compiler_params=pltpu.CompilerParams(vmem_limit_bytes=VMEM_LIMIT),
        cost_estimate=COST,
    )(*pieces, hbm(w_out))


def act_back_body(g0, g1, g2, g3, gate_factor_ref, up_factor_ref, down_w, gate_ref, up_ref, down_held, sems):
    arriving = Weights((down_w,), (down_held,), sems, True)
    rows = jnp.concatenate([g0[...], g1[...], g2[...], g3[...]], axis=0)
    for t in range(WIDTH // TILE):
        at = pl.ds(t * TILE, TILE)
        arriving.wait(t)
        grad = product_right(rows, down_held[at])
        gate_ref[:, at] = (grad * gate_factor_ref[:, at].astype(F32)).astype(BF16)
        up_ref[:, at] = (grad * up_factor_ref[:, at].astype(F32)).astype(BF16)


def act_back(pieces, w_down, gate_factor, up_factor):
    return streamed(act_back_body, [((TOK, WIDTH), BF16)] * 2, [*pieces, gate_factor, up_factor], [w_down])


def columns_body(relative, *refs):
    *ins, own_ref, other_ref = refs
    x, z, core = (lax.axis_index(n) for n in ("x", "z", "c"))
    xs, zs = [x, x ^ 1, 3 - x, 3 - (x ^ 1)], [z, z ^ 1, 3 - z, 3 - (z ^ 1)]
    for k in range(BLOCKS):
        block = xs[k // 4] * 4 + zs[k % 4] if relative else k
        at = pl.ds(pl.multiple_of(block * 128, 128), 128)
        rows = jnp.concatenate([ref[:, at].astype(F32) for ref in ins], axis=0)
        turned = rows.T
        low, high = turned[:ROWS], turned[ROWS:]
        to = pl.ds(k * ROWS, ROWS)
        own_ref[to] = jnp.where(core == 0, low, high).astype(BF16)
        other_ref[to] = jnp.where(core == 0, high, low).astype(BF16)


def columns(relative, values, far=()):
    return call(functools.partial(columns_body, relative), [((BLOCKS * ROWS, TOK), BF16)] * 2, list(values), far=far)


def all_columns_body(*refs):
    *ins, out_ref = refs
    x, z = lax.axis_index("x"), lax.axis_index("z")
    xs, zs = [x, x ^ 1, 3 - x, 3 - (x ^ 1)], [z, z ^ 1, 3 - z, 3 - (z ^ 1)]
    for k in range(BLOCKS):
        at = pl.ds(pl.multiple_of((xs[k // 4] * 4 + zs[k % 4]) * 128, 128), 128)
        rows = jnp.concatenate([ref[:, at].astype(F32) for ref in ins], axis=0)
        out_ref[pl.ds(k * 128, 128)] = rows.T.astype(BF16)


def all_columns(values, far=()):
    return call(all_columns_body, [((WIDTH, TOK), BF16)], list(values), far=far)[0]


def spread_part(left, right, outs):
    core = lax.axis_index("c")
    for p, out in enumerate(outs):
        blocks = [jnp.where(core == 0, p * 4 + i, i * 4 + p) * 128 for i in range(4)]
        rows = [pl.ds(pl.multiple_of(block, 128), 128) for block in blocks]
        now = jnp.concatenate([jnp.concatenate([ref[r] for ref in left], axis=1) for r in rows], axis=0)
        out[:512, :512] = product(now, right).astype(BF16)


def spread_first_body(s0, s1, g0, g1, b0, b1, *outs):
    core = lax.axis_index("c")
    right = jnp.concatenate([b0[...], b1[...]], axis=0)

    @pl.when(core == 0)
    def _():
        spread_part((s0, s1), right, outs)

    @pl.when(core == 1)
    def _():
        spread_part((g0, g1), right, outs)


def spread_last_body(s0, s1, b0, b1, riders_ref, *refs):
    ins, outs = refs[:4], refs[4:]
    riders = split_rows(riders_ref[...])
    for ref, out in zip(ins, outs):
        out[:512, 512:] = ref[...]
        out[512:] = riders
    spread_part((s0, s1), jnp.concatenate([b0[...], b1[...]], axis=0), outs)


def spread_first(states_left, branch_left, right):
    return call(spread_first_body, [((512, 512), BF16)] * 4, [*states_left, *branch_left, *right])


def spread_last(states_left, right, riders, pieces):
    return call(spread_last_body, [((528, 1024), BF16)] * 4, [*states_left, *right, riders, *pieces])


def add_body(*refs):
    ins, outs = refs[:4], refs[4:]
    total = total_of([ref.at[pl.ds(0, 512)] for ref in ins])
    riders = [joined_rows(ref[512:], 5) for ref in ins]
    riders = split_rows((riders[0] + riders[1]) + (riders[2] + riders[3]))
    for n, out in enumerate(outs):
        out[:128] = total[n * 128 : (n + 1) * 128].astype(BF16)
        out[128:] = riders


def add_pieces(pieces):
    return call(add_body, [((144, 1024), BF16)] * 4, list(pieces))


def around(value, k, first):
    pairs = []
    for x in range(4):
        for z in range(4):
            for core in range(2):
                to = (PAIRINGS[k][x], z) if (core == 0) == first else (x, PAIRINGS[k][z])
                pairs.append(((x * 4 + z) * 2 + core, (to[0] * 4 + to[1]) * 2 + core))
    return lax.ppermute(value, ("x", "z", "c"), pairs)


def last_body(p0, p1, p2, p3, mine_ref, send_ref, riders_ref):
    core = lax.axis_index("c")
    total = total_of((p0, p1, p2, p3))
    low, high = total[:ROWS], total[ROWS:128]
    mine_ref[...] = jnp.where(core == 0, low, high)
    send_ref[...] = jnp.where(core == 0, high, low).astype(BF16)
    riders_ref[...] = total[128 : 128 + 5] + total[128 + 5 : 128 + 10]


def last_sum(pieces):
    outs = [((ROWS, 1024), F32), ((ROWS, 1024), BF16), ((5, 1024), F32)]
    return call(last_body, outs, list(pieces))


def sum_four(pieces):
    return (pieces[0].astype(F32) + pieces[1].astype(F32)) + (pieces[2].astype(F32) + pieces[3].astype(F32))


def plain_body(base, count, *refs):
    width = 512
    each = WIDTH // width
    inputs, (out_ref, mark_ref, held, sems) = refs[: 4 * count], refs[-4:]
    copies = []
    for n in range(count * each):
        a0, a1, b0, b1 = inputs[4 * (n // each) : 4 * (n // each) + 4]
        at = pl.ds((n % each) * width, width)
        slot = n % 2
        if n >= 2:
            copies[n - 2].wait()
        left = jnp.concatenate([a0[...], a1[...]], axis=1)
        held[slot] = product(left, jnp.concatenate([b0[:, at], b1[:, at]], axis=0)).astype(BF16)
        to = out_ref.at[:, pl.ds((base * each + n) * width, width)]
        copies.append(pltpu.make_async_copy(held.at[slot], to, sems.at[slot]))
        copies[n].start()
    copies[-2].wait()
    copies[-1].wait()
    mark_ref[...] = jnp.zeros((8, 128), F32)


def plain(base, pairs, into=None):
    operands = [value for left, right in pairs for value in (*left, *right)]
    in_specs = [pl.BlockSpec(memory_space=pltpu.VMEM)] * len(operands)
    aliases = {}
    if into is not None:
        aliases = {len(operands): 0}
        in_specs.append(pl.BlockSpec(memory_space=pltpu.HBM))
        operands.append(hbm(into))
    return pl.pallas_call(
        functools.partial(plain_body, base, len(pairs)),
        out_shape=[pltpu.HBM((BLOCKS * ROWS, 3 * WIDTH), BF16), jax.ShapeDtypeStruct((8, 128), F32)],
        in_specs=in_specs,
        out_specs=[pl.BlockSpec(memory_space=pltpu.HBM), pl.BlockSpec(memory_space=pltpu.VMEM)],
        scratch_shapes=[pltpu.VMEM((2, BLOCKS * ROWS, 512), BF16), pltpu.SemaphoreType.DMA((2,))],
        input_output_aliases=aliases,
        compiler_params=pltpu.CompilerParams(vmem_limit_bytes=VMEM_LIMIT),
        cost_estimate=COST,
    )(*operands)


def rolled_columns(value, shift):
    return lax.dynamic_slice_in_dim(jnp.concatenate([value, value], axis=1), shift, TOK, 1)


class Line:
    def __init__(self, token):
        self.token = token

    def __call__(self, *values):
        values, self.token = lax.optimization_barrier((values, self.token))
        return values if len(values) > 1 else values[0]


def local(
    states,
    w_query,
    w_key,
    w_value,
    w_out,
    w_gate,
    w_up,
    w_down,
    q_gain,
    k_gain,
    attn_gain,
    mlp_gain,
    cotangent,
    segments,
    sources,
    group_weights,
):
    x = lax.axis_index("x")
    own_x, z_high, z_low, head, core, roll = place()

    def own_rows(value):
        return lax.dynamic_slice_in_dim(value, roll, ROWS, 0)

    here = (jnp.arange(TOK, dtype=jnp.int32) + roll) & (TOK - 1)
    own_block = block_of(own_x, z_high, z_low, core)
    q_blocks = jnp.stack([block_of(own_x ^ (a >> 1), z_high ^ (a & 1), z_low, core) for a in range(4)])
    q_pos = (q_blocks[:, None] * TOK + here[None]).reshape(4, 1, TOK)
    seq_segments = lax.dynamic_slice_in_dim(segments, (x >> 1) * SEQ, SEQ)
    by_block = seq_segments.reshape(BLOCKS, TOK)
    q_segments = jnp.stack([lax.dynamic_index_in_dim(by_block, q_blocks[a], 0, False) for a in range(4)])
    q_segments = lax.dynamic_slice_in_dim(jnp.concatenate([q_segments, q_segments], axis=1), roll, TOK, 1)
    q_start = jnp.sum((seq_segments[:, None, None] < q_segments[None]).astype(jnp.int32), axis=0).reshape(4, 1, TOK)

    inverse = 1.0 / theta_base ** (jnp.arange(0, HD, 2, dtype=F32) / HD)
    angles = (own_block * TOK + here).astype(F32)[:, None] * inverse[None, :]
    cosine, sine = jnp.cos(angles), jnp.sin(angles)
    cos_table = jnp.concatenate([cosine, cosine], axis=-1)
    sin_table = jnp.concatenate([-sine, sine], axis=-1)
    gains = jnp.stack([q_gain, k_gain]).reshape(2, 1, 512)

    states_here = rolled_rows(states)
    query_raw = product(states_here, w_query)
    key_raw = product(states_here, w_key)
    squares = jnp.concatenate(
        [jnp.sum(query_raw * query_raw, axis=1)[None], jnp.sum(key_raw * key_raw, axis=1)[None], jnp.zeros((6, TOK), F32)]
    )
    squares = rolled_columns(squares, (TOK - roll) & (TOK - 1))
    chosen = own_rows(sources)[:, None] == jnp.arange(group_weights.shape[0], dtype=jnp.int32)[None, :]
    token_share = jnp.sum(jnp.where(chosen, group_weights[None, :], 0), axis=1).astype(F32) / weight_unit
    token_share = jnp.broadcast_to(token_share[:, None], (ROWS, 128))
    line = Line(roll)
    token_share = line(token_share)
    from_squares = swap(line(squares), "y", FIRST)
    value_low = line(product(states_here, w_value).astype(BF16))
    squares = line(squares + line(from_squares))
    from_squares = swap(squares, "y", SECOND)
    cos_table, sin_table = line(cos_table, sin_table)
    from_squares = line(from_squares)
    mine, to_z, to_x, to_xz, rates = enter(
        query_raw, key_raw, value_low, (squares, from_squares), gains, cos_table, sin_table
    )

    def exchange(to_z, to_x, to_xz):
        return swap(to_z, "z", SECOND), swap(to_x, "x", FIRST), swap_xz(to_xz, FIRST, SECOND)

    from_others = exchange(*line(to_z, to_x, to_xz))
    q_start = line(q_start)
    pieces = [mine, *line(from_others)]
    kv_own = line(jnp.stack([p[1:] for p in pieces], axis=1))
    kv_z = swap(kv_own, "z", FIRST)
    kv_c = swap_core(kv_own)
    q_here = line(jnp.stack([p[0] for p in pieces]))
    kv_c = line(kv_c)
    state = line(attend_first(q_here, (kv_own, kv_c), q_pos, q_start))
    kv_z = line(kv_z)
    kv_zc = line(swap_core(kv_z))
    *mixed, mixed_turned, log_total = line(attend_last(q_here, (kv_z, kv_zc), q_pos, q_start, state))
    mixed = line([mixed[0], *exchange(*mixed[1:])])
    mixed_low, *branch = line(out_product(mixed, w_out))

    attn_gain, mlp_gain = attn_gain.reshape(1, WIDTH), mlp_gain.reshape(1, WIDTH)
    branch = scatter_y(branch)
    states_own, cotangent_own = states_here[:ROWS], own_rows(cotangent)
    states_own, cotangent_own = line(states_own, cotangent_own)
    branch = line(branch)
    hidden, hidden_own, b_norm, b_rate = branch_norm(branch, states_own, attn_gain)
    hidden_pieces = line(gather_y(line(hidden_own)))
    act_low, gate_factor, up_factor = line(act_product(hidden_pieces, w_gate, w_up))
    down = scatter_y(line(rows_product([(act_low, w_down)], turned=False)))

    def shared_left(pair):
        return pair[0], swap_core(pair[1])

    def shared(right):
        return right, swap_core(right)

    act_right = shared(act_low)
    hidden_left = line(columns(False, hidden_pieces))
    down = line(down)
    output_own, grad_down_own, grad_top, local_mlp_gain = top_norm(down, hidden, mlp_gain, cotangent_own, token_share)

    hidden_left, act_right = line(shared_left(hidden_left), act_right)
    grad_down_pieces = gather_y(line(grad_down_own))
    states_left = shared(line(all_columns([states_here], far=(0,))))
    grad_down_pieces, states_left = line(grad_down_pieces, states_left)
    grad_gate_proj, grad_up_proj = line(act_back(grad_down_pieces, w_down, gate_factor, up_factor))
    gate_right, up_right = shared(grad_gate_proj), shared(grad_up_proj)
    down_left = shared_left(line(columns(False, grad_down_pieces)))
    hidden_part = line(rows_product([(grad_gate_proj, w_gate), (grad_up_proj, w_up)]))
    gate_right, up_right, down_left = line(gate_right, up_right, down_left)
    hidden_sum = scatter_y(line(hidden_part))

    wide_grads, mark = plain(
        0, line([(hidden_left, gate_right), (hidden_left, up_right), (down_left, act_right)])
    )
    mark = line(mark)
    wide_grads = lax.psum_scatter(wide_grads, ("x", "z"), scatter_dimension=0, tiled=True)
    hidden_sum = line(hidden_sum)
    grad_hidden, grad_branch_own, wide_gains = hidden_norm(
        hidden_sum, grad_top, b_norm, b_rate, attn_gain, local_mlp_gain, mark
    )

    grad_branch_pieces = line(gather_y(line(grad_branch_own)))
    to = line(mixed_back(grad_branch_pieces, w_out))
    grad_mixed_here = [to[0], *exchange(to[1], to[2], to[3])]

    branch_left = line(all_columns(grad_branch_pieces))
    grad_mixed_here = line(grad_mixed_here)
    branch_left = shared(branch_left)
    dq_part, keep_z, send_z = line(
        attend_back(True, q_here, (kv_z, kv_zc), q_pos, q_start, grad_mixed_here, mixed_turned, log_total)
    )
    branch_left = line(branch_left)
    keep_z = line(merge(keep_z, line(swap_core(send_z))))
    from_z = swap(keep_z, "z", FIRST)
    output = gather_y(line(output_own))
    from_gains = swap(line(wide_gains), "y", FIRST)

    *dq, keep_own, send_c = line(
        attend_back(
            False, q_here, (kv_own, kv_c), q_pos, q_start, grad_mixed_here, mixed_turned, log_total, dq_part
        )
    )
    output, from_z = line(output, from_z)
    came = line(swap_core(line(send_c)))
    pieces = line(merge_own(keep_own, came, from_z, dq))
    pieces = [pieces[0], *exchange(*pieces[1:])]
    wide_gains = line(wide_gains + line(from_gains))
    from_gains = swap(wide_gains, "y", SECOND)
    output = line(unrolled(output))
    pieces = line(pieces)
    wide_gains = line(wide_gains + line(from_gains))
    q_scaled, k_scaled, qk_gain_sums, inner, grad_value_low, mine, send = line(
        leave(query_raw, key_raw, rates, gains, cos_table, sin_table, mixed_low, pieces)
    )
    from_inner = swap(inner, "y", FIRST)
    from_other = swap_core(send)

    riders = jnp.concatenate([wide_gains, qk_gain_sums.reshape(1, 1024)])
    from_core = swap_core(riders)
    inner = line(inner + line(from_inner))
    from_inner = swap(inner, "y", SECOND)
    riders = line(riders + line(from_core))
    first_right = (mine, line(from_other))
    grad_query_raw, grad_key_raw, mine, send = line(
        finish(query_raw, key_raw, q_scaled, k_scaled, rates, (inner, line(from_inner)))
    )
    from_other = swap_core(send)
    pairs = [(grad_query_raw, w_query), (grad_key_raw, w_key), (grad_value_low, w_value)]
    input_sum = scatter_y(line(rows_product(pairs)))

    first_right, riders = line(first_right, riders)
    pieces = spread_first(states_left, branch_left, first_right)
    pieces = list(line(spread_last(states_left, (mine, line(from_other)), riders, pieces)))
    pieces[1], pieces[2] = around(pieces[1], 1, True), around(pieces[2], 2, True)
    input_sum = line(input_sum)
    grad_states_own = line(states_sum(input_sum, grad_hidden))
    pieces[3] = around(line(pieces[3]), 3, True)
    wide_grads = line(wide_grads)
    grad_states = lax.all_gather(line(grad_states_own), "y", axis=0, tiled=True)
    wide_grads = wide_grads.astype(F32)
    wide_grads = line(
        wide_grads[:, :WIDTH], wide_grads[:, WIDTH : 2 * WIDTH], jnp.transpose(wide_grads[:, 2 * WIDTH :])
    )

    pieces = line(add_pieces(line(pieces)))
    pieces = [pieces[0]] + [around(pieces[k], k, False) for k in (1, 2, 3)]
    own, to_other, riders = line(last_sum(line(pieces)))
    other = line(swap_core(to_other)).astype(F32)
    grad_states = line(grad_states)
    with_query, with_key = jnp.where(core == 0, own, other), jnp.where(core == 0, other, own)
    wide_gains = riders[:4].reshape(2, WIDTH)
    qk_gains = riders[4].reshape(2, 512)
    q_gain_last = jnp.where(line.token < TOK, qk_gains[0], 0.0)

    return (
        output,
        grad_states.astype(F32),
        with_query[:, :512],
        with_key[:, :512],
        with_query[:, 512:],
        jnp.transpose(with_key[:, 512:]),
        wide_grads[0],
        wide_grads[1],
        wide_grads[2],
        q_gain_last,
        qk_gains[1],
        wide_gains[0],
        wide_gains[1],
    )


def solution(mesh):
    split = Mesh(mesh.devices.reshape(4, 4, 2, 4), ("x", "z", "c", "y"))
    dp, mp = ("x", "z", "c"), "y"
    placed = (
        P(dp, None),
        P(None, mp),
        P(None, mp),
        P(None, mp),
        P(mp, None),
        P(None, mp),
        P(None, mp),
        P(mp, None),
        P(mp),
        P(mp),
        P(),
        P(),
        P(dp, None),
        P(),
        P(dp),
        P(),
    )
    return jax.shard_map(
        local,
        mesh=split,
        in_specs=placed,
        out_specs=(
            P(dp, None),
            P(dp, None),
            P(dp, mp),
            P(dp, mp),
            P(dp, mp),
            P(mp, dp),
            P(dp, mp),
            P(dp, mp),
            P(mp, dp),
            P(mp),
            P(mp),
            P(),
            P(),
        ),
        check_vma=False,
    )
```

```python
import functools

import jax
import jax.numpy as jnp
from jax import lax
from jax.experimental import pallas as pl
from jax.experimental.pallas import tpu as pltpu
from jax.sharding import Mesh
from jax.sharding import PartitionSpec as P

HD = 128
HEADS = 4
TOK = 256
ROWS = 64
BLOCKS = 16
SEQ = 4096
WIDTH = 2048
epsilon = 1e-06
theta_base = 500000.0
weight_unit = 16.0
far_below = -1e30
score_scale = HD ** (-0.5)
LOG2E = 1.4426950408889634
F32 = jnp.float32
BF16 = jnp.bfloat16

FIRST = (1, 0, 3, 2)
SECOND = (3, 2, 1, 0)
BOTH = (2, 3, 0, 1)
HERE = (0, 1, 2, 3)
PAIRINGS = (HERE, FIRST, SECOND, BOTH)
VMEM_LIMIT = 10 * 1024 * 1024
COST = pl.CostEstimate(flops=1, bytes_accessed=1, transcendentals=0)
LONG = pl.CostEstimate(flops=10**12, bytes_accessed=1, transcendentals=0)


def product(left, right):
    return jnp.dot(left, right, preferred_element_type=F32)


def product_right(left, right):
    return lax.dot_general(left, right, (((1,), (1,)), ((), ())), preferred_element_type=F32)


def product_left(left, right):
    return lax.dot_general(left, right, (((0,), (0,)), ((), ())), preferred_element_type=F32)


def swap(value, axis, pairing):
    return lax.ppermute(value, axis, [(i, pairing[i]) for i in range(4)])


def swap_core(value):
    return lax.ppermute(value, "c", [(0, 1), (1, 0)])


def swap_xz(value, x_pairing, z_pairing):
    pairs = [(i * 4 + j, x_pairing[i] * 4 + z_pairing[j]) for i in range(4) for j in range(4)]
    return lax.ppermute(value, ("x", "z"), pairs)


def shift_y(value, step):
    return lax.ppermute(value, "y", [(i, (i + step) % 4) for i in range(4)])


def scatter_y(pieces):
    return [pieces[0]] + [shift_y(pieces[k], k) for k in (1, 2, 3)]


def gather_y(own):
    return [own] + [shift_y(own, -k) for k in (1, 2, 3)]


def rows_of(value):
    return [value[k * ROWS : (k + 1) * ROWS] for k in range(4)]


def fetching(body, far, *refs):
    held, sems = refs[-1 - len(far) : -1], refs[-1]
    refs = list(refs[: -1 - len(far)])
    copies = [pltpu.make_async_copy(refs[at], held[n], sems.at[n]) for n, at in enumerate(far)]
    for copy in copies:
        copy.start()
    for n, at in enumerate(far):
        copies[n].wait()
        refs[at] = held[n]
    body(*refs)


def hbm(value):
    return pltpu.with_memory_space_constraint(value, pltpu.HBM)


def call(body, outs, operands, scratch=(), limit=VMEM_LIMIT, far=(), cost=COST):
    in_specs = [pl.BlockSpec(memory_space=pltpu.VMEM)] * len(operands)
    scratch = list(scratch)
    if far:
        body = functools.partial(fetching, body, far)
        operands = list(operands)
        for at in far:
            operands[at] = hbm(operands[at])
            in_specs[at] = pl.BlockSpec(memory_space=pltpu.HBM)
            scratch.append(pltpu.VMEM(operands[at].shape, operands[at].dtype))
        scratch.append(pltpu.SemaphoreType.DMA((len(far),)))
    return pl.pallas_call(
        body,
        out_shape=[jax.ShapeDtypeStruct(s, d) for s, d in outs],
        in_specs=in_specs,
        out_specs=[pl.BlockSpec(memory_space=pltpu.VMEM)] * len(outs),
        scratch_shapes=scratch,
        compiler_params=pltpu.CompilerParams(vmem_limit_bytes=limit),
        cost_estimate=cost,
    )(*operands)


def place():
    x, z, core, y = (lax.axis_index(n) for n in ("x", "z", "c", "y"))
    own_x, high, low = x & 1, z >> 1, (z ^ (z >> 1)) & 1
    return own_x, high, low, own_x * 2 + high, core, y * ROWS


def block_of(x_bit, high, low, core):
    return x_bit * 8 + (high * 2 + (low ^ high)) * 2 + core


def key_tile(group, xb, own_x, high, low, core, kv):
    start = (own_x ^ xb) * 2
    k = kv[0, pl.ds(start, 2)].reshape(2 * TOK, HD)
    v = kv[1, pl.ds(start, 2)].reshape(2 * TOK, HD)
    return start, k, v


def tile_blocks(group, xb, high, low, core):
    return [block_of(xb, high ^ n, low ^ (group >> 1), core ^ (group & 1)) for n in (0, 1)]


def allowed(first, second, roll, qpos, qstart):
    row = lax.broadcasted_iota(jnp.int32, (2 * TOK, TOK), 0)
    at = ((row + roll) & (TOK - 1)) + jnp.where(row < TOK, first, second) * TOK
    return (at <= qpos) & (at >= qstart)


def attend_body(groups, q_ref, kva, kvb, qpos_ref, qstart_ref, *refs):
    own_x, high, low, _, core, roll = place()
    last = groups == (2, 3)
    if last:
        m_in, l_in, acc_in, o0, o1, o2, o3, ot_ref, lse_ref, m_ref, l_ref, acc_ref = refs
        m_ref[...] = m_in[...]
        l_ref[...] = l_in[...]
        acc_ref[...] = acc_in[...]
    else:
        m_ref, l_ref, acc_ref = refs
        m_ref[...] = jnp.full_like(m_ref, far_below)
        l_ref[...] = jnp.zeros_like(l_ref)
        acc_ref[...] = jnp.zeros_like(acc_ref)

    @pl.loop(0, 4)
    def _(a):
        block = block_of(own_x ^ (a >> 1), high ^ (a & 1), low, core)
        q = q_ref[a]
        qpos = qpos_ref[a]
        qstart = qstart_ref[a]
        for xb in range(2):
            for group, kv in zip(groups, (kva, kvb)):
                first, second = tile_blocks(group, xb, high, low, core)

                @pl.when(jnp.minimum(first, second) <= block)
                def _(group=group, kv=kv, xb=xb, first=first, second=second):
                    _, k, v = key_tile(group, xb, own_x, high, low, core, kv)
                    s = product_right(k, q)
                    s = jnp.where(allowed(first, second, roll, qpos, qstart), s, far_below)
                    m_old = m_ref[a]
                    m_new = jnp.maximum(m_old, jnp.max(s, axis=0, keepdims=True))
                    p = jnp.exp2((s - m_new) * (score_scale * LOG2E))
                    alpha = jnp.exp2((m_old - m_new) * (score_scale * LOG2E))
                    l_ref[a] = alpha * l_ref[a] + jnp.sum(p, axis=0, keepdims=True)
                    acc_ref[a] = alpha * acc_ref[a] + product_left(v, p.astype(BF16))
                    m_ref[a] = m_new

    if last:
        for a, out in enumerate((o0, o1, o2, o3)):
            mixed = acc_ref[a] / l_ref[a]
            ot_ref[a] = mixed
            out[...] = mixed.T.astype(BF16)
            lse_ref[a] = m_ref[a] * (score_scale * LOG2E) + jnp.log2(l_ref[a])


STATE = [((4, 1, TOK), F32), ((4, 1, TOK), F32), ((4, HD, TOK), F32)]


def attend_first(q, kvs, qpos, qstart):
    return call(functools.partial(attend_body, (0, 1)), STATE, [q, *kvs, qpos, qstart])


def attend_last(q, kvs, qpos, qstart, state):
    outs = [((TOK, HD), BF16)] * 4 + [((4, HD, TOK), F32), ((4, 1, TOK), F32)]
    scratch = [pltpu.VMEM(shape, kind) for shape, kind in STATE]
    return call(functools.partial(attend_body, (2, 3)), outs, [q, *kvs, qpos, qstart, *state], scratch=scratch)


def attend_back_body(groups, q_ref, kva, kvb, qpos_ref, qstart_ref, do0, do1, do2, do3, ot_ref, lse_ref, *refs):
    own_x, high, low, _, core, roll = place()
    last = groups == (0, 1)
    if last:
        dq_in, d0, d1, d2, d3, keep_ref, send_ref, late_ref, acc_ref, dqt_ref, do_ref = refs
        dqt_ref[...] = dq_in[...]
        sends = (send_ref, late_ref)
    else:
        dqt_ref, keep_ref, send_ref, acc_ref, do_ref = refs
        sends = (send_ref,)
        dqt_ref[...] = jnp.zeros_like(dqt_ref)
    acc_ref[...] = jnp.zeros_like(acc_ref)
    for a, ref in enumerate((do0, do1, do2, do3)):
        do_ref[a] = ref[...]

    @pl.loop(0, 4)
    def _(a):
        block = block_of(own_x ^ (a >> 1), high ^ (a & 1), low, core)
        q = q_ref[a]
        do = do_ref[a]
        delta = jnp.sum(do.astype(F32).T * ot_ref[a], axis=0, keepdims=True)
        lse = lse_ref[a]
        qpos = qpos_ref[a]
        qstart = qstart_ref[a]
        for xb in range(2):
            for n, (group, kv) in enumerate(zip(groups, (kva, kvb))):
                first, second = tile_blocks(group, xb, high, low, core)

                @pl.when(jnp.minimum(first, second) <= block)
                def _(n=n, group=group, kv=kv, xb=xb, first=first, second=second):
                    start, k, v = key_tile(group, xb, own_x, high, low, core, kv)
                    s = product_right(k, q)
                    dp = product_right(v, do)
                    keep = allowed(first, second, roll, qpos, qstart)
                    p = jnp.where(keep, jnp.exp2(s * (score_scale * LOG2E) - lse), 0.0)
                    ds = (p * (dp - delta)).astype(BF16)
                    dqt_ref[a] += product_left(k, ds)
                    acc_ref[n, 0, pl.ds(start, 2)] += product(ds, q).reshape(2, TOK, HD)
                    acc_ref[n, 1, pl.ds(start, 2)] += product(p.astype(BF16), do).reshape(2, TOK, HD)

    if last:
        for a, out in enumerate((d0, d1, d2, d3)):
            out[...] = (dqt_ref[a] * score_scale).T.astype(BF16)
    for n, outs in enumerate(((keep_ref,), sends)):
        for at in range(4):
            for j in range(2):
                factor = score_scale if j == 0 else 1.0
                out = outs[at * len(outs) // 4]
                row = ((at * 2 + j) * TOK) % out.shape[0]
                out[pl.ds(row, TOK)] = (acc_ref[n, j, at] * factor).astype(BF16)


PIECES = ((8 * TOK, HD), BF16)


def attend_back(first, q, kvs, qpos, qstart, do, ot, lse, dq=None):
    scratch = [pltpu.VMEM((2, 2, 4, TOK, HD), F32)]
    operands = [q, *kvs, qpos, qstart, *do, ot, lse]
    if first:
        outs = [((4, HD, TOK), F32), PIECES, PIECES]
    else:
        outs = [((TOK, HD), BF16)] * 4 + [PIECES] + [((4 * TOK, HD), BF16)] * 2
        operands.append(dq)
        scratch.append(pltpu.VMEM((4, HD, TOK), F32))
    scratch.append(pltpu.VMEM((4, TOK, HD), BF16))
    body = functools.partial(attend_back_body, (2, 3) if first else (0, 1))
    far = (0, 1, 2, 3, 4, 9, 10) if first else ()
    return call(body, outs, operands, scratch=scratch, limit=16 * 1024 * 1024, far=far)


def merge_body(*refs):
    *ins, out = refs
    total = ins[0][...].astype(F32)
    for ref in ins[1:]:
        total = total + ref[...].astype(F32)
    out[...] = total.astype(BF16)


def merge(*values):
    return call(merge_body, [PIECES], list(values))[0]


def merge_own_body(keep_ref, came0, came1, from_ref, q0, q1, q2, q3, *outs):
    for a, (out, q) in enumerate(zip(outs, (q0, q1, q2, q3))):
        at = pl.ds(a * 2 * TOK, 2 * TOK)
        came = (came0, came1)[a // 2][pl.ds(a % 2 * 2 * TOK, 2 * TOK)]
        out[:TOK] = q[...]
        out[TOK:] = (keep_ref[at].astype(F32) + came.astype(F32) + from_ref[at].astype(F32)).astype(BF16)


def merge_own(keep, came, from_z, dq):
    return call(merge_own_body, [((3 * TOK, HD), BF16)] * 4, [keep, *came, from_z, *dq])


def enter_body(q_ref, k_ref, v_ref, s0, s1, gain_ref, cos_ref, sin_ref, o0, o1, o2, o3, rates_ref):
    _, _, _, head, _, roll = place()
    cos, sin = cos_ref[...], sin_ref[...]
    total = pltpu.roll(s0[...] + s1[...], (TOK - roll) & (TOK - 1), 1)
    rates = lax.rsqrt(total / WIDTH + epsilon)
    rates_ref[...] = rates
    turned_rates = rates.T
    for r, out in enumerate((o0, o1, o2, o3)):
        at = pl.ds(pl.multiple_of((head ^ r) * HD, HD), HD)
        for j, raw_ref in enumerate((q_ref, k_ref)):
            value = raw_ref[:, at] * turned_rates[:, j : j + 1] * gain_ref[j, :, at]
            turned = pltpu.roll(value, HD // 2, 1)
            out[j] = (value * cos + turned * sin).astype(BF16)
        out[2] = v_ref[:, at]


def enter(q_raw, k_raw, v_low, squares, gains, cos, sin):
    outs = [((3, TOK, HD), BF16)] * 4 + [((8, TOK), F32)]
    return call(enter_body, outs, [q_raw, k_raw, v_low, *squares, gains, cos, sin])


def leave_body(
    q_raw, k_raw, rates_ref, gain_ref, cos_ref, sin_ref, mixed_ref, g0, g1, g2, g3,
    q_out, k_out, gains_out, inner_out, low, mine_ref, send_ref,
):
    _, _, _, head, core, roll = place()
    cos, sin = cos_ref[...], sin_ref[...]
    rates = rates_ref[...].T
    inner = [jnp.zeros((TOK, 1), F32), jnp.zeros((TOK, 1), F32)]
    for r, ref in enumerate((g0, g1, g2, g3)):
        at = pl.ds(pl.multiple_of((head ^ r) * HD, HD), HD)
        low[:, at] = ref[2 * TOK :]
        for j, (raw_ref, out) in enumerate(((q_raw, q_out), (k_raw, k_out))):
            grad = ref[j * TOK : (j + 1) * TOK].astype(F32)
            grad = grad * cos - pltpu.roll(grad, HD // 2, 1) * sin
            raw = raw_ref[:, at]
            gains_out[j, :, at] = jnp.sum(grad * raw * rates[:, j : j + 1], axis=0, keepdims=True)
            scaled = grad * gain_ref[j, :, at]
            out[:, at] = scaled
            inner[j] = inner[j] + jnp.sum(raw * scaled, axis=1, keepdims=True)
    lane = lax.broadcasted_iota(jnp.int32, (TOK, 8), 1)
    both = jnp.where(lane == 0, inner[0], jnp.where(lane == 1, inner[1], 0.0))
    inner_out[...] = pltpu.roll(both.T, roll, 1)
    give(core, low, mixed_ref, mine_ref, send_ref)


def give(core, first_ref, second_ref, mine_ref, send_ref):
    @pl.when(core == 0)
    def _():
        mine_ref[...] = first_ref[...]
        send_ref[...] = second_ref[...]

    @pl.when(core == 1)
    def _():
        mine_ref[...] = second_ref[...]
        send_ref[...] = first_ref[...]


def leave(q_raw, k_raw, rates, gains, cos, sin, mixed_low, pieces):
    outs = [((TOK, 512), F32), ((TOK, 512), F32), ((2, 1, 512), F32), ((8, TOK), F32)] + [((TOK, 512), BF16)] * 3
    operands = [q_raw, k_raw, rates, gains, cos, sin, mixed_low, *pieces]
    return call(leave_body, outs, operands, far=(0, 1, 3, 4, 5, 6))


def finish_body(q_raw, k_raw, q_scaled, k_scaled, rates_ref, i0, i1, q_out, k_out, mine_ref, send_ref):
    core, roll = place()[4:]
    rates = rates_ref[...]
    inner = pltpu.roll(i0[...] + i1[...], (TOK - roll) & (TOK - 1), 1)
    factor = (rates * rates * rates * inner / WIDTH).T
    rates = rates.T
    for j, raw, scaled, out in ((0, q_raw, q_scaled, q_out), (1, k_raw, k_scaled, k_out)):
        out[...] = (rates[:, j : j + 1] * scaled[...] - raw[...] * factor[:, j : j + 1]).astype(BF16)
    give(core, q_out, k_out, mine_ref, send_ref)


def finish(q_raw, k_raw, q_scaled, k_scaled, rates, inner):
    outs = [((TOK, 512), BF16)] * 4
    return call(finish_body, outs, [q_raw, k_raw, q_scaled, k_scaled, rates, *inner], far=(0, 1))


def mean_row(value):
    return jnp.sum(value, axis=1, keepdims=True) / WIDTH


def total_of(refs):
    return (refs[0][...].astype(F32) + refs[1][...].astype(F32)) + (refs[2][...].astype(F32) + refs[3][...].astype(F32))


def branch_body(p0, p1, p2, p3, states_ref, gain_ref, hidden_ref, low_ref, norm_ref, rate_ref):
    branch = total_of((p0, p1, p2, p3))
    rate = lax.rsqrt(mean_row(branch * branch) + epsilon)
    norm = branch * rate
    hidden = states_ref[...].astype(F32) + gain_ref[...] * norm
    hidden_ref[...] = hidden
    low_ref[...] = hidden.astype(BF16)
    norm_ref[...] = norm
    rate_ref[...] = rate


def branch_norm(pieces, states, gain):
    wide = (ROWS, WIDTH)
    outs = [(wide, F32), (wide, BF16), (wide, F32), ((ROWS, 1), F32)]
    return call(branch_body, outs, [*pieces, states, gain], far=(4, 5))


def top_body(p0, p1, p2, p3, hidden_ref, gain_ref, cotangent_ref, share_ref, out_ref, low_ref, top_ref, sum_ref):
    down = total_of((p0, p1, p2, p3))
    rate = lax.rsqrt(mean_row(down * down) + epsilon)
    norm = down * rate
    gain = gain_ref[...]
    out_ref[...] = (hidden_ref[...] + gain * norm).astype(BF16)
    top = cotangent_ref[...].astype(F32) * share_ref[:, :1]
    top_ref[...] = top
    sum_ref[...] = jnp.sum(top * norm, axis=0, keepdims=True)
    scaled = gain * top
    low_ref[...] = (rate * (scaled - norm * mean_row(scaled * norm))).astype(BF16)


def top_norm(pieces, hidden, gain, cotangent, share):
    wide = (ROWS, WIDTH)
    outs = [(wide, BF16), (wide, BF16), (wide, F32), ((1, WIDTH), F32)]
    return call(top_body, outs, [*pieces, hidden, gain, cotangent, share], far=(5, 6, 7))


def split_rows(value):
    high = value.astype(BF16).astype(F32)
    filler = jnp.zeros((16 - 2 * value.shape[0], value.shape[1]), F32)
    return jnp.concatenate([high, value - high, filler], axis=0).astype(BF16)


def joined_rows(value, count):
    return value[:count].astype(F32) + value[count : 2 * count].astype(F32)


def hidden_body(p0, p1, p2, p3, top_ref, norm_ref, rate_ref, gain_ref, mlp_ref, mark_ref, grad_ref, low_ref, sum_ref):
    grad = top_ref[...] + total_of((p0, p1, p2, p3))
    grad_ref[...] = grad
    norm = norm_ref[...]
    scaled = gain_ref[...] * grad
    low_ref[...] = (rate_ref[...] * (scaled - norm * mean_row(scaled * norm))).astype(BF16)
    sums = (jnp.sum(grad * norm, axis=0, keepdims=True), mlp_ref[...])
    for n in range(4):
        sum_ref[n : n + 1] = sums[n // 2][:, (n % 2) * 1024 : (n % 2 + 1) * 1024]


def hidden_norm(pieces, top, norm, rate, gain, mlp_gain_sum, mark):
    outs = [((ROWS, WIDTH), F32), ((ROWS, WIDTH), BF16), ((4, 1024), F32)]
    operands = [*pieces, top, norm, rate, gain, mlp_gain_sum, mark]
    return call(hidden_body, outs, operands, far=(7,), cost=LONG)


TILE = 512


def prefetch_body(count, *refs):
    weights, outs, sems = refs[:count], refs[count:-1], refs[-1]
    copies = []
    for n, (weight, out) in enumerate(zip(weights, outs)):
        rows = weight.shape[0] // 4
        for t in range(4):
            at = pl.ds(t * rows, rows)
            copies.append(pltpu.make_async_copy(weight.at[at], out.at[at], sems.at[n, t]))
    for copy in copies:
        copy.start()
    for copy in copies:
        copy.wait()


def prefetch(*weights):
    return pl.pallas_call(
        functools.partial(prefetch_body, len(weights)),
        out_shape=[jax.ShapeDtypeStruct(w.shape, w.dtype) for w in weights],
        in_specs=[pl.BlockSpec(memory_space=pltpu.HBM)] * len(weights),
        out_specs=[pl.BlockSpec(memory_space=pltpu.VMEM)] * len(weights),
        scratch_shapes=[pltpu.SemaphoreType.DMA((len(weights), 4))],
        compiler_params=pltpu.CompilerParams(vmem_limit_bytes=VMEM_LIMIT),
        cost_estimate=COST,
    )(*[hbm(w) for w in weights])


def rows_body(count, turned, *refs):
    lefts, weights, outs = refs[:count], refs[count : 2 * count], refs[2 * count :]
    for t in range(WIDTH // TILE):
        at = pl.ds(t * TILE, TILE)
        total = None
        for n in range(count):
            if turned:
                now = product_right(lefts[n][...], weights[n][at])
            else:
                now = product(lefts[n][...], weights[n][:, at])
            total = now if total is None else total + now
        for k, out in enumerate(outs):
            out[:, at] = total[k * ROWS : (k + 1) * ROWS].astype(BF16)


def rows_product(pairs, turned=True):
    body = functools.partial(rows_body, len(pairs), turned)
    operands = [left for left, _ in pairs] + [right for _, right in pairs]
    return call(body, [((ROWS, WIDTH), BF16)] * 4, operands)


def rolled_rows_body(x_ref, out_ref, sems):
    y = lax.axis_index("y")
    copies = [
        pltpu.make_async_copy(x_ref.at[pl.ds(((k + y) & 3) * ROWS, ROWS)], out_ref.at[pl.ds(k * ROWS, ROWS)], sems.at[k])
        for k in range(4)
    ]
    for copy in copies:
        copy.start()
    for copy in copies:
        copy.wait()


def rolled_rows(value):
    return pl.pallas_call(
        rolled_rows_body,
        out_shape=jax.ShapeDtypeStruct(value.shape, value.dtype),
        in_specs=[pl.BlockSpec(memory_space=pltpu.HBM)],
        out_specs=pl.BlockSpec(memory_space=pltpu.VMEM),
        scratch_shapes=[pltpu.SemaphoreType.DMA((4,))],
        compiler_params=pltpu.CompilerParams(vmem_limit_bytes=VMEM_LIMIT),
        cost_estimate=COST,
    )(hbm(value))


def states_body(p0, p1, p2, p3, grad_ref, out_ref):
    out_ref[...] = (total_of((p0, p1, p2, p3)) + grad_ref[...]).astype(BF16)


def states_sum(pieces, grad):
    return call(states_body, [((ROWS, WIDTH), BF16)], [*pieces, grad], far=(4,))[0]


def unrolled_body(p0, p1, p2, p3, out_ref):
    y = lax.axis_index("y")
    for k, ref in enumerate((p0, p1, p2, p3)):
        at = pl.multiple_of(((k + y) & 3) * ROWS, ROWS)
        out_ref[pl.ds(at, ROWS)] = ref[...].astype(out_ref.dtype)


def unrolled(pieces, kind=BF16):
    return call(unrolled_body, [((TOK, WIDTH), kind)], list(pieces))[0]


def act_body(h0, h1, h2, h3, gate_w, up_w, act_ref, gate_factor_ref, up_factor_ref):
    rows = jnp.concatenate([h0[...], h1[...], h2[...], h3[...]], axis=0)
    for t in range(WIDTH // TILE):
        at = pl.ds(t * TILE, TILE)
        gate = product(rows, gate_w[:, at])
        up = product(rows, up_w[:, at])
        sigmoid = jax.nn.sigmoid(gate)
        silu = gate * sigmoid
        act_ref[:, at] = (silu * up).astype(BF16)
        gate_factor_ref[:, at] = (up * (sigmoid + silu * (1.0 - sigmoid))).astype(BF16)
        up_factor_ref[:, at] = silu.astype(BF16)


def act_product(pieces, w_gate, w_up):
    return call(act_body, [((TOK, WIDTH), BF16)] * 3, [*pieces, w_gate, w_up])


def out_body(m0, m1, m2, m3, out_w, to_ref, o0, o1, o2, o3, held, low_ref, sems):
    copy = pltpu.make_async_copy(out_w, held, sems.at[0])
    copy.start()
    head = place()[3]
    for r, ref in enumerate((m0, m1, m2, m3)):
        low_ref[:, pl.ds(pl.multiple_of((head ^ r) * HD, HD), HD)] = ref[...]
    keep = pltpu.make_async_copy(low_ref, to_ref, sems.at[1])
    keep.start()
    copy.wait()
    branch = product(low_ref[...], held[...])
    for k, out in enumerate((o0, o1, o2, o3)):
        out[...] = branch[k * ROWS : (k + 1) * ROWS].astype(BF16)
    keep.wait()


def out_product(mixed, w_out):
    return pl.pallas_call(
        out_body,
        out_shape=[pltpu.HBM((TOK, 512), BF16)] + [jax.ShapeDtypeStruct((ROWS, WIDTH), BF16)] * 4,
        in_specs=[pl.BlockSpec(memory_space=pltpu.VMEM)] * 4 + [pl.BlockSpec(memory_space=pltpu.HBM)],
        out_specs=[pl.BlockSpec(memory_space=pltpu.HBM)] + [pl.BlockSpec(memory_space=pltpu.VMEM)] * 4,
        scratch_shapes=[pltpu.VMEM(w_out.shape, BF16), pltpu.VMEM((TOK, 512), BF16), pltpu.SemaphoreType.DMA((2,))],
        compiler_params=pltpu.CompilerParams(vmem_limit_bytes=VMEM_LIMIT),
        cost_estimate=COST,
    )(*mixed, hbm(w_out))


def mixed_back_body(g0, g1, g2, g3, out_w, o0, o1, o2, o3, held, sem):
    copy = pltpu.make_async_copy(out_w, held, sem)
    copy.start()
    head = place()[3]
    rows = jnp.concatenate([g0[...], g1[...], g2[...], g3[...]], axis=0)
    copy.wait()
    for r, out in enumerate((o0, o1, o2, o3)):
        at = pl.ds(pl.multiple_of((head ^ r) * HD, HD), HD)
        out[...] = product_right(rows, held[at]).astype(BF16)


def mixed_back(pieces, w_out):
    return pl.pallas_call(
        mixed_back_body,
        out_shape=[jax.ShapeDtypeStruct((TOK, HD), BF16)] * 4,
        in_specs=[pl.BlockSpec(memory_space=pltpu.VMEM)] * 4 + [pl.BlockSpec(memory_space=pltpu.HBM)],
        out_specs=[pl.BlockSpec(memory_space=pltpu.VMEM)] * 4,
        scratch_shapes=[pltpu.VMEM(w_out.shape, BF16), pltpu.SemaphoreType.DMA],
        compiler_params=pltpu.CompilerParams(vmem_limit_bytes=VMEM_LIMIT),
        cost_estimate=COST,
    )(*pieces, hbm(w_out))


def act_back_body(g0, g1, g2, g3, gate_factor_ref, up_factor_ref, down_w, gate_ref, up_ref):
    rows = jnp.concatenate([g0[...], g1[...], g2[...], g3[...]], axis=0)
    for t in range(WIDTH // TILE):
        at = pl.ds(t * TILE, TILE)
        grad = product_right(rows, down_w[at])
        gate_ref[:, at] = (grad * gate_factor_ref[:, at].astype(F32)).astype(BF16)
        up_ref[:, at] = (grad * up_factor_ref[:, at].astype(F32)).astype(BF16)


def act_back(pieces, w_down, gate_factor, up_factor):
    return call(act_back_body, [((TOK, WIDTH), BF16)] * 2, [*pieces, gate_factor, up_factor, w_down])


def columns_body(relative, *refs):
    *ins, own_ref, other_ref = refs
    x, z, core = (lax.axis_index(n) for n in ("x", "z", "c"))
    xs, zs = [x, x ^ 1, 3 - x, 3 - (x ^ 1)], [z, z ^ 1, 3 - z, 3 - (z ^ 1)]
    for k in range(BLOCKS):
        block = xs[k // 4] * 4 + zs[k % 4] if relative else k
        at = pl.ds(pl.multiple_of(block * 128, 128), 128)
        rows = jnp.concatenate([ref[:, at].astype(F32) for ref in ins], axis=0)
        turned = rows.T
        low, high = turned[:ROWS], turned[ROWS:]
        to = pl.ds(k * ROWS, ROWS)
        own_ref[to] = jnp.where(core == 0, low, high).astype(BF16)
        other_ref[to] = jnp.where(core == 0, high, low).astype(BF16)


def columns(relative, values, far=()):
    return call(functools.partial(columns_body, relative), [((BLOCKS * ROWS, TOK), BF16)] * 2, list(values), far=far)


def all_columns_body(*refs):
    *ins, out_ref = refs
    x, z = lax.axis_index("x"), lax.axis_index("z")
    xs, zs = [x, x ^ 1, 3 - x, 3 - (x ^ 1)], [z, z ^ 1, 3 - z, 3 - (z ^ 1)]
    for k in range(BLOCKS):
        at = pl.ds(pl.multiple_of((xs[k // 4] * 4 + zs[k % 4]) * 128, 128), 128)
        rows = jnp.concatenate([ref[:, at].astype(F32) for ref in ins], axis=0)
        out_ref[pl.ds(k * 128, 128)] = rows.T.astype(BF16)


def all_columns(values, far=()):
    return call(all_columns_body, [((WIDTH, TOK), BF16)], list(values), far=far)[0]


def spread_part(left, right, outs):
    core = lax.axis_index("c")
    for p, out in enumerate(outs):
        blocks = [jnp.where(core == 0, p * 4 + i, i * 4 + p) * 128 for i in range(4)]
        rows = [pl.ds(pl.multiple_of(block, 128), 128) for block in blocks]
        now = jnp.concatenate([jnp.concatenate([ref[r] for ref in left], axis=1) for r in rows], axis=0)
        out[:512, :512] = product(now, right).astype(BF16)


def spread_first_body(s0, s1, g0, g1, b0, b1, *outs):
    core = lax.axis_index("c")
    right = jnp.concatenate([b0[...], b1[...]], axis=0)

    @pl.when(core == 0)
    def _():
        spread_part((s0, s1), right, outs)

    @pl.when(core == 1)
    def _():
        spread_part((g0, g1), right, outs)


def spread_last_body(s0, s1, b0, b1, riders_ref, *refs):
    ins, outs = refs[:4], refs[4:]
    riders = split_rows(riders_ref[...])
    for ref, out in zip(ins, outs):
        out[:512, 512:] = ref[...]
        out[512:] = riders
    spread_part((s0, s1), jnp.concatenate([b0[...], b1[...]], axis=0), outs)


def spread_first(states_left, branch_left, right):
    return call(spread_first_body, [((512, 512), BF16)] * 4, [*states_left, *branch_left, *right])


def spread_last(states_left, right, riders, pieces):
    return call(spread_last_body, [((528, 1024), BF16)] * 4, [*states_left, *right, riders, *pieces])


def add_body(*refs):
    ins, outs = refs[:4], refs[4:]
    total = total_of([ref.at[pl.ds(0, 512)] for ref in ins])
    riders = [joined_rows(ref[512:], 5) for ref in ins]
    riders = split_rows((riders[0] + riders[1]) + (riders[2] + riders[3]))
    for n, out in enumerate(outs):
        out[:128] = total[n * 128 : (n + 1) * 128].astype(BF16)
        out[128:] = riders


def add_pieces(pieces):
    return call(add_body, [((144, 1024), BF16)] * 4, list(pieces))


def around(value, k, first):
    pairs = []
    for x in range(4):
        for z in range(4):
            for core in range(2):
                to = (PAIRINGS[k][x], z) if (core == 0) == first else (x, PAIRINGS[k][z])
                pairs.append(((x * 4 + z) * 2 + core, (to[0] * 4 + to[1]) * 2 + core))
    return lax.ppermute(value, ("x", "z", "c"), pairs)


def last_body(p0, p1, p2, p3, mine_ref, send_ref, attn_ref, mlp_ref, q_ref, k_ref):
    core = lax.axis_index("c")
    total = total_of((p0, p1, p2, p3))
    low, high = total[:ROWS], total[ROWS:128]
    mine_ref[...] = jnp.where(core == 0, low, high)
    send_ref[...] = jnp.where(core == 0, high, low).astype(BF16)
    riders = total[128 : 128 + 5] + total[128 + 5 : 128 + 10]
    for n, out in enumerate((attn_ref, mlp_ref)):
        out[:, :1024] = riders[2 * n : 2 * n + 1]
        out[:, 1024:] = riders[2 * n + 1 : 2 * n + 2]
    q_ref[...] = riders[4:5, :512]
    k_ref[...] = riders[4:5, 512:]


def last_sum(pieces):
    outs = [((ROWS, 1024), F32), ((ROWS, 1024), BF16)] + [((1, WIDTH), F32)] * 2 + [((1, 512), F32)] * 2
    return call(last_body, outs, list(pieces))


def apart_body(own_ref, other_ref, q_ref, k_ref, v_ref, out_ref):
    core = lax.axis_index("c")
    own, other = own_ref[...], other_ref[...].astype(F32)
    with_query, with_key = jnp.where(core == 0, own, other), jnp.where(core == 0, other, own)
    q_ref[...] = with_query[:, :512]
    v_ref[...] = with_query[:, 512:]
    k_ref[...] = with_key[:, :512]
    out_ref[...] = with_key[:, 512:]


def apart(own, other):
    return call(apart_body, [((ROWS, 512), F32)] * 4, [own, other])


def sum_four(pieces):
    return (pieces[0].astype(F32) + pieces[1].astype(F32)) + (pieces[2].astype(F32) + pieces[3].astype(F32))


SLOTS = 4


def plain_body(base, count, *refs):
    width = 512
    each = WIDTH // width
    inputs, (out_ref, mark_ref, held, sems) = refs[: 4 * count], refs[-4:]
    copies = []
    for n in range(count * each):
        a0, a1, b0, b1 = inputs[4 * (n // each) : 4 * (n // each) + 4]
        at = pl.ds((n % each) * width, width)
        slot = n % SLOTS
        if n >= SLOTS:
            copies[n - SLOTS].wait()
        left = jnp.concatenate([a0[...], a1[...]], axis=1)
        held[slot] = product(left, jnp.concatenate([b0[:, at], b1[:, at]], axis=0)).astype(BF16)
        to = out_ref.at[:, pl.ds((base * each + n) * width, width)]
        copies.append(pltpu.make_async_copy(held.at[slot], to, sems.at[slot]))
        copies[n].start()
    for copy in copies[-SLOTS:]:
        copy.wait()
    mark_ref[...] = jnp.zeros((8, 128), F32)


def plain(base, pairs, into=None):
    operands = [value for left, right in pairs for value in (*left, *right)]
    in_specs = [pl.BlockSpec(memory_space=pltpu.VMEM)] * len(operands)
    aliases = {}
    if into is not None:
        aliases = {len(operands): 0}
        in_specs.append(pl.BlockSpec(memory_space=pltpu.HBM))
        operands.append(hbm(into))
    return pl.pallas_call(
        functools.partial(plain_body, base, len(pairs)),
        out_shape=[pltpu.HBM((BLOCKS * ROWS, 3 * WIDTH), BF16), jax.ShapeDtypeStruct((8, 128), F32)],
        in_specs=in_specs,
        out_specs=[pl.BlockSpec(memory_space=pltpu.HBM), pl.BlockSpec(memory_space=pltpu.VMEM)],
        scratch_shapes=[pltpu.VMEM((SLOTS, BLOCKS * ROWS, 512), BF16), pltpu.SemaphoreType.DMA((SLOTS,))],
        input_output_aliases=aliases,
        compiler_params=pltpu.CompilerParams(vmem_limit_bytes=VMEM_LIMIT),
        cost_estimate=COST,
    )(*operands)


def rolled_columns(value, shift):
    return lax.dynamic_slice_in_dim(jnp.concatenate([value, value], axis=1), shift, TOK, 1)


class Line:
    def __init__(self, token):
        self.token = token

    def __call__(self, *values):
        values, self.token = lax.optimization_barrier((values, self.token))
        return values if len(values) > 1 else values[0]


def local(
    states,
    w_query,
    w_key,
    w_value,
    w_out,
    w_gate,
    w_up,
    w_down,
    q_gain,
    k_gain,
    attn_gain,
    mlp_gain,
    cotangent,
    segments,
    sources,
    group_weights,
):
    x = lax.axis_index("x")
    own_x, z_high, z_low, head, core, roll = place()

    def own_rows(value):
        return lax.dynamic_slice_in_dim(value, roll, ROWS, 0)

    here = (jnp.arange(TOK, dtype=jnp.int32) + roll) & (TOK - 1)
    own_block = block_of(own_x, z_high, z_low, core)
    q_blocks = jnp.stack([block_of(own_x ^ (a >> 1), z_high ^ (a & 1), z_low, core) for a in range(4)])
    q_pos = (q_blocks[:, None] * TOK + here[None]).reshape(4, 1, TOK)
    seq_segments = lax.dynamic_slice_in_dim(segments, (x >> 1) * SEQ, SEQ)
    by_block = seq_segments.reshape(BLOCKS, TOK)
    q_segments = jnp.stack([lax.dynamic_index_in_dim(by_block, q_blocks[a], 0, False) for a in range(4)])
    q_segments = lax.dynamic_slice_in_dim(jnp.concatenate([q_segments, q_segments], axis=1), roll, TOK, 1)
    q_start = jnp.sum((seq_segments[:, None, None] < q_segments[None]).astype(jnp.int32), axis=0).reshape(4, 1, TOK)

    inverse = 1.0 / theta_base ** (jnp.arange(0, HD, 2, dtype=F32) / HD)
    angles = (own_block * TOK + here).astype(F32)[:, None] * inverse[None, :]
    cosine, sine = jnp.cos(angles), jnp.sin(angles)
    cos_table = jnp.concatenate([cosine, cosine], axis=-1)
    sin_table = jnp.concatenate([-sine, sine], axis=-1)
    gains = jnp.stack([q_gain, k_gain]).reshape(2, 1, 512)

    states_here = rolled_rows(states)
    query_raw = product(states_here, w_query)
    key_raw = product(states_here, w_key)
    squares = jnp.concatenate(
        [jnp.sum(query_raw * query_raw, axis=1)[None], jnp.sum(key_raw * key_raw, axis=1)[None], jnp.zeros((6, TOK), F32)]
    )
    squares = rolled_columns(squares, (TOK - roll) & (TOK - 1))
    chosen = own_rows(sources)[:, None] == jnp.arange(group_weights.shape[0], dtype=jnp.int32)[None, :]
    token_share = jnp.sum(jnp.where(chosen, group_weights[None, :], 0), axis=1).astype(F32) / weight_unit
    token_share = jnp.broadcast_to(token_share[:, None], (ROWS, 128))
    line = Line(roll)
    from_squares = swap(line(squares), "y", FIRST)
    value_low = line(product(states_here, w_value).astype(BF16))
    squares = line(squares + line(from_squares))
    from_squares = swap(squares, "y", SECOND)
    cos_table, sin_table, token_share = line(cos_table, sin_table, token_share)
    from_squares = line(from_squares)
    mine, to_z, to_x, to_xz, rates = enter(
        query_raw, key_raw, value_low, (squares, from_squares), gains, cos_table, sin_table
    )

    def exchange(to_z, to_x, to_xz):
        return swap(to_z, "z", SECOND), swap(to_x, "x", FIRST), swap_xz(to_xz, FIRST, SECOND)

    from_others = exchange(*line(to_z, to_x, to_xz))
    q_start = line(q_start)
    pieces = [mine, *line(from_others)]
    kv_own = line(jnp.stack([p[1:] for p in pieces], axis=1))
    kv_z = swap(kv_own, "z", FIRST)
    kv_c = swap_core(kv_own)
    q_here = line(jnp.stack([p[0] for p in pieces]))
    kv_c = line(kv_c)
    state = line(attend_first(q_here, (kv_own, kv_c), q_pos, q_start))
    kv_z = line(kv_z)
    kv_zc = line(swap_core(kv_z))
    *mixed, mixed_turned, log_total = line(attend_last(q_here, (kv_z, kv_zc), q_pos, q_start, state))
    mixed = line([mixed[0], *exchange(*mixed[1:])])
    mixed_low, *branch = line(out_product(mixed, w_out))

    attn_gain, mlp_gain = attn_gain.reshape(1, WIDTH), mlp_gain.reshape(1, WIDTH)
    branch = scatter_y(branch)
    states_own, cotangent_own = states_here[:ROWS], own_rows(cotangent)
    states_own, cotangent_own = line(states_own, cotangent_own)
    w_gate, w_up = line(prefetch(w_gate, w_up))
    branch = line(branch)
    hidden, hidden_own, b_norm, b_rate = branch_norm(branch, states_own, attn_gain)
    hidden_pieces = gather_y(line(hidden_own))
    w_down = line(prefetch(w_down)[0])
    hidden_pieces = line(hidden_pieces)
    act_low, gate_factor, up_factor = line(act_product(hidden_pieces, w_gate, w_up))
    down = scatter_y(line(rows_product([(act_low, w_down)], turned=False)))

    def shared_left(pair):
        return pair[0], swap_core(pair[1])

    def shared(right):
        return right, swap_core(right)

    act_right = shared(act_low)
    hidden_left = line(columns(False, hidden_pieces))
    down = line(down)
    output_own, grad_down_own, grad_top, local_mlp_gain = top_norm(down, hidden, mlp_gain, cotangent_own, token_share)

    hidden_left, act_right = line(shared_left(hidden_left), act_right)
    grad_down_pieces = gather_y(line(grad_down_own))
    states_left = shared(line(all_columns([states_here], far=(0,))))
    grad_down_pieces, states_left = line(grad_down_pieces, states_left)
    grad_gate_proj, grad_up_proj = line(act_back(grad_down_pieces, w_down, gate_factor, up_factor))
    gate_right, up_right = shared(grad_gate_proj), shared(grad_up_proj)
    down_left = shared_left(line(columns(False, grad_down_pieces)))
    hidden_part = line(rows_product([(grad_gate_proj, w_gate), (grad_up_proj, w_up)]))
    gate_right, up_right, down_left = line(gate_right, up_right, down_left)
    hidden_sum = scatter_y(line(hidden_part))

    wide_grads, mark = plain(
        0, line([(hidden_left, gate_right), (hidden_left, up_right), (down_left, act_right)])
    )
    mark = line(mark)
    wide_grads = lax.psum_scatter(wide_grads, ("x", "z"), scatter_dimension=0, tiled=True)
    hidden_sum = line(hidden_sum)
    grad_hidden, grad_branch_own, wide_gains = hidden_norm(
        hidden_sum, grad_top, b_norm, b_rate, attn_gain, local_mlp_gain, mark
    )

    grad_branch_pieces = line(gather_y(line(grad_branch_own)))
    to = line(mixed_back(grad_branch_pieces, w_out))
    grad_mixed_here = [to[0], *exchange(to[1], to[2], to[3])]

    branch_left = line(all_columns(grad_branch_pieces))
    grad_mixed_here = line(grad_mixed_here)
    branch_left = shared(branch_left)
    dq_part, keep_z, send_z = line(
        attend_back(True, q_here, (kv_z, kv_zc), q_pos, q_start, grad_mixed_here, mixed_turned, log_total)
    )
    branch_left = line(branch_left)
    keep_z = line(merge(keep_z, line(swap_core(send_z))))
    from_z = swap(keep_z, "z", FIRST)
    output = gather_y(line(output_own))

    *dq, keep_own, send_c, send_late = line(
        attend_back(
            False, q_here, (kv_own, kv_c), q_pos, q_start, grad_mixed_here, mixed_turned, log_total, dq_part
        )
    )
    output, from_z = line(output, from_z)
    came = line(swap_core(line(send_c)), swap_core(line(send_late)))
    pieces = line(merge_own(keep_own, came, from_z, dq))
    pieces = [pieces[0], *exchange(*pieces[1:])]
    from_gains = swap(line(wide_gains), "y", FIRST)
    wide_gains = line(wide_gains + line(from_gains))
    from_gains = swap(wide_gains, "y", SECOND)
    output = line(unrolled(output))
    pieces = line(pieces)
    wide_gains = line(wide_gains + line(from_gains))
    q_scaled, k_scaled, qk_gain_sums, inner, grad_value_low, mine, send = line(
        leave(query_raw, key_raw, rates, gains, cos_table, sin_table, mixed_low, pieces)
    )
    from_inner = swap(inner, "y", FIRST)
    from_other = swap_core(send)

    riders = jnp.concatenate([wide_gains, qk_gain_sums.reshape(1, 1024)])
    from_core = swap_core(riders)
    inner = line(inner + line(from_inner))
    from_inner = swap(inner, "y", SECOND)
    riders = line(riders + line(from_core))
    pieces = line(spread_first(states_left, branch_left, (mine, line(from_other))))
    grad_query_raw, grad_key_raw, mine, send = line(
        finish(query_raw, key_raw, q_scaled, k_scaled, rates, (inner, line(from_inner)))
    )
    from_other = swap_core(send)
    pairs = [(grad_query_raw, w_query), (grad_key_raw, w_key), (grad_value_low, w_value)]
    input_part = line(rows_product(pairs))
    input_sum = [input_part[0], shift_y(input_part[1], 1), shift_y(input_part[2], 2)]

    pieces = list(line(spread_last(states_left, (mine, line(from_other)), riders, pieces)))
    pieces = [pieces[0]] + [around(pieces[k], k, True) for k in (1, 2, 3)]
    pieces[1] = line(pieces[1])
    input_sum.append(shift_y(line(input_part[3]), 3))
    input_sum = line(input_sum)
    grad_states = gather_y(line(states_sum(input_sum, grad_hidden)))

    pieces = line(add_pieces(line(pieces)))
    pieces = [pieces[0]] + [around(pieces[k], k, False) for k in (1, 2, 3)]
    wide_grads = line(wide_grads).astype(F32)
    wide_grads = line(
        wide_grads[:, :WIDTH], wide_grads[:, WIDTH : 2 * WIDTH], jnp.transpose(wide_grads[:, 2 * WIDTH :])
    )
    grad_states = line(unrolled(line(grad_states), F32))
    own, to_other, *gain_grads = line(last_sum(line(pieces)))
    query_grad, key_grad, value_grad, out_grad = apart(own, line(swap_core(to_other)))
    q_gain_grad = jnp.where(line.token < TOK, gain_grads[2].reshape(512), 0.0)

    return (
        output,
        grad_states,
        query_grad,
        key_grad,
        value_grad,
        jnp.transpose(out_grad),
        wide_grads[0],
        wide_grads[1],
        wide_grads[2],
        q_gain_grad,
        gain_grads[3].reshape(512),
        gain_grads[0].reshape(WIDTH),
        gain_grads[1].reshape(WIDTH),
    )


def solution(mesh):
    split = Mesh(mesh.devices.reshape(4, 4, 2, 4), ("x", "z", "c", "y"))
    dp, mp = ("x", "z", "c"), "y"
    placed = (
        P(dp, None),
        P(None, mp),
        P(None, mp),
        P(None, mp),
        P(mp, None),
        P(None, mp),
        P(None, mp),
        P(mp, None),
        P(mp),
        P(mp),
        P(),
        P(),
        P(dp, None),
        P(),
        P(dp),
        P(),
    )
    return jax.shard_map(
        local,
        mesh=split,
        in_specs=placed,
        out_specs=(
            P(dp, None),
            P(dp, None),
            P(dp, mp),
            P(dp, mp),
            P(dp, mp),
            P(mp, dp),
            P(dp, mp),
            P(dp, mp),
            P(mp, dp),
            P(mp),
            P(mp),
            P(),
            P(),
        ),
        check_vma=False,
    )
```

```python
import functools

import jax
import jax.numpy as jnp
from jax import lax
from jax.experimental import pallas as pl
from jax.experimental.pallas import tpu as pltpu
from jax.sharding import Mesh
from jax.sharding import PartitionSpec as P

HD = 128
HEADS = 4
TOK = 256
ROWS = 64
BLOCKS = 16
SEQ = 4096
WIDTH = 2048
epsilon = 1e-06
theta_base = 500000.0
weight_unit = 16.0
far_below = -1e30
score_scale = HD ** (-0.5)
LOG2E = 1.4426950408889634
F32 = jnp.float32
BF16 = jnp.bfloat16

FIRST = (1, 0, 3, 2)
SECOND = (3, 2, 1, 0)
BOTH = (2, 3, 0, 1)
HERE = (0, 1, 2, 3)
PAIRINGS = (HERE, FIRST, SECOND, BOTH)
VMEM_LIMIT = 10 * 1024 * 1024
COST = pl.CostEstimate(flops=1, bytes_accessed=1, transcendentals=0)
LONG = pl.CostEstimate(flops=10**12, bytes_accessed=1, transcendentals=0)


def product(left, right):
    return jnp.dot(left, right, preferred_element_type=F32)


def product_right(left, right):
    return lax.dot_general(left, right, (((1,), (1,)), ((), ())), preferred_element_type=F32)


def product_left(left, right):
    return lax.dot_general(left, right, (((0,), (0,)), ((), ())), preferred_element_type=F32)


def swap(value, axis, pairing):
    return lax.ppermute(value, axis, [(i, pairing[i]) for i in range(4)])


def swap_core(value):
    return lax.ppermute(value, "c", [(0, 1), (1, 0)])


def swap_xz(value, x_pairing, z_pairing):
    pairs = [(i * 4 + j, x_pairing[i] * 4 + z_pairing[j]) for i in range(4) for j in range(4)]
    return lax.ppermute(value, ("x", "z"), pairs)


def shift_y(value, step):
    return lax.ppermute(value, "y", [(i, (i + step) % 4) for i in range(4)])


def scatter_y(pieces):
    return [pieces[0]] + [shift_y(pieces[k], k) for k in (2, 1, 3)]


def gather_y(own):
    return [own] + [shift_y(own, -k) for k in (1, 3, 2)]


def in_order(pieces):
    return [pieces[k] for k in (0, 1, 3, 2)]


def rows_of(value):
    return [value[k * ROWS : (k + 1) * ROWS] for k in range(4)]


def fetching(body, far, *refs):
    held, sems = refs[-1 - len(far) : -1], refs[-1]
    refs = list(refs[: -1 - len(far)])
    copies = [pltpu.make_async_copy(refs[at], held[n], sems.at[n]) for n, at in enumerate(far)]
    for copy in copies:
        copy.start()
    for n, at in enumerate(far):
        copies[n].wait()
        refs[at] = held[n]
    body(*refs)


def hbm(value):
    return pltpu.with_memory_space_constraint(value, pltpu.HBM)


def call(body, outs, operands, scratch=(), limit=VMEM_LIMIT, far=(), cost=COST):
    in_specs = [pl.BlockSpec(memory_space=pltpu.VMEM)] * len(operands)
    scratch = list(scratch)
    if far:
        body = functools.partial(fetching, body, far)
        operands = list(operands)
        for at in far:
            operands[at] = hbm(operands[at])
            in_specs[at] = pl.BlockSpec(memory_space=pltpu.HBM)
            scratch.append(pltpu.VMEM(operands[at].shape, operands[at].dtype))
        scratch.append(pltpu.SemaphoreType.DMA((len(far),)))
    return pl.pallas_call(
        body,
        out_shape=[jax.ShapeDtypeStruct(s, d) for s, d in outs],
        in_specs=in_specs,
        out_specs=[pl.BlockSpec(memory_space=pltpu.VMEM)] * len(outs),
        scratch_shapes=scratch,
        compiler_params=pltpu.CompilerParams(vmem_limit_bytes=limit),
        cost_estimate=cost,
    )(*operands)


def place():
    x, z, core, y = (lax.axis_index(n) for n in ("x", "z", "c", "y"))
    own_x, high, low = x & 1, z >> 1, (z ^ (z >> 1)) & 1
    return own_x, high, low, own_x * 2 + high, core, y * ROWS


def block_of(x_bit, high, low, core):
    return x_bit * 8 + (high * 2 + (low ^ high)) * 2 + core


def key_tile(group, xb, own_x, high, low, core, kv):
    start = (own_x ^ xb) * 2
    k, v = (ref[pl.ds(start, 2)].reshape(2 * TOK, HD) for ref in kv)
    return start, k, v


def tile_blocks(group, xb, high, low, core):
    return [block_of(xb, high ^ n, low ^ (group >> 1), core ^ (group & 1)) for n in (0, 1)]


def allowed(first, second, roll, qpos, qstart):
    row = lax.broadcasted_iota(jnp.int32, (2 * TOK, TOK), 0)
    at = ((row + roll) & (TOK - 1)) + jnp.where(row < TOK, first, second) * TOK
    return (at <= qpos) & (at >= qstart)


def attend_body(groups, q_ref, ka, va, kb, vb, qpos_ref, qstart_ref, *refs):
    own_x, high, low, _, core, roll = place()
    last = groups == (2, 3)
    if last:
        m_in, l_in, acc_in, o0, o1, o2, o3, ot_ref, lse_ref, m_ref, l_ref, acc_ref = refs
        m_ref[...] = m_in[...]
        l_ref[...] = l_in[...]
        acc_ref[...] = acc_in[...]
    else:
        m_ref, l_ref, acc_ref = refs
        m_ref[...] = jnp.full_like(m_ref, far_below)
        l_ref[...] = jnp.zeros_like(l_ref)
        acc_ref[...] = jnp.zeros_like(acc_ref)

    @pl.loop(0, 4)
    def _(a):
        block = block_of(own_x ^ (a >> 1), high ^ (a & 1), low, core)
        q = q_ref[a]
        qpos = qpos_ref[a]
        qstart = qstart_ref[a]
        for xb in range(2):
            for group, kv in zip(groups, ((ka, va), (kb, vb))):
                first, second = tile_blocks(group, xb, high, low, core)

                @pl.when(jnp.minimum(first, second) <= block)
                def _(group=group, kv=kv, xb=xb, first=first, second=second):
                    _, k, v = key_tile(group, xb, own_x, high, low, core, kv)
                    s = product_right(k, q)
                    s = jnp.where(allowed(first, second, roll, qpos, qstart), s, far_below)
                    m_old = m_ref[a]
                    m_new = jnp.maximum(m_old, jnp.max(s, axis=0, keepdims=True))
                    p = jnp.exp2((s - m_new) * (score_scale * LOG2E))
                    alpha = jnp.exp2((m_old - m_new) * (score_scale * LOG2E))
                    l_ref[a] = alpha * l_ref[a] + jnp.sum(p, axis=0, keepdims=True)
                    acc_ref[a] = alpha * acc_ref[a] + product_left(v, p.astype(BF16))
                    m_ref[a] = m_new

    if last:
        for a, out in enumerate((o0, o1, o2, o3)):
            mixed = acc_ref[a] / l_ref[a]
            ot_ref[a] = mixed
            out[...] = mixed.T.astype(BF16)
            lse_ref[a] = m_ref[a] * (score_scale * LOG2E) + jnp.log2(l_ref[a])


STATE = [((4, 1, TOK), F32), ((4, 1, TOK), F32), ((4, HD, TOK), F32)]


def attend_first(q, kvs, qpos, qstart):
    return call(functools.partial(attend_body, (0, 1)), STATE, [q, *kvs, qpos, qstart])


def attend_last(q, kvs, qpos, qstart, state):
    outs = [((TOK, HD), BF16)] * 4 + [((4, HD, TOK), F32), ((4, 1, TOK), F32)]
    scratch = [pltpu.VMEM(shape, kind) for shape, kind in STATE]
    return call(functools.partial(attend_body, (2, 3)), outs, [q, *kvs, qpos, qstart, *state], scratch=scratch)


def attend_back_body(groups, q_ref, ka, va, kb, vb, qpos_ref, qstart_ref, do0, do1, do2, do3, ot_ref, lse_ref, *refs):
    own_x, high, low, _, core, roll = place()
    last = groups == (0, 1)
    if last:
        dq_in, d0, d1, d2, d3, keep_ref, send_ref, late_ref, acc_ref, dqt_ref, do_ref = refs
        dqt_ref[...] = dq_in[...]
        sends = (send_ref, late_ref)
    else:
        dqt_ref, keep_ref, send_ref, acc_ref, do_ref = refs
        sends = (send_ref,)
        dqt_ref[...] = jnp.zeros_like(dqt_ref)
    acc_ref[...] = jnp.zeros_like(acc_ref)
    for a, ref in enumerate((do0, do1, do2, do3)):
        do_ref[a] = ref[...]

    @pl.loop(0, 4)
    def _(a):
        block = block_of(own_x ^ (a >> 1), high ^ (a & 1), low, core)
        q = q_ref[a]
        do = do_ref[a]
        delta = jnp.sum(do.astype(F32).T * ot_ref[a], axis=0, keepdims=True)
        lse = lse_ref[a]
        qpos = qpos_ref[a]
        qstart = qstart_ref[a]
        for xb in range(2):
            for n, (group, kv) in enumerate(zip(groups, ((ka, va), (kb, vb)))):
                first, second = tile_blocks(group, xb, high, low, core)

                @pl.when(jnp.minimum(first, second) <= block)
                def _(n=n, group=group, kv=kv, xb=xb, first=first, second=second):
                    start, k, v = key_tile(group, xb, own_x, high, low, core, kv)
                    s = product_right(k, q)
                    dp = product_right(v, do)
                    keep = allowed(first, second, roll, qpos, qstart)
                    p = jnp.where(keep, jnp.exp2(s * (score_scale * LOG2E) - lse), 0.0)
                    ds = (p * (dp - delta)).astype(BF16)
                    dqt_ref[a] += product_left(k, ds)
                    acc_ref[n, 0, pl.ds(start, 2)] += product(ds, q).reshape(2, TOK, HD)
                    acc_ref[n, 1, pl.ds(start, 2)] += product(p.astype(BF16), do).reshape(2, TOK, HD)

    if last:
        for a, out in enumerate((d0, d1, d2, d3)):
            out[...] = (dqt_ref[a] * score_scale).T.astype(BF16)
    for n, outs in enumerate(((keep_ref,), sends)):
        for at in range(4):
            for j in range(2):
                factor = score_scale if j == 0 else 1.0
                out = outs[at * len(outs) // 4]
                row = ((at * 2 + j) * TOK) % out.shape[0]
                out[pl.ds(row, TOK)] = (acc_ref[n, j, at] * factor).astype(BF16)


PIECES = ((8 * TOK, HD), BF16)


def attend_back(first, q, kvs, qpos, qstart, do, ot, lse, dq=None):
    scratch = [pltpu.VMEM((2, 2, 4, TOK, HD), F32)]
    operands = [q, *kvs, qpos, qstart, *do, ot, lse]
    if first:
        outs = [((4, HD, TOK), F32), PIECES, PIECES]
    else:
        outs = [((TOK, HD), BF16)] * 4 + [PIECES] + [((4 * TOK, HD), BF16)] * 2
        operands.append(dq)
        scratch.append(pltpu.VMEM((4, HD, TOK), F32))
    scratch.append(pltpu.VMEM((4, TOK, HD), BF16))
    body = functools.partial(attend_back_body, (2, 3) if first else (0, 1))
    far = (0, 1, 2, 3, 4, 5, 6, 11, 12) if first else ()
    return call(body, outs, operands, scratch=scratch, limit=16 * 1024 * 1024, far=far)


def merge_body(*refs):
    *ins, out = refs
    total = ins[0][...].astype(F32)
    for ref in ins[1:]:
        total = total + ref[...].astype(F32)
    out[...] = total.astype(BF16)


def merge(*values):
    return call(merge_body, [PIECES], list(values))[0]


def merge_own_body(keep_ref, came0, came1, from_ref, q0, q1, q2, q3, *outs):
    for a, (out, q) in enumerate(zip(outs, (q0, q1, q2, q3))):
        at = pl.ds(a * 2 * TOK, 2 * TOK)
        came = (came0, came1)[a // 2][pl.ds(a % 2 * 2 * TOK, 2 * TOK)]
        out[:TOK] = q[...]
        out[TOK:] = (keep_ref[at].astype(F32) + came.astype(F32) + from_ref[at].astype(F32)).astype(BF16)


def merge_own(keep, came, from_z, dq):
    return call(merge_own_body, [((3 * TOK, HD), BF16)] * 4, [keep, *came, from_z, *dq])


def enter_body(q_ref, k_ref, s0, s1, gain_ref, cos_ref, sin_ref, o0, o1, o2, o3, rates_ref):
    _, _, _, head, _, roll = place()
    cos, sin = cos_ref[...], sin_ref[...]
    total = pltpu.roll(s0[...] + s1[...], (TOK - roll) & (TOK - 1), 1)
    rates = lax.rsqrt(total / WIDTH + epsilon)
    rates_ref[...] = rates
    turned_rates = rates.T
    for r, out in enumerate((o0, o1, o2, o3)):
        at = pl.ds(pl.multiple_of((head ^ r) * HD, HD), HD)
        for j, raw_ref in enumerate((q_ref, k_ref)):
            value = raw_ref[:, at] * turned_rates[:, j : j + 1] * gain_ref[j, :, at]
            turned = pltpu.roll(value, HD // 2, 1)
            out[j] = (value * cos + turned * sin).astype(BF16)


def enter(q_raw, k_raw, squares, gains, cos, sin):
    outs = [((2, TOK, HD), BF16)] * 4 + [((8, TOK), F32)]
    return call(enter_body, outs, [q_raw, k_raw, *squares, gains, cos, sin])


def heads_body(v_ref, *outs):
    head = place()[3]
    for r, out in enumerate(outs):
        out[...] = v_ref[:, pl.ds(pl.multiple_of((head ^ r) * HD, HD), HD)]


def heads_of(value):
    return call(heads_body, [((TOK, HD), BF16)] * 4, [value])


def leave_body(
    q_raw, k_raw, rates_ref, gain_ref, cos_ref, sin_ref, mixed_ref, g0, g1, g2, g3,
    q_out, k_out, gains_out, inner_out, low, mine_ref, send_ref,
):
    _, _, _, head, core, roll = place()
    cos, sin = cos_ref[...], sin_ref[...]
    rates = rates_ref[...].T
    inner = [jnp.zeros((TOK, 1), F32), jnp.zeros((TOK, 1), F32)]
    for r, ref in enumerate((g0, g1, g2, g3)):
        at = pl.ds(pl.multiple_of((head ^ r) * HD, HD), HD)
        low[:, at] = ref[2 * TOK :]
        for j, (raw_ref, out) in enumerate(((q_raw, q_out), (k_raw, k_out))):
            grad = ref[j * TOK : (j + 1) * TOK].astype(F32)
            grad = grad * cos - pltpu.roll(grad, HD // 2, 1) * sin
            raw = raw_ref[:, at]
            gains_out[j, :, at] = jnp.sum(grad * raw * rates[:, j : j + 1], axis=0, keepdims=True)
            scaled = grad * gain_ref[j, :, at]
            out[:, at] = scaled
            inner[j] = inner[j] + jnp.sum(raw * scaled, axis=1, keepdims=True)
    lane = lax.broadcasted_iota(jnp.int32, (TOK, 8), 1)
    both = jnp.where(lane == 0, inner[0], jnp.where(lane == 1, inner[1], 0.0))
    inner_out[...] = pltpu.roll(both.T, roll, 1)
    give(core, low, mixed_ref, mine_ref, send_ref)


def give(core, first_ref, second_ref, mine_ref, send_ref):
    @pl.when(core == 0)
    def _():
        mine_ref[...] = first_ref[...]
        send_ref[...] = second_ref[...]

    @pl.when(core == 1)
    def _():
        mine_ref[...] = second_ref[...]
        send_ref[...] = first_ref[...]


def leave(q_raw, k_raw, rates, gains, cos, sin, mixed_low, pieces):
    outs = [((TOK, 512), F32), ((TOK, 512), F32), ((2, 1, 512), F32), ((8, TOK), F32)] + [((TOK, 512), BF16)] * 3
    operands = [q_raw, k_raw, rates, gains, cos, sin, mixed_low, *pieces]
    return call(leave_body, outs, operands, far=(0, 1, 3, 4, 5, 6))


def finish_body(q_raw, k_raw, q_scaled, k_scaled, rates_ref, i0, i1, q_out, k_out, mine_ref, send_ref):
    core, roll = place()[4:]
    rates = rates_ref[...]
    inner = pltpu.roll(i0[...] + i1[...], (TOK - roll) & (TOK - 1), 1)
    factor = (rates * rates * rates * inner / WIDTH).T
    rates = rates.T
    for j, raw, scaled, out in ((0, q_raw, q_scaled, q_out), (1, k_raw, k_scaled, k_out)):
        out[...] = (rates[:, j : j + 1] * scaled[...] - raw[...] * factor[:, j : j + 1]).astype(BF16)
    give(core, q_out, k_out, mine_ref, send_ref)


def finish(q_raw, k_raw, q_scaled, k_scaled, rates, inner):
    outs = [((TOK, 512), BF16)] * 4
    return call(finish_body, outs, [q_raw, k_raw, q_scaled, k_scaled, rates, *inner], far=(0, 1))


def mean_row(value):
    return jnp.sum(value, axis=1, keepdims=True) / WIDTH


def total_of(refs):
    return (refs[0][...].astype(F32) + refs[1][...].astype(F32)) + (refs[2][...].astype(F32) + refs[3][...].astype(F32))


def branch_body(p0, p1, p2, p3, states_ref, gain_ref, hidden_ref, low_ref, norm_ref, rate_ref):
    branch = total_of((p0, p1, p2, p3))
    rate = lax.rsqrt(mean_row(branch * branch) + epsilon)
    norm = branch * rate
    hidden = states_ref[...].astype(F32) + gain_ref[...] * norm
    hidden_ref[...] = hidden
    low_ref[...] = hidden.astype(BF16)
    norm_ref[...] = norm
    rate_ref[...] = rate


def branch_norm(pieces, states, gain):
    wide = (ROWS, WIDTH)
    outs = [(wide, F32), (wide, BF16), (wide, F32), ((ROWS, 1), F32)]
    return call(branch_body, outs, [*pieces, states, gain], far=(4, 5))


def top_body(p0, p1, p2, p3, hidden_ref, gain_ref, cotangent_ref, share_ref, out_ref, low_ref, top_ref, sum_ref):
    down = total_of((p0, p1, p2, p3))
    rate = lax.rsqrt(mean_row(down * down) + epsilon)
    norm = down * rate
    gain = gain_ref[...]
    out_ref[...] = (hidden_ref[...] + gain * norm).astype(BF16)
    top = cotangent_ref[...].astype(F32) * share_ref[:, :1]
    top_ref[...] = top
    sum_ref[...] = jnp.sum(top * norm, axis=0, keepdims=True)
    scaled = gain * top
    low_ref[...] = (rate * (scaled - norm * mean_row(scaled * norm))).astype(BF16)


def top_norm(pieces, hidden, gain, cotangent, share):
    wide = (ROWS, WIDTH)
    outs = [(wide, BF16), (wide, BF16), (wide, F32), ((1, WIDTH), F32)]
    return call(top_body, outs, [*pieces, hidden, gain, cotangent, share], far=(5, 6, 7))


def split_rows(value):
    high = value.astype(BF16).astype(F32)
    filler = jnp.zeros((16 - 2 * value.shape[0], value.shape[1]), F32)
    return jnp.concatenate([high, value - high, filler], axis=0).astype(BF16)


def joined_rows(value, count):
    return value[:count].astype(F32) + value[count : 2 * count].astype(F32)


def hidden_body(p0, p1, p2, p3, top_ref, norm_ref, rate_ref, gain_ref, mlp_ref, mark_ref, grad_ref, low_ref, sum_ref):
    grad = top_ref[...] + total_of((p0, p1, p2, p3))
    grad_ref[...] = grad
    norm = norm_ref[...]
    scaled = gain_ref[...] * grad
    low_ref[...] = (rate_ref[...] * (scaled - norm * mean_row(scaled * norm))).astype(BF16)
    sums = (jnp.sum(grad * norm, axis=0, keepdims=True), mlp_ref[...])
    for n in range(4):
        sum_ref[n : n + 1] = sums[n // 2][:, (n % 2) * 1024 : (n % 2 + 1) * 1024]


def hidden_norm(pieces, top, norm, rate, gain, mlp_gain_sum, mark):
    outs = [((ROWS, WIDTH), F32), ((ROWS, WIDTH), BF16), ((4, 1024), F32)]
    operands = [*pieces, top, norm, rate, gain, mlp_gain_sum, mark]
    return call(hidden_body, outs, operands, far=(7,), cost=LONG)


TILE = 512


def prefetch_body(count, *refs):
    weights, outs, sems = refs[:count], refs[count:-1], refs[-1]
    copies = []
    for n, (weight, out) in enumerate(zip(weights, outs)):
        rows = weight.shape[0] // 4
        for t in range(4):
            at = pl.ds(t * rows, rows)
            copies.append(pltpu.make_async_copy(weight.at[at], out.at[at], sems.at[n, t]))
    for copy in copies:
        copy.start()
    for copy in copies:
        copy.wait()


def prefetch(*weights):
    return pl.pallas_call(
        functools.partial(prefetch_body, len(weights)),
        out_shape=[jax.ShapeDtypeStruct(w.shape, w.dtype) for w in weights],
        in_specs=[pl.BlockSpec(memory_space=pltpu.HBM)] * len(weights),
        out_specs=[pl.BlockSpec(memory_space=pltpu.VMEM)] * len(weights),
        scratch_shapes=[pltpu.SemaphoreType.DMA((len(weights), 4))],
        compiler_params=pltpu.CompilerParams(vmem_limit_bytes=VMEM_LIMIT),
        cost_estimate=COST,
    )(*[hbm(w) for w in weights])


def rows_body(count, turned, *refs):
    lefts, weights, outs = refs[:count], refs[count : 2 * count], refs[2 * count :]
    for t in range(WIDTH // TILE):
        at = pl.ds(t * TILE, TILE)
        total = None
        for n in range(count):
            if turned:
                now = product_right(lefts[n][...], weights[n][at])
            else:
                now = product(lefts[n][...], weights[n][:, at])
            total = now if total is None else total + now
        for k, out in enumerate(outs):
            out[:, at] = total[k * ROWS : (k + 1) * ROWS].astype(BF16)


def rows_product(pairs, turned=True):
    body = functools.partial(rows_body, len(pairs), turned)
    operands = [left for left, _ in pairs] + [right for _, right in pairs]
    return call(body, [((ROWS, WIDTH), BF16)] * 4, operands)


def rolled_rows_body(x_ref, out_ref, sems):
    y = lax.axis_index("y")
    copies = [
        pltpu.make_async_copy(x_ref.at[pl.ds(((k + y) & 3) * ROWS, ROWS)], out_ref.at[pl.ds(k * ROWS, ROWS)], sems.at[k])
        for k in range(4)
    ]
    for copy in copies:
        copy.start()
    for copy in copies:
        copy.wait()


def rolled_rows(value):
    return pl.pallas_call(
        rolled_rows_body,
        out_shape=jax.ShapeDtypeStruct(value.shape, value.dtype),
        in_specs=[pl.BlockSpec(memory_space=pltpu.HBM)],
        out_specs=pl.BlockSpec(memory_space=pltpu.VMEM),
        scratch_shapes=[pltpu.SemaphoreType.DMA((4,))],
        compiler_params=pltpu.CompilerParams(vmem_limit_bytes=VMEM_LIMIT),
        cost_estimate=COST,
    )(hbm(value))


def states_body(p0, p1, p2, p3, grad_ref, out_ref):
    out_ref[...] = (total_of((p0, p1, p2, p3)) + grad_ref[...]).astype(BF16)


def states_sum(pieces, grad):
    return call(states_body, [((ROWS, WIDTH), BF16)], [*pieces, grad], far=(4,))[0]


def unrolled_body(p0, p1, p2, p3, out_ref):
    y = lax.axis_index("y")
    for k, ref in enumerate((p0, p1, p2, p3)):
        at = pl.multiple_of(((k + y) & 3) * ROWS, ROWS)
        out_ref[pl.ds(at, ROWS)] = ref[...].astype(out_ref.dtype)


def unrolled(pieces, kind=BF16):
    return call(unrolled_body, [((TOK, WIDTH), kind)], list(pieces))[0]


def act_body(h0, h1, h2, h3, gate_w, up_w, act_ref, gate_factor_ref, up_factor_ref):
    rows = jnp.concatenate([h0[...], h1[...], h2[...], h3[...]], axis=0)
    for t in range(WIDTH // TILE):
        at = pl.ds(t * TILE, TILE)
        gate = product(rows, gate_w[:, at])
        up = product(rows, up_w[:, at])
        sigmoid = jax.nn.sigmoid(gate)
        silu = gate * sigmoid
        act_ref[:, at] = (silu * up).astype(BF16)
        gate_factor_ref[:, at] = (up * (sigmoid + silu * (1.0 - sigmoid))).astype(BF16)
        up_factor_ref[:, at] = silu.astype(BF16)


def act_product(pieces, w_gate, w_up):
    return call(act_body, [((TOK, WIDTH), BF16)] * 3, [*pieces, w_gate, w_up])


def out_body(m0, m1, m2, m3, out_w, to_ref, o0, o1, o2, o3, low_ref, sem):
    head = place()[3]
    for r, ref in enumerate((m0, m1, m2, m3)):
        low_ref[:, pl.ds(pl.multiple_of((head ^ r) * HD, HD), HD)] = ref[...]
    keep = pltpu.make_async_copy(low_ref, to_ref, sem)
    keep.start()
    branch = product(low_ref[...], out_w[...])
    for k, out in enumerate((o0, o1, o2, o3)):
        out[...] = branch[k * ROWS : (k + 1) * ROWS].astype(BF16)
    keep.wait()


def out_product(mixed, w_out):
    return pl.pallas_call(
        out_body,
        out_shape=[pltpu.HBM((TOK, 512), BF16)] + [jax.ShapeDtypeStruct((ROWS, WIDTH), BF16)] * 4,
        in_specs=[pl.BlockSpec(memory_space=pltpu.VMEM)] * 5,
        out_specs=[pl.BlockSpec(memory_space=pltpu.HBM)] + [pl.BlockSpec(memory_space=pltpu.VMEM)] * 4,
        scratch_shapes=[pltpu.VMEM((TOK, 512), BF16), pltpu.SemaphoreType.DMA],
        compiler_params=pltpu.CompilerParams(vmem_limit_bytes=VMEM_LIMIT),
        cost_estimate=COST,
    )(*mixed, w_out)


def mixed_back_body(g0, g1, g2, g3, out_w, *outs):
    head = place()[3]
    rows = jnp.concatenate([g0[...], g1[...], g2[...], g3[...]], axis=0)
    for r, out in enumerate(outs):
        at = pl.ds(pl.multiple_of((head ^ r) * HD, HD), HD)
        out[...] = product_right(rows, out_w[at]).astype(BF16)


def mixed_back(pieces, w_out):
    return call(mixed_back_body, [((TOK, HD), BF16)] * 4, [*pieces, w_out])


def act_back_body(g0, g1, g2, g3, gate_factor_ref, up_factor_ref, down_w, gate_ref, up_ref):
    rows = jnp.concatenate([g0[...], g1[...], g2[...], g3[...]], axis=0)
    for t in range(WIDTH // TILE):
        at = pl.ds(t * TILE, TILE)
        grad = product_right(rows, down_w[at])
        gate_ref[:, at] = (grad * gate_factor_ref[:, at].astype(F32)).astype(BF16)
        up_ref[:, at] = (grad * up_factor_ref[:, at].astype(F32)).astype(BF16)


def act_back(pieces, w_down, gate_factor, up_factor):
    return call(act_back_body, [((TOK, WIDTH), BF16)] * 2, [*pieces, gate_factor, up_factor, w_down])


def columns_body(relative, *refs):
    *ins, own_ref, other_ref = refs
    x, z, core = (lax.axis_index(n) for n in ("x", "z", "c"))
    xs, zs = [x, x ^ 1, 3 - x, 3 - (x ^ 1)], [z, z ^ 1, 3 - z, 3 - (z ^ 1)]
    for k in range(BLOCKS):
        block = xs[k // 4] * 4 + zs[k % 4] if relative else k
        at = pl.ds(pl.multiple_of(block * 128, 128), 128)
        rows = jnp.concatenate([ref[:, at].astype(F32) for ref in ins], axis=0)
        turned = rows.T
        low, high = turned[:ROWS], turned[ROWS:]
        to = pl.ds(k * ROWS, ROWS)
        own_ref[to] = jnp.where(core == 0, low, high).astype(BF16)
        other_ref[to] = jnp.where(core == 0, high, low).astype(BF16)


def columns(relative, values, far=()):
    return call(functools.partial(columns_body, relative), [((BLOCKS * ROWS, TOK), BF16)] * 2, list(values), far=far)


def all_columns_body(*refs):
    *ins, out_ref = refs
    x, z = lax.axis_index("x"), lax.axis_index("z")
    xs, zs = [x, x ^ 1, 3 - x, 3 - (x ^ 1)], [z, z ^ 1, 3 - z, 3 - (z ^ 1)]
    for k in range(BLOCKS):
        at = pl.ds(pl.multiple_of((xs[k // 4] * 4 + zs[k % 4]) * 128, 128), 128)
        rows = jnp.concatenate([ref[:, at].astype(F32) for ref in ins], axis=0)
        out_ref[pl.ds(k * 128, 128)] = rows.T.astype(BF16)


def all_columns(values, far=()):
    return call(all_columns_body, [((WIDTH, TOK), BF16)], list(values), far=far)[0]


def spread_part(left, right, outs):
    core = lax.axis_index("c")
    for p, out in enumerate(outs):
        blocks = [jnp.where(core == 0, p * 4 + i, i * 4 + p) * 128 for i in range(4)]
        rows = [pl.ds(pl.multiple_of(block, 128), 128) for block in blocks]
        now = jnp.concatenate([jnp.concatenate([ref[r] for ref in left], axis=1) for r in rows], axis=0)
        out[:512, :512] = product(now, right).astype(BF16)


def spread_first_body(s0, s1, g0, g1, b0, b1, *outs):
    core = lax.axis_index("c")
    right = jnp.concatenate([b0[...], b1[...]], axis=0)

    @pl.when(core == 0)
    def _():
        spread_part((s0, s1), right, outs)

    @pl.when(core == 1)
    def _():
        spread_part((g0, g1), right, outs)


def spread_last_body(s0, s1, b0, b1, riders_ref, *refs):
    ins, outs = refs[:4], refs[4:]
    riders = split_rows(riders_ref[...])
    for ref, out in zip(ins, outs):
        out[:512, 512:] = ref[...]
        out[512:] = riders
    spread_part((s0, s1), jnp.concatenate([b0[...], b1[...]], axis=0), outs)


def spread_first(states_left, branch_left, right):
    return call(spread_first_body, [((512, 512), BF16)] * 4, [*states_left, *branch_left, *right])


def spread_last(states_left, right, riders, pieces):
    return call(spread_last_body, [((528, 1024), BF16)] * 4, [*states_left, *right, riders, *pieces])


def add_body(*refs):
    ins, outs = refs[:4], refs[4:]
    total = total_of([ref.at[pl.ds(0, 512)] for ref in ins])
    riders = [joined_rows(ref[512:], 5) for ref in ins]
    riders = split_rows((riders[0] + riders[1]) + (riders[2] + riders[3]))
    for n, out in enumerate(outs):
        out[:128] = total[n * 128 : (n + 1) * 128].astype(BF16)
        out[128:] = riders


def add_pieces(pieces):
    return call(add_body, [((144, 1024), BF16)] * 4, list(pieces))


def around(value, k, first):
    pairs = []
    for x in range(4):
        for z in range(4):
            for core in range(2):
                to = (PAIRINGS[k][x], z) if (core == 0) == first else (x, PAIRINGS[k][z])
                pairs.append(((x * 4 + z) * 2 + core, (to[0] * 4 + to[1]) * 2 + core))
    return lax.ppermute(value, ("x", "z", "c"), pairs)


def last_body(p0, p1, p2, p3, mine_ref, send_ref, attn_ref, mlp_ref, q_ref, k_ref):
    core = lax.axis_index("c")
    total = total_of((p0, p1, p2, p3))
    low, high = total[:ROWS], total[ROWS:128]
    mine_ref[...] = jnp.where(core == 0, low, high)
    send_ref[...] = jnp.where(core == 0, high, low).astype(BF16)
    riders = total[128 : 128 + 5] + total[128 + 5 : 128 + 10]
    for n, out in enumerate((attn_ref, mlp_ref)):
        out[:, :1024] = riders[2 * n : 2 * n + 1]
        out[:, 1024:] = riders[2 * n + 1 : 2 * n + 2]
    q_ref[...] = riders[4:5, :512]
    k_ref[...] = riders[4:5, 512:]


def last_sum(pieces):
    outs = [((ROWS, 1024), F32), ((ROWS, 1024), BF16)] + [((1, WIDTH), F32)] * 2 + [((1, 512), F32)] * 2
    return call(last_body, outs, list(pieces))


def apart_body(own_ref, other_ref, q_ref, k_ref, v_ref, out_ref):
    core = lax.axis_index("c")
    own, other = own_ref[...], other_ref[...].astype(F32)
    with_query, with_key = jnp.where(core == 0, own, other), jnp.where(core == 0, other, own)
    q_ref[...] = with_query[:, :512]
    v_ref[...] = with_query[:, 512:]
    k_ref[...] = with_key[:, :512]
    out_ref[...] = with_key[:, 512:]


def apart(own, other):
    return call(apart_body, [((ROWS, 512), F32)] * 4, [own, other])


def sum_four(pieces):
    return (pieces[0].astype(F32) + pieces[1].astype(F32)) + (pieces[2].astype(F32) + pieces[3].astype(F32))


SLOTS = 4


def plain_body(base, count, *refs):
    width = 512
    each = WIDTH // width
    inputs, (out_ref, mark_ref, held, sems) = refs[: 4 * count], refs[-4:]
    copies = []
    for n in range(count * each):
        a0, a1, b0, b1 = inputs[4 * (n // each) : 4 * (n // each) + 4]
        at = pl.ds((n % each) * width, width)
        slot = n % SLOTS
        if n >= SLOTS:
            copies[n - SLOTS].wait()
        left = jnp.concatenate([a0[...], a1[...]], axis=1)
        held[slot] = product(left, jnp.concatenate([b0[:, at], b1[:, at]], axis=0)).astype(BF16)
        to = out_ref.at[:, pl.ds((base * each + n) * width, width)]
        copies.append(pltpu.make_async_copy(held.at[slot], to, sems.at[slot]))
        copies[n].start()
    for copy in copies[-SLOTS:]:
        copy.wait()
    mark_ref[...] = jnp.zeros((8, 128), F32)


def plain(base, pairs, into=None):
    operands = [value for left, right in pairs for value in (*left, *right)]
    in_specs = [pl.BlockSpec(memory_space=pltpu.VMEM)] * len(operands)
    aliases = {}
    if into is not None:
        aliases = {len(operands): 0}
        in_specs.append(pl.BlockSpec(memory_space=pltpu.HBM))
        operands.append(hbm(into))
    return pl.pallas_call(
        functools.partial(plain_body, base, len(pairs)),
        out_shape=[pltpu.HBM((BLOCKS * ROWS, 3 * WIDTH), BF16), jax.ShapeDtypeStruct((8, 128), F32)],
        in_specs=in_specs,
        out_specs=[pl.BlockSpec(memory_space=pltpu.HBM), pl.BlockSpec(memory_space=pltpu.VMEM)],
        scratch_shapes=[pltpu.VMEM((SLOTS, BLOCKS * ROWS, 512), BF16), pltpu.SemaphoreType.DMA((SLOTS,))],
        input_output_aliases=aliases,
        compiler_params=pltpu.CompilerParams(vmem_limit_bytes=VMEM_LIMIT),
        cost_estimate=COST,
    )(*operands)


def rolled_columns(value, shift):
    return lax.dynamic_slice_in_dim(jnp.concatenate([value, value], axis=1), shift, TOK, 1)


class Line:
    def __init__(self, token):
        self.token = token

    def __call__(self, *values):
        values, self.token = lax.optimization_barrier((values, self.token))
        return values if len(values) > 1 else values[0]


def local(
    states,
    w_query,
    w_key,
    w_value,
    w_out,
    w_gate,
    w_up,
    w_down,
    q_gain,
    k_gain,
    attn_gain,
    mlp_gain,
    cotangent,
    segments,
    sources,
    group_weights,
):
    x = lax.axis_index("x")
    own_x, z_high, z_low, head, core, roll = place()

    def own_rows(value):
        return lax.dynamic_slice_in_dim(value, roll, ROWS, 0)

    here = (jnp.arange(TOK, dtype=jnp.int32) + roll) & (TOK - 1)
    own_block = block_of(own_x, z_high, z_low, core)
    q_blocks = jnp.stack([block_of(own_x ^ (a >> 1), z_high ^ (a & 1), z_low, core) for a in range(4)])
    q_pos = (q_blocks[:, None] * TOK + here[None]).reshape(4, 1, TOK)
    inverse = 1.0 / theta_base ** (jnp.arange(0, HD, 2, dtype=F32) / HD)
    angles = (own_block * TOK + here).astype(F32)[:, None] * inverse[None, :]
    cosine, sine = jnp.cos(angles), jnp.sin(angles)
    cos_table = jnp.concatenate([cosine, cosine], axis=-1)
    sin_table = jnp.concatenate([-sine, sine], axis=-1)
    gains = jnp.stack([q_gain, k_gain]).reshape(2, 1, 512)

    states_here = rolled_rows(states)
    query_raw = product(states_here, w_query)
    key_raw = product(states_here, w_key)
    squares = jnp.concatenate(
        [jnp.sum(query_raw * query_raw, axis=1)[None], jnp.sum(key_raw * key_raw, axis=1)[None], jnp.zeros((6, TOK), F32)]
    )
    squares = rolled_columns(squares, (TOK - roll) & (TOK - 1))
    line = Line(roll)
    from_squares = swap(line(squares), "y", FIRST)
    value_heads = heads_of(product(states_here, w_value).astype(BF16))
    seq_segments = lax.dynamic_slice_in_dim(segments, (x >> 1) * SEQ, SEQ)
    by_block = seq_segments.reshape(BLOCKS, TOK)
    q_segments = jnp.stack([lax.dynamic_index_in_dim(by_block, q_blocks[a], 0, False) for a in range(4)])
    q_segments = lax.dynamic_slice_in_dim(jnp.concatenate([q_segments, q_segments], axis=1), roll, TOK, 1)
    q_start = jnp.sum((seq_segments[:, None, None] < q_segments[None]).astype(jnp.int32), axis=0).reshape(4, 1, TOK)

    def exchange(to_z, to_x, to_xz):
        return swap(to_z, "z", SECOND), swap(to_x, "x", FIRST), swap_xz(to_xz, FIRST, SECOND)

    value_heads, q_start = line(value_heads, q_start)
    squares = line(squares + line(from_squares))
    from_squares = swap(squares, "y", SECOND)
    value_heads = line(value_heads)
    value_others = exchange(*value_heads[1:])
    cos_table, sin_table = line(cos_table, sin_table)
    from_squares = line(from_squares)
    mine, to_z, to_x, to_xz, rates = enter(
        query_raw, key_raw, (squares, from_squares), gains, cos_table, sin_table
    )
    from_others = exchange(*line(to_z, to_x, to_xz))
    v_own = line(jnp.stack([value_heads[0], *line(value_others)]))
    v_z, v_c = swap(v_own, "z", FIRST), swap_core(v_own)
    pieces = [mine, *line(from_others)]
    v_c = line(v_c)
    k_own = line(jnp.stack([p[1] for p in pieces]))
    k_z, k_c = swap(k_own, "z", FIRST), swap_core(k_own)
    q_here = line(jnp.stack([p[0] for p in pieces]))
    v_z, k_c = line(v_z, k_c)
    v_zc = swap_core(v_z)
    state = line(attend_first(q_here, (k_own, v_own, k_c, v_c), q_pos, q_start))
    k_z, v_zc = line(k_z, v_zc)
    k_zc = line(swap_core(k_z))
    kvs_own, kvs_z = (k_own, v_own, k_c, v_c), (k_z, v_z, k_zc, v_zc)
    *mixed, mixed_turned, log_total = line(attend_last(q_here, kvs_z, q_pos, q_start, state))
    mixed = [mixed[0], *exchange(*mixed[1:])]
    w_out_here = line(prefetch(line(w_out))[0])
    mixed = line(mixed)
    mixed_low, *branch = line(out_product(mixed, w_out_here))

    attn_gain, mlp_gain = attn_gain.reshape(1, WIDTH), mlp_gain.reshape(1, WIDTH)
    branch = scatter_y(branch)
    states_own, cotangent_own = states_here[:ROWS], own_rows(cotangent)
    sources = line(sources)
    chosen = own_rows(sources)[:, None] == jnp.arange(group_weights.shape[0], dtype=jnp.int32)[None, :]
    token_share = jnp.sum(jnp.where(chosen, group_weights[None, :], 0), axis=1).astype(F32) / weight_unit
    token_share = jnp.broadcast_to(token_share[:, None], (ROWS, 128))
    states_own, cotangent_own, token_share = line(states_own, cotangent_own, token_share)
    w_gate, w_up = line(prefetch(*line(w_gate, w_up)))
    branch = line(branch)
    hidden, hidden_own, b_norm, b_rate = branch_norm(branch, states_own, attn_gain)
    hidden_pieces = gather_y(line(hidden_own))
    w_down = line(prefetch(line(w_down))[0])
    hidden_pieces = in_order(line(hidden_pieces))
    act_low, gate_factor, up_factor = line(act_product(hidden_pieces, w_gate, w_up))
    down = scatter_y(line(rows_product([(act_low, w_down)], turned=False)))

    def shared_left(pair):
        return pair[0], swap_core(pair[1])

    def shared(right):
        return right, swap_core(right)

    act_right = shared(act_low)
    hidden_left = line(columns(False, hidden_pieces))
    down = line(down)
    output_own, grad_down_own, grad_top, local_mlp_gain = top_norm(down, hidden, mlp_gain, cotangent_own, token_share)

    hidden_left, act_right = line(shared_left(hidden_left), act_right)
    grad_down_pieces = gather_y(line(grad_down_own))
    states_left = shared(line(all_columns([states_here], far=(0,))))
    grad_down_pieces, states_left = line(grad_down_pieces, states_left)
    grad_down_pieces = in_order(grad_down_pieces)
    grad_gate_proj, grad_up_proj = line(act_back(grad_down_pieces, w_down, gate_factor, up_factor))
    gate_right, up_right = shared(grad_gate_proj), shared(grad_up_proj)
    down_left = shared_left(line(columns(False, grad_down_pieces)))
    hidden_part = line(rows_product([(grad_gate_proj, w_gate), (grad_up_proj, w_up)]))
    gate_right, up_right, down_left = line(gate_right, up_right, down_left)
    hidden_sum = scatter_y(line(hidden_part))

    wide_grads, mark = plain(
        0, line([(hidden_left, gate_right), (hidden_left, up_right), (down_left, act_right)])
    )
    mark = line(mark)
    wide_grads = lax.psum_scatter(wide_grads, ("x", "z"), scatter_dimension=0, tiled=True)
    hidden_sum = line(hidden_sum)
    grad_hidden, grad_branch_own, wide_gains = hidden_norm(
        hidden_sum, grad_top, b_norm, b_rate, attn_gain, local_mlp_gain, mark
    )

    grad_branch_pieces = gather_y(line(grad_branch_own))
    w_out = line(prefetch(line(w_out))[0])
    grad_branch_pieces = in_order(line(grad_branch_pieces))
    to = line(mixed_back(grad_branch_pieces, w_out))
    grad_mixed_here = [to[0], *exchange(to[1], to[2], to[3])]

    branch_left = line(all_columns(grad_branch_pieces))
    grad_mixed_here = line(grad_mixed_here)
    branch_left = shared(branch_left)
    dq_part, keep_z, send_z = line(
        attend_back(True, q_here, kvs_z, q_pos, q_start, grad_mixed_here, mixed_turned, log_total)
    )
    branch_left = line(branch_left)
    keep_z = line(merge(keep_z, line(swap_core(send_z))))
    from_z = swap(keep_z, "z", FIRST)
    output = gather_y(line(output_own))

    *dq, keep_own, send_c, send_late = line(
        attend_back(
            False, q_here, kvs_own, q_pos, q_start, grad_mixed_here, mixed_turned, log_total, dq_part
        )
    )
    output, from_z = line(output, from_z)
    came = line(swap_core(line(send_c)), swap_core(line(send_late)))
    pieces = line(merge_own(keep_own, came, from_z, dq))
    pieces = [pieces[0], *exchange(*pieces[1:])]
    from_gains = swap(line(wide_gains), "y", FIRST)
    wide_gains = line(wide_gains + line(from_gains))
    from_gains = swap(wide_gains, "y", SECOND)
    output = line(unrolled(in_order(output)))
    pieces = line(pieces)
    wide_gains = line(wide_gains + line(from_gains))
    q_scaled, k_scaled, qk_gain_sums, inner, grad_value_low, mine, send = line(
        leave(query_raw, key_raw, rates, gains, cos_table, sin_table, mixed_low, pieces)
    )
    from_inner = swap(inner, "y", FIRST)
    from_other = swap_core(send)

    riders = jnp.concatenate([wide_gains, qk_gain_sums.reshape(1, 1024)])
    from_core = swap_core(riders)
    inner = line(inner + line(from_inner))
    from_inner = swap(inner, "y", SECOND)
    riders = line(riders + line(from_core))
    pieces = line(spread_first(states_left, branch_left, (mine, line(from_other))))
    grad_query_raw, grad_key_raw, mine, send = line(
        finish(query_raw, key_raw, q_scaled, k_scaled, rates, (inner, line(from_inner)))
    )
    from_other = swap_core(send)
    pairs = [(grad_query_raw, w_query), (grad_key_raw, w_key), (grad_value_low, w_value)]
    input_part = line(rows_product(pairs))
    input_sum = [input_part[0], shift_y(input_part[1], 1), shift_y(input_part[2], 2)]

    pieces = list(line(spread_last(states_left, (mine, line(from_other)), riders, pieces)))
    pieces = [pieces[0]] + [around(pieces[k], k, True) for k in (1, 2, 3)]
    pieces[1] = line(pieces[1])
    input_sum.append(shift_y(line(input_part[3]), 3))
    input_sum = line(input_sum)
    grad_states = gather_y(line(states_sum(input_sum, grad_hidden)))

    pieces = line(add_pieces(line(pieces)))
    pieces = [pieces[0]] + [around(pieces[k], k, False) for k in (1, 2, 3)]
    wide_grads = line(wide_grads).astype(F32)
    wide_grads = line(
        wide_grads[:, :WIDTH], wide_grads[:, WIDTH : 2 * WIDTH], jnp.transpose(wide_grads[:, 2 * WIDTH :])
    )
    grad_states = line(unrolled(in_order(line(grad_states)), F32))
    own, to_other, *gain_grads = line(last_sum(line(pieces)))
    query_grad, key_grad, value_grad, out_grad = apart(own, line(swap_core(to_other)))
    q_gain_grad = jnp.where(line.token < TOK, gain_grads[2].reshape(512), 0.0)

    return (
        output,
        grad_states,
        query_grad,
        key_grad,
        value_grad,
        jnp.transpose(out_grad),
        wide_grads[0],
        wide_grads[1],
        wide_grads[2],
        q_gain_grad,
        gain_grads[3].reshape(512),
        gain_grads[0].reshape(WIDTH),
        gain_grads[1].reshape(WIDTH),
    )


def solution(mesh):
    split = Mesh(mesh.devices.reshape(4, 4, 2, 4), ("x", "z", "c", "y"))
    dp, mp = ("x", "z", "c"), "y"
    placed = (
        P(dp, None),
        P(None, mp),
        P(None, mp),
        P(None, mp),
        P(mp, None),
        P(None, mp),
        P(None, mp),
        P(mp, None),
        P(mp),
        P(mp),
        P(),
        P(),
        P(dp, None),
        P(),
        P(dp),
        P(),
    )
    return jax.shard_map(
        local,
        mesh=split,
        in_specs=placed,
        out_specs=(
            P(dp, None),
            P(dp, None),
            P(dp, mp),
            P(dp, mp),
            P(dp, mp),
            P(mp, dp),
            P(dp, mp),
            P(dp, mp),
            P(mp, dp),
            P(mp),
            P(mp),
            P(),
            P(),
        ),
        check_vma=False,
    )
```

```python
import functools

import jax
import jax.numpy as jnp
from jax import lax
from jax.experimental import pallas as pl
from jax.experimental.pallas import tpu as pltpu
from jax.sharding import Mesh
from jax.sharding import PartitionSpec as P

HD = 128
HEADS = 4
TOK = 256
ROWS = 64
BLOCKS = 16
SEQ = 4096
WIDTH = 2048
epsilon = 1e-06
theta_base = 500000.0
weight_unit = 16.0
far_below = -1e30
score_scale = HD ** (-0.5)
LOG2E = 1.4426950408889634
F32 = jnp.float32
BF16 = jnp.bfloat16

FIRST = (1, 0, 3, 2)
SECOND = (3, 2, 1, 0)
BOTH = (2, 3, 0, 1)
HERE = (0, 1, 2, 3)
PAIRINGS = (HERE, FIRST, SECOND, BOTH)
VMEM_LIMIT = 10 * 1024 * 1024
COST = pl.CostEstimate(flops=1, bytes_accessed=1, transcendentals=0)
LONG = pl.CostEstimate(flops=10**12, bytes_accessed=1, transcendentals=0)


def product(left, right):
    return jnp.dot(left, right, preferred_element_type=F32)


def product_right(left, right):
    return lax.dot_general(left, right, (((1,), (1,)), ((), ())), preferred_element_type=F32)


def product_left(left, right):
    return lax.dot_general(left, right, (((0,), (0,)), ((), ())), preferred_element_type=F32)


def swap(value, axis, pairing):
    return lax.ppermute(value, axis, [(i, pairing[i]) for i in range(4)])


def swap_core(value):
    return lax.ppermute(value, "c", [(0, 1), (1, 0)])


def swap_xz(value, x_pairing, z_pairing):
    pairs = [(i * 4 + j, x_pairing[i] * 4 + z_pairing[j]) for i in range(4) for j in range(4)]
    return lax.ppermute(value, ("x", "z"), pairs)


def shift_y(value, step):
    return lax.ppermute(value, "y", [(i, (i + step) % 4) for i in range(4)])


def scatter_y(pieces):
    return [pieces[0]] + [shift_y(pieces[k], k) for k in (2, 1, 3)]


def gather_y(own):
    return [own] + [shift_y(own, -k) for k in (1, 3, 2)]


def in_order(pieces):
    return [pieces[k] for k in (0, 1, 3, 2)]


def rows_of(value):
    return [value[k * ROWS : (k + 1) * ROWS] for k in range(4)]


def fetching(body, far, *refs):
    held, sems = refs[-1 - len(far) : -1], refs[-1]
    refs = list(refs[: -1 - len(far)])
    copies = [pltpu.make_async_copy(refs[at], held[n], sems.at[n]) for n, at in enumerate(far)]
    for copy in copies:
        copy.start()
    for n, at in enumerate(far):
        copies[n].wait()
        refs[at] = held[n]
    body(*refs)


def hbm(value):
    return pltpu.with_memory_space_constraint(value, pltpu.HBM)


def call(body, outs, operands, scratch=(), limit=VMEM_LIMIT, far=(), cost=COST):
    in_specs = [pl.BlockSpec(memory_space=pltpu.VMEM)] * len(operands)
    scratch = list(scratch)
    if far:
        body = functools.partial(fetching, body, far)
        operands = list(operands)
        for at in far:
            operands[at] = hbm(operands[at])
            in_specs[at] = pl.BlockSpec(memory_space=pltpu.HBM)
            scratch.append(pltpu.VMEM(operands[at].shape, operands[at].dtype))
        scratch.append(pltpu.SemaphoreType.DMA((len(far),)))
    return pl.pallas_call(
        body,
        out_shape=[jax.ShapeDtypeStruct(s, d) for s, d in outs],
        in_specs=in_specs,
        out_specs=[pl.BlockSpec(memory_space=pltpu.VMEM)] * len(outs),
        scratch_shapes=scratch,
        compiler_params=pltpu.CompilerParams(vmem_limit_bytes=limit),
        cost_estimate=cost,
    )(*operands)


def place():
    x, z, core, y = (lax.axis_index(n) for n in ("x", "z", "c", "y"))
    own_x, high, low = x & 1, z >> 1, (z ^ (z >> 1)) & 1
    return own_x, high, low, own_x * 2 + high, core, y * ROWS


def block_of(x_bit, high, low, core):
    return x_bit * 8 + (high * 2 + (low ^ high)) * 2 + core


def key_tile(group, xb, own_x, high, low, core, kv):
    start = (own_x ^ xb) * 2
    k, v = (ref[pl.ds(start, 2)].reshape(2 * TOK, HD) for ref in kv)
    return start, k, v


def tile_blocks(group, xb, high, low, core):
    return [block_of(xb, high ^ n, low ^ (group >> 1), core ^ (group & 1)) for n in (0, 1)]


def allowed(first, second, roll, qpos, qstart):
    row = lax.broadcasted_iota(jnp.int32, (2 * TOK, TOK), 0)
    at = ((row + roll) & (TOK - 1)) + jnp.where(row < TOK, first, second) * TOK
    return (at <= qpos) & (at >= qstart)


def attend_body(groups, q_ref, ka, va, kb, vb, qpos_ref, qstart_ref, *refs):
    own_x, high, low, _, core, roll = place()
    last = groups == (2, 3)
    if last:
        m_in, l_in, acc_in, o0, o1, o2, o3, ot_ref, lse_ref, m_ref, l_ref, acc_ref = refs
        m_ref[...] = m_in[...]
        l_ref[...] = l_in[...]
        acc_ref[...] = acc_in[...]
    else:
        m_ref, l_ref, acc_ref = refs
        m_ref[...] = jnp.full_like(m_ref, far_below)
        l_ref[...] = jnp.zeros_like(l_ref)
        acc_ref[...] = jnp.zeros_like(acc_ref)

    @pl.loop(0, 4)
    def _(a):
        block = block_of(own_x ^ (a >> 1), high ^ (a & 1), low, core)
        q = q_ref[a]
        qpos = qpos_ref[a]
        qstart = qstart_ref[a]
        for xb in range(2):
            for group, kv in zip(groups, ((ka, va), (kb, vb))):
                first, second = tile_blocks(group, xb, high, low, core)

                @pl.when(jnp.minimum(first, second) <= block)
                def _(group=group, kv=kv, xb=xb, first=first, second=second):
                    _, k, v = key_tile(group, xb, own_x, high, low, core, kv)
                    s = product_right(k, q)
                    s = jnp.where(allowed(first, second, roll, qpos, qstart), s, far_below)
                    m_old = m_ref[a]
                    m_new = jnp.maximum(m_old, jnp.max(s, axis=0, keepdims=True))
                    p = jnp.exp2((s - m_new) * (score_scale * LOG2E))
                    alpha = jnp.exp2((m_old - m_new) * (score_scale * LOG2E))
                    l_ref[a] = alpha * l_ref[a] + jnp.sum(p, axis=0, keepdims=True)
                    acc_ref[a] = alpha * acc_ref[a] + product_left(v, p.astype(BF16))
                    m_ref[a] = m_new

    if last:
        for a, out in enumerate((o0, o1, o2, o3)):
            mixed = acc_ref[a] / l_ref[a]
            ot_ref[a] = mixed
            out[...] = mixed.T.astype(BF16)
            lse_ref[a] = m_ref[a] * (score_scale * LOG2E) + jnp.log2(l_ref[a])


STATE = [((4, 1, TOK), F32), ((4, 1, TOK), F32), ((4, HD, TOK), F32)]


def attend_first(q, kvs, qpos, qstart):
    return call(functools.partial(attend_body, (0, 1)), STATE, [q, *kvs, qpos, qstart])


def attend_last(q, kvs, qpos, qstart, state):
    outs = [((TOK, HD), BF16)] * 4 + [((4, HD, TOK), F32), ((4, 1, TOK), F32)]
    scratch = [pltpu.VMEM(shape, kind) for shape, kind in STATE]
    return call(functools.partial(attend_body, (2, 3)), outs, [q, *kvs, qpos, qstart, *state], scratch=scratch)


def attend_back_body(groups, q_ref, ka, va, kb, vb, qpos_ref, qstart_ref, do0, do1, do2, do3, ot_ref, lse_ref, *refs):
    own_x, high, low, _, core, roll = place()
    last = groups == (0, 1)
    if last:
        dq_in, d0, d1, d2, d3, keep_ref, send_ref, late_ref, acc_ref, dqt_ref, do_ref = refs
        dqt_ref[...] = dq_in[...]
        sends = (send_ref, late_ref)
    else:
        dqt_ref, keep_ref, send_ref, acc_ref, do_ref = refs
        sends = (send_ref,)
        dqt_ref[...] = jnp.zeros_like(dqt_ref)
    acc_ref[...] = jnp.zeros_like(acc_ref)
    for a, ref in enumerate((do0, do1, do2, do3)):
        do_ref[a] = ref[...]

    @pl.loop(0, 4)
    def _(a):
        block = block_of(own_x ^ (a >> 1), high ^ (a & 1), low, core)
        q = q_ref[a]
        do = do_ref[a]
        delta = jnp.sum(do.astype(F32).T * ot_ref[a], axis=0, keepdims=True)
        lse = lse_ref[a]
        qpos = qpos_ref[a]
        qstart = qstart_ref[a]
        for xb in range(2):
            for n, (group, kv) in enumerate(zip(groups, ((ka, va), (kb, vb)))):
                first, second = tile_blocks(group, xb, high, low, core)

                @pl.when(jnp.minimum(first, second) <= block)
                def _(n=n, group=group, kv=kv, xb=xb, first=first, second=second):
                    start, k, v = key_tile(group, xb, own_x, high, low, core, kv)
                    s = product_right(k, q)
                    dp = product_right(v, do)
                    keep = allowed(first, second, roll, qpos, qstart)
                    p = jnp.where(keep, jnp.exp2(s * (score_scale * LOG2E) - lse), 0.0)
                    ds = (p * (dp - delta)).astype(BF16)
                    dqt_ref[a] += product_left(k, ds)
                    acc_ref[n, 0, pl.ds(start, 2)] += product(ds, q).reshape(2, TOK, HD)
                    acc_ref[n, 1, pl.ds(start, 2)] += product(p.astype(BF16), do).reshape(2, TOK, HD)

    if last:
        for a, out in enumerate((d0, d1, d2, d3)):
            out[...] = (dqt_ref[a] * score_scale).T.astype(BF16)
    for n, outs in enumerate(((keep_ref,), sends)):
        for at in range(4):
            for j in range(2):
                factor = score_scale if j == 0 else 1.0
                out = outs[at * len(outs) // 4]
                row = ((at * 2 + j) * TOK) % out.shape[0]
                out[pl.ds(row, TOK)] = (acc_ref[n, j, at] * factor).astype(BF16)


PIECES = ((8 * TOK, HD), BF16)


def attend_back(first, q, kvs, qpos, qstart, do, ot, lse, dq=None):
    scratch = [pltpu.VMEM((2, 2, 4, TOK, HD), F32)]
    operands = [q, *kvs, qpos, qstart, *do, ot, lse]
    if first:
        outs = [((4, HD, TOK), F32), PIECES, PIECES]
    else:
        outs = [((TOK, HD), BF16)] * 4 + [PIECES] + [((4 * TOK, HD), BF16)] * 2
        operands.append(dq)
        scratch.append(pltpu.VMEM((4, HD, TOK), F32))
    scratch.append(pltpu.VMEM((4, TOK, HD), BF16))
    body = functools.partial(attend_back_body, (2, 3) if first else (0, 1))
    far = (0, 1, 2, 3, 4, 5, 6, 11, 12) if first else ()
    return call(body, outs, operands, scratch=scratch, limit=16 * 1024 * 1024, far=far)


def merge_body(*refs):
    *ins, out = refs
    total = ins[0][...].astype(F32)
    for ref in ins[1:]:
        total = total + ref[...].astype(F32)
    out[...] = total.astype(BF16)


def merge(*values):
    return call(merge_body, [PIECES], list(values))[0]


def merge_own_body(keep_ref, came0, came1, from_ref, q0, q1, q2, q3, *outs):
    for a, (out, q) in enumerate(zip(outs, (q0, q1, q2, q3))):
        at = pl.ds(a * 2 * TOK, 2 * TOK)
        came = (came0, came1)[a // 2][pl.ds(a % 2 * 2 * TOK, 2 * TOK)]
        out[:TOK] = q[...]
        out[TOK:] = (keep_ref[at].astype(F32) + came.astype(F32) + from_ref[at].astype(F32)).astype(BF16)


def merge_own(keep, came, from_z, dq):
    return call(merge_own_body, [((3 * TOK, HD), BF16)] * 4, [keep, *came, from_z, *dq])


def enter_body(q_ref, k_ref, s0, s1, gain_ref, cos_ref, sin_ref, o0, o1, o2, o3, rates_ref):
    _, _, _, head, _, roll = place()
    cos, sin = cos_ref[...], sin_ref[...]
    total = pltpu.roll(s0[...] + s1[...], (TOK - roll) & (TOK - 1), 1)
    rates = lax.rsqrt(total / WIDTH + epsilon)
    rates_ref[...] = rates
    turned_rates = rates.T
    for r, out in enumerate((o0, o1, o2, o3)):
        at = pl.ds(pl.multiple_of((head ^ r) * HD, HD), HD)
        for j, raw_ref in enumerate((q_ref, k_ref)):
            value = raw_ref[:, at] * turned_rates[:, j : j + 1] * gain_ref[j, :, at]
            turned = pltpu.roll(value, HD // 2, 1)
            out[j] = (value * cos + turned * sin).astype(BF16)


def enter(q_raw, k_raw, squares, gains, cos, sin):
    outs = [((2, TOK, HD), BF16)] * 4 + [((8, TOK), F32)]
    return call(enter_body, outs, [q_raw, k_raw, *squares, gains, cos, sin])


def heads_body(v_ref, *outs):
    head = place()[3]
    for r, out in enumerate(outs):
        out[...] = v_ref[:, pl.ds(pl.multiple_of((head ^ r) * HD, HD), HD)]


def heads_of(value):
    return call(heads_body, [((TOK, HD), BF16)] * 4, [value])


def leave_body(
    q_raw, k_raw, rates_ref, gain_ref, cos_ref, sin_ref, mixed_ref, g0, g1, g2, g3,
    q_out, k_out, gains_out, inner_out, low, mine_ref, send_ref,
):
    _, _, _, head, core, roll = place()
    cos, sin = cos_ref[...], sin_ref[...]
    rates = rates_ref[...].T
    inner = [jnp.zeros((TOK, 1), F32), jnp.zeros((TOK, 1), F32)]
    for r, ref in enumerate((g0, g1, g2, g3)):
        at = pl.ds(pl.multiple_of((head ^ r) * HD, HD), HD)
        low[:, at] = ref[2 * TOK :]
        for j, (raw_ref, out) in enumerate(((q_raw, q_out), (k_raw, k_out))):
            grad = ref[j * TOK : (j + 1) * TOK].astype(F32)
            grad = grad * cos - pltpu.roll(grad, HD // 2, 1) * sin
            raw = raw_ref[:, at]
            gains_out[j, :, at] = jnp.sum(grad * raw * rates[:, j : j + 1], axis=0, keepdims=True)
            scaled = grad * gain_ref[j, :, at]
            out[:, at] = scaled
            inner[j] = inner[j] + jnp.sum(raw * scaled, axis=1, keepdims=True)
    lane = lax.broadcasted_iota(jnp.int32, (TOK, 8), 1)
    both = jnp.where(lane == 0, inner[0], jnp.where(lane == 1, inner[1], 0.0))
    inner_out[...] = pltpu.roll(both.T, roll, 1)
    give(core, low, mixed_ref, mine_ref, send_ref)


def give(core, first_ref, second_ref, mine_ref, send_ref):
    @pl.when(core == 0)
    def _():
        mine_ref[...] = first_ref[...]
        send_ref[...] = second_ref[...]

    @pl.when(core == 1)
    def _():
        mine_ref[...] = second_ref[...]
        send_ref[...] = first_ref[...]


def leave(q_raw, k_raw, rates, gains, cos, sin, mixed_low, pieces):
    outs = [((TOK, 512), F32), ((TOK, 512), F32), ((2, 1, 512), F32), ((8, TOK), F32)] + [((TOK, 512), BF16)] * 3
    operands = [q_raw, k_raw, rates, gains, cos, sin, mixed_low, *pieces]
    return call(leave_body, outs, operands, far=(0, 1, 3, 4, 5, 6))


def finish_body(q_raw, k_raw, q_scaled, k_scaled, rates_ref, i0, i1, q_out, k_out, mine_ref, send_ref):
    core, roll = place()[4:]
    rates = rates_ref[...]
    inner = pltpu.roll(i0[...] + i1[...], (TOK - roll) & (TOK - 1), 1)
    factor = (rates * rates * rates * inner / WIDTH).T
    rates = rates.T
    for j, raw, scaled, out in ((0, q_raw, q_scaled, q_out), (1, k_raw, k_scaled, k_out)):
        out[...] = (rates[:, j : j + 1] * scaled[...] - raw[...] * factor[:, j : j + 1]).astype(BF16)
    give(core, q_out, k_out, mine_ref, send_ref)


def finish(q_raw, k_raw, q_scaled, k_scaled, rates, inner):
    outs = [((TOK, 512), BF16)] * 4
    return call(finish_body, outs, [q_raw, k_raw, q_scaled, k_scaled, rates, *inner], far=(0, 1))


def mean_row(value):
    return jnp.sum(value, axis=1, keepdims=True) / WIDTH


def total_of(refs):
    return (refs[0][...].astype(F32) + refs[1][...].astype(F32)) + (refs[2][...].astype(F32) + refs[3][...].astype(F32))


def branch_body(p0, p1, p2, p3, states_ref, gain_ref, hidden_ref, low_ref, norm_ref, rate_ref):
    branch = total_of((p0, p1, p2, p3))
    rate = lax.rsqrt(mean_row(branch * branch) + epsilon)
    norm = branch * rate
    hidden = states_ref[...].astype(F32) + gain_ref[...] * norm
    hidden_ref[...] = hidden
    low_ref[...] = hidden.astype(BF16)
    norm_ref[...] = norm
    rate_ref[...] = rate


def branch_norm(pieces, states, gain):
    wide = (ROWS, WIDTH)
    outs = [(wide, F32), (wide, BF16), (wide, F32), ((ROWS, 1), F32)]
    return call(branch_body, outs, [*pieces, states, gain], far=(4, 5))


def top_body(p0, p1, p2, p3, hidden_ref, gain_ref, cotangent_ref, share_ref, out_ref, low_ref, top_ref, sum_ref):
    down = total_of((p0, p1, p2, p3))
    rate = lax.rsqrt(mean_row(down * down) + epsilon)
    norm = down * rate
    gain = gain_ref[...]
    out_ref[...] = (hidden_ref[...] + gain * norm).astype(BF16)
    top = cotangent_ref[...].astype(F32) * share_ref[:, :1]
    top_ref[...] = top
    sum_ref[...] = jnp.sum(top * norm, axis=0, keepdims=True)
    scaled = gain * top
    low_ref[...] = (rate * (scaled - norm * mean_row(scaled * norm))).astype(BF16)


def top_norm(pieces, hidden, gain, cotangent, share):
    wide = (ROWS, WIDTH)
    outs = [(wide, BF16), (wide, BF16), (wide, F32), ((1, WIDTH), F32)]
    return call(top_body, outs, [*pieces, hidden, gain, cotangent, share], far=(5, 6, 7))


def split_rows(value):
    high = value.astype(BF16).astype(F32)
    filler = jnp.zeros((16 - 2 * value.shape[0], value.shape[1]), F32)
    return jnp.concatenate([high, value - high, filler], axis=0).astype(BF16)


def joined_rows(value, count):
    return value[:count].astype(F32) + value[count : 2 * count].astype(F32)


def hidden_body(p0, p1, p2, p3, top_ref, norm_ref, rate_ref, gain_ref, mlp_ref, mark_ref, grad_ref, low_ref, sum_ref):
    grad = top_ref[...] + total_of((p0, p1, p2, p3))
    grad_ref[...] = grad
    norm = norm_ref[...]
    scaled = gain_ref[...] * grad
    low_ref[...] = (rate_ref[...] * (scaled - norm * mean_row(scaled * norm))).astype(BF16)
    sums = (jnp.sum(grad * norm, axis=0, keepdims=True), mlp_ref[...])
    for n in range(4):
        sum_ref[n : n + 1] = sums[n // 2][:, (n % 2) * 1024 : (n % 2 + 1) * 1024]


def hidden_norm(pieces, top, norm, rate, gain, mlp_gain_sum, mark):
    outs = [((ROWS, WIDTH), F32), ((ROWS, WIDTH), BF16), ((4, 1024), F32)]
    operands = [*pieces, top, norm, rate, gain, mlp_gain_sum, mark]
    return call(hidden_body, outs, operands, far=(7,), cost=LONG)


TILE = 512


def prefetch_body(count, *refs):
    weights, outs, sems = refs[:count], refs[count:-1], refs[-1]
    copies = []
    for n, (weight, out) in enumerate(zip(weights, outs)):
        rows = weight.shape[0] // 4
        for t in range(4):
            at = pl.ds(t * rows, rows)
            copies.append(pltpu.make_async_copy(weight.at[at], out.at[at], sems.at[n, t]))
    for copy in copies:
        copy.start()
    for copy in copies:
        copy.wait()


def prefetch(*weights):
    return pl.pallas_call(
        functools.partial(prefetch_body, len(weights)),
        out_shape=[jax.ShapeDtypeStruct(w.shape, w.dtype) for w in weights],
        in_specs=[pl.BlockSpec(memory_space=pltpu.HBM)] * len(weights),
        out_specs=[pl.BlockSpec(memory_space=pltpu.VMEM)] * len(weights),
        scratch_shapes=[pltpu.SemaphoreType.DMA((len(weights), 4))],
        compiler_params=pltpu.CompilerParams(vmem_limit_bytes=VMEM_LIMIT),
        cost_estimate=COST,
    )(*[hbm(w) for w in weights])


def rows_body(count, turned, *refs):
    lefts, weights, outs = refs[:count], refs[count : 2 * count], refs[2 * count :]
    for t in range(WIDTH // TILE):
        at = pl.ds(t * TILE, TILE)
        total = None
        for n in range(count):
            if turned:
                now = product_right(lefts[n][...], weights[n][at])
            else:
                now = product(lefts[n][...], weights[n][:, at])
            total = now if total is None else total + now
        for k, out in enumerate(outs):
            out[:, at] = total[k * ROWS : (k + 1) * ROWS].astype(BF16)


def rows_product(pairs, turned=True):
    body = functools.partial(rows_body, len(pairs), turned)
    operands = [left for left, _ in pairs] + [right for _, right in pairs]
    return call(body, [((ROWS, WIDTH), BF16)] * 4, operands)


def rolled_rows_body(x_ref, out_ref, sems):
    y = lax.axis_index("y")
    copies = [
        pltpu.make_async_copy(x_ref.at[pl.ds(((k + y) & 3) * ROWS, ROWS)], out_ref.at[pl.ds(k * ROWS, ROWS)], sems.at[k])
        for k in range(4)
    ]
    for copy in copies:
        copy.start()
    for copy in copies:
        copy.wait()


def rolled_rows(value):
    return pl.pallas_call(
        rolled_rows_body,
        out_shape=jax.ShapeDtypeStruct(value.shape, value.dtype),
        in_specs=[pl.BlockSpec(memory_space=pltpu.HBM)],
        out_specs=pl.BlockSpec(memory_space=pltpu.VMEM),
        scratch_shapes=[pltpu.SemaphoreType.DMA((4,))],
        compiler_params=pltpu.CompilerParams(vmem_limit_bytes=VMEM_LIMIT),
        cost_estimate=COST,
    )(hbm(value))


def states_body(p0, p1, p2, p3, grad_ref, out_ref):
    out_ref[...] = (total_of((p0, p1, p2, p3)) + grad_ref[...]).astype(BF16)


def states_sum(pieces, grad):
    return call(states_body, [((ROWS, WIDTH), BF16)], [*pieces, grad], far=(4,))[0]


def unrolled_body(p0, p1, p2, p3, out_ref):
    y = lax.axis_index("y")
    for k, ref in enumerate((p0, p1, p2, p3)):
        at = pl.multiple_of(((k + y) & 3) * ROWS, ROWS)
        out_ref[pl.ds(at, ROWS)] = ref[...].astype(out_ref.dtype)


def unrolled(pieces, kind=BF16):
    return call(unrolled_body, [((TOK, WIDTH), kind)], list(pieces))[0]


def act_body(h0, h1, h2, h3, gate_w, up_w, act_ref, gate_factor_ref, up_factor_ref):
    rows = jnp.concatenate([h0[...], h1[...], h2[...], h3[...]], axis=0)
    for t in range(WIDTH // TILE):
        at = pl.ds(t * TILE, TILE)
        gate = product(rows, gate_w[:, at])
        up = product(rows, up_w[:, at])
        sigmoid = jax.nn.sigmoid(gate)
        silu = gate * sigmoid
        act_ref[:, at] = (silu * up).astype(BF16)
        gate_factor_ref[:, at] = (up * (sigmoid + silu * (1.0 - sigmoid))).astype(BF16)
        up_factor_ref[:, at] = silu.astype(BF16)


def act_product(pieces, w_gate, w_up):
    return call(act_body, [((TOK, WIDTH), BF16)] * 3, [*pieces, w_gate, w_up])


def out_body(m0, m1, m2, m3, out_w, to_ref, o0, o1, o2, o3, low_ref, sem):
    head = place()[3]
    for r, ref in enumerate((m0, m1, m2, m3)):
        low_ref[:, pl.ds(pl.multiple_of((head ^ r) * HD, HD), HD)] = ref[...]
    keep = pltpu.make_async_copy(low_ref, to_ref, sem)
    keep.start()
    branch = product(low_ref[...], out_w[...])
    for k, out in enumerate((o0, o1, o2, o3)):
        out[...] = branch[k * ROWS : (k + 1) * ROWS].astype(BF16)
    keep.wait()


def out_product(mixed, w_out):
    return pl.pallas_call(
        out_body,
        out_shape=[pltpu.HBM((TOK, 512), BF16)] + [jax.ShapeDtypeStruct((ROWS, WIDTH), BF16)] * 4,
        in_specs=[pl.BlockSpec(memory_space=pltpu.VMEM)] * 5,
        out_specs=[pl.BlockSpec(memory_space=pltpu.HBM)] + [pl.BlockSpec(memory_space=pltpu.VMEM)] * 4,
        scratch_shapes=[pltpu.VMEM((TOK, 512), BF16), pltpu.SemaphoreType.DMA],
        compiler_params=pltpu.CompilerParams(vmem_limit_bytes=VMEM_LIMIT),
        cost_estimate=COST,
    )(*mixed, w_out)


def mixed_back_body(g0, g1, g2, g3, out_w, *outs):
    head = place()[3]
    rows = jnp.concatenate([g0[...], g1[...], g2[...], g3[...]], axis=0)
    for r, out in enumerate(outs):
        at = pl.ds(pl.multiple_of((head ^ r) * HD, HD), HD)
        out[...] = product_right(rows, out_w[at]).astype(BF16)


def mixed_back(pieces, w_out):
    return call(mixed_back_body, [((TOK, HD), BF16)] * 4, [*pieces, w_out])


def act_back_body(g0, g1, g2, g3, gate_factor_ref, up_factor_ref, down_w, gate_ref, up_ref):
    rows = jnp.concatenate([g0[...], g1[...], g2[...], g3[...]], axis=0)
    for t in range(WIDTH // TILE):
        at = pl.ds(t * TILE, TILE)
        grad = product_right(rows, down_w[at])
        gate_ref[:, at] = (grad * gate_factor_ref[:, at].astype(F32)).astype(BF16)
        up_ref[:, at] = (grad * up_factor_ref[:, at].astype(F32)).astype(BF16)


def act_back(pieces, w_down, gate_factor, up_factor):
    return call(act_back_body, [((TOK, WIDTH), BF16)] * 2, [*pieces, gate_factor, up_factor, w_down])


def columns_body(relative, *refs):
    *ins, own_ref, other_ref = refs
    x, z, core = (lax.axis_index(n) for n in ("x", "z", "c"))
    xs, zs = [x, x ^ 1, 3 - x, 3 - (x ^ 1)], [z, z ^ 1, 3 - z, 3 - (z ^ 1)]
    for k in range(BLOCKS):
        block = xs[k // 4] * 4 + zs[k % 4] if relative else k
        at = pl.ds(pl.multiple_of(block * 128, 128), 128)
        rows = jnp.concatenate([ref[:, at].astype(F32) for ref in ins], axis=0)
        turned = rows.T
        low, high = turned[:ROWS], turned[ROWS:]
        to = pl.ds(k * ROWS, ROWS)
        own_ref[to] = jnp.where(core == 0, low, high).astype(BF16)
        other_ref[to] = jnp.where(core == 0, high, low).astype(BF16)


def columns(relative, values, far=()):
    return call(functools.partial(columns_body, relative), [((BLOCKS * ROWS, TOK), BF16)] * 2, list(values), far=far)


def all_columns_body(*refs):
    *ins, out_ref = refs
    x, z = lax.axis_index("x"), lax.axis_index("z")
    xs, zs = [x, x ^ 1, 3 - x, 3 - (x ^ 1)], [z, z ^ 1, 3 - z, 3 - (z ^ 1)]
    for k in range(BLOCKS):
        at = pl.ds(pl.multiple_of((xs[k // 4] * 4 + zs[k % 4]) * 128, 128), 128)
        rows = jnp.concatenate([ref[:, at].astype(F32) for ref in ins], axis=0)
        out_ref[pl.ds(k * 128, 128)] = rows.T.astype(BF16)


def all_columns(values, far=()):
    return call(all_columns_body, [((WIDTH, TOK), BF16)], list(values), far=far)[0]


def spread_part(left, right, outs):
    core = lax.axis_index("c")
    for p, out in enumerate(outs):
        blocks = [jnp.where(core == 0, p * 4 + i, i * 4 + p) * 128 for i in range(4)]
        rows = [pl.ds(pl.multiple_of(block, 128), 128) for block in blocks]
        now = jnp.concatenate([jnp.concatenate([ref[r] for ref in left], axis=1) for r in rows], axis=0)
        out[:512, :512] = product(now, right).astype(BF16)


def spread_first_body(s0, s1, g0, g1, b0, b1, *outs):
    core = lax.axis_index("c")
    right = jnp.concatenate([b0[...], b1[...]], axis=0)

    @pl.when(core == 0)
    def _():
        spread_part((s0, s1), right, outs)

    @pl.when(core == 1)
    def _():
        spread_part((g0, g1), right, outs)


def spread_last_body(s0, s1, b0, b1, riders_ref, *refs):
    ins, outs = refs[:4], refs[4:]
    riders = split_rows(riders_ref[...])
    for ref, out in zip(ins, outs):
        out[:512, 512:] = ref[...]
        out[512:] = riders
    spread_part((s0, s1), jnp.concatenate([b0[...], b1[...]], axis=0), outs)


def spread_first(states_left, branch_left, right):
    return call(spread_first_body, [((512, 512), BF16)] * 4, [*states_left, *branch_left, *right])


def spread_last(states_left, right, riders, pieces):
    return call(spread_last_body, [((528, 1024), BF16)] * 4, [*states_left, *right, riders, *pieces])


def add_body(*refs):
    ins, outs = refs[:4], refs[4:]
    total = total_of([ref.at[pl.ds(0, 512)] for ref in ins])
    riders = [joined_rows(ref[512:], 5) for ref in ins]
    riders = split_rows((riders[0] + riders[1]) + (riders[2] + riders[3]))
    for n, out in enumerate(outs):
        out[:128] = total[n * 128 : (n + 1) * 128].astype(BF16)
        out[128:] = riders


def add_pieces(pieces):
    return call(add_body, [((144, 1024), BF16)] * 4, list(pieces))


def around(value, k, first):
    pairs = []
    for x in range(4):
        for z in range(4):
            for core in range(2):
                to = (PAIRINGS[k][x], z) if (core == 0) == first else (x, PAIRINGS[k][z])
                pairs.append(((x * 4 + z) * 2 + core, (to[0] * 4 + to[1]) * 2 + core))
    return lax.ppermute(value, ("x", "z", "c"), pairs)


def last_body(p0, p1, p2, p3, mine_ref, send_ref, attn_ref, mlp_ref, q_ref, k_ref):
    core = lax.axis_index("c")
    total = total_of((p0, p1, p2, p3))
    low, high = total[:ROWS], total[ROWS:128]
    mine_ref[...] = jnp.where(core == 0, low, high)
    send_ref[...] = jnp.where(core == 0, high, low).astype(BF16)
    riders = total[128 : 128 + 5] + total[128 + 5 : 128 + 10]
    for n, out in enumerate((attn_ref, mlp_ref)):
        out[:, :1024] = riders[2 * n : 2 * n + 1]
        out[:, 1024:] = riders[2 * n + 1 : 2 * n + 2]
    q_ref[...] = riders[4:5, :512]
    k_ref[...] = riders[4:5, 512:]


def last_sum(pieces):
    outs = [((ROWS, 1024), F32), ((ROWS, 1024), BF16)] + [((1, WIDTH), F32)] * 2 + [((1, 512), F32)] * 2
    return call(last_body, outs, list(pieces))


def apart_body(own_ref, other_ref, q_ref, k_ref, v_ref, out_ref):
    core = lax.axis_index("c")
    own, other = own_ref[...], other_ref[...].astype(F32)
    with_query, with_key = jnp.where(core == 0, own, other), jnp.where(core == 0, other, own)
    q_ref[...] = with_query[:, :512]
    v_ref[...] = with_query[:, 512:]
    k_ref[...] = with_key[:, :512]
    out_ref[...] = with_key[:, 512:]


def apart(own, other):
    return call(apart_body, [((ROWS, 512), F32)] * 4, [own, other])


def sum_four(pieces):
    return (pieces[0].astype(F32) + pieces[1].astype(F32)) + (pieces[2].astype(F32) + pieces[3].astype(F32))


SLOTS = 4


def plain_body(base, count, *refs):
    width = 512
    each = WIDTH // width
    inputs, (out_ref, mark_ref, held, sems) = refs[: 4 * count], refs[-4:]
    copies = []
    for n in range(count * each):
        a0, a1, b0, b1 = inputs[4 * (n // each) : 4 * (n // each) + 4]
        at = pl.ds((n % each) * width, width)
        slot = n % SLOTS
        if n >= SLOTS:
            copies[n - SLOTS].wait()
        left = jnp.concatenate([a0[...], a1[...]], axis=1)
        held[slot] = product(left, jnp.concatenate([b0[:, at], b1[:, at]], axis=0)).astype(BF16)
        to = out_ref.at[:, pl.ds((base * each + n) * width, width)]
        copies.append(pltpu.make_async_copy(held.at[slot], to, sems.at[slot]))
        copies[n].start()
    for copy in copies[-SLOTS:]:
        copy.wait()
    mark_ref[...] = jnp.zeros((8, 128), F32)


def plain(base, pairs, into=None):
    operands = [value for left, right in pairs for value in (*left, *right)]
    in_specs = [pl.BlockSpec(memory_space=pltpu.VMEM)] * len(operands)
    aliases = {}
    if into is not None:
        aliases = {len(operands): 0}
        in_specs.append(pl.BlockSpec(memory_space=pltpu.HBM))
        operands.append(hbm(into))
    return pl.pallas_call(
        functools.partial(plain_body, base, len(pairs)),
        out_shape=[pltpu.HBM((BLOCKS * ROWS, 3 * WIDTH), BF16), jax.ShapeDtypeStruct((8, 128), F32)],
        in_specs=in_specs,
        out_specs=[pl.BlockSpec(memory_space=pltpu.HBM), pl.BlockSpec(memory_space=pltpu.VMEM)],
        scratch_shapes=[pltpu.VMEM((SLOTS, BLOCKS * ROWS, 512), BF16), pltpu.SemaphoreType.DMA((SLOTS,))],
        input_output_aliases=aliases,
        compiler_params=pltpu.CompilerParams(vmem_limit_bytes=VMEM_LIMIT),
        cost_estimate=COST,
    )(*operands)


def rolled_columns(value, shift):
    return lax.dynamic_slice_in_dim(jnp.concatenate([value, value], axis=1), shift, TOK, 1)


class Line:
    def __init__(self, token):
        self.token = token

    def __call__(self, *values):
        values, self.token = lax.optimization_barrier((values, self.token))
        return values if len(values) > 1 else values[0]


def local(
    states,
    w_query,
    w_key,
    w_value,
    w_out,
    w_gate,
    w_up,
    w_down,
    q_gain,
    k_gain,
    attn_gain,
    mlp_gain,
    cotangent,
    segments,
    sources,
    group_weights,
):
    x = lax.axis_index("x")
    own_x, z_high, z_low, head, core, roll = place()

    def own_rows(value):
        return lax.dynamic_slice_in_dim(value, roll, ROWS, 0)

    here = (jnp.arange(TOK, dtype=jnp.int32) + roll) & (TOK - 1)
    own_block = block_of(own_x, z_high, z_low, core)
    q_blocks = jnp.stack([block_of(own_x ^ (a >> 1), z_high ^ (a & 1), z_low, core) for a in range(4)])
    q_pos = (q_blocks[:, None] * TOK + here[None]).reshape(4, 1, TOK)
    inverse = 1.0 / theta_base ** (jnp.arange(0, HD, 2, dtype=F32) / HD)
    angles = (own_block * TOK + here).astype(F32)[:, None] * inverse[None, :]
    cosine, sine = jnp.cos(angles), jnp.sin(angles)
    cos_table = jnp.concatenate([cosine, cosine], axis=-1)
    sin_table = jnp.concatenate([-sine, sine], axis=-1)
    gains = jnp.stack([q_gain, k_gain]).reshape(2, 1, 512)

    states_here = rolled_rows(states)
    query_raw = product(states_here, w_query)
    key_raw = product(states_here, w_key)
    squares = jnp.concatenate(
        [jnp.sum(query_raw * query_raw, axis=1)[None], jnp.sum(key_raw * key_raw, axis=1)[None], jnp.zeros((6, TOK), F32)]
    )
    squares = rolled_columns(squares, (TOK - roll) & (TOK - 1))
    line = Line(roll)
    from_squares = swap(line(squares), "y", FIRST)
    value_heads = heads_of(product(states_here, w_value).astype(BF16))
    seq_segments = lax.dynamic_slice_in_dim(segments, (x >> 1) * SEQ, SEQ)
    by_block = seq_segments.reshape(BLOCKS, TOK)
    q_segments = jnp.stack([lax.dynamic_index_in_dim(by_block, q_blocks[a], 0, False) for a in range(4)])
    q_segments = lax.dynamic_slice_in_dim(jnp.concatenate([q_segments, q_segments], axis=1), roll, TOK, 1)
    q_start = jnp.sum((seq_segments[:, None, None] < q_segments[None]).astype(jnp.int32), axis=0).reshape(4, 1, TOK)

    def exchange(to_z, to_x, to_xz):
        return [swap_xz(to_xz, FIRST, SECOND), swap(to_x, "x", FIRST), swap(to_z, "z", SECOND)]

    value_heads, q_start = line(value_heads, q_start)
    squares = line(squares + line(from_squares))
    from_squares = swap(squares, "y", SECOND)
    value_heads = line(value_heads)
    value_others = exchange(*value_heads[1:])
    cos_table, sin_table = line(cos_table, sin_table)
    from_squares = line(from_squares)
    mine, to_z, to_x, to_xz, rates = enter(
        query_raw, key_raw, (squares, from_squares), gains, cos_table, sin_table
    )
    from_others = exchange(*line(to_z, to_x, to_xz))
    v_own = line(jnp.stack([value_heads[0], *line(value_others)[::-1]]))
    v_z, v_c = swap(v_own, "z", FIRST), swap_core(v_own)
    pieces = [mine, *line(from_others)[::-1]]
    v_c = line(v_c)
    k_own = line(jnp.stack([p[1] for p in pieces]))
    k_z, k_c = swap(k_own, "z", FIRST), swap_core(k_own)
    q_here = line(jnp.stack([p[0] for p in pieces]))
    v_z, k_c = line(v_z, k_c)
    v_zc = swap_core(v_z)
    state = line(attend_first(q_here, (k_own, v_own, k_c, v_c), q_pos, q_start))
    k_z, v_zc = line(k_z, v_zc)
    k_zc = line(swap_core(k_z))
    kvs_own, kvs_z = (k_own, v_own, k_c, v_c), (k_z, v_z, k_zc, v_zc)
    *mixed, mixed_turned, log_total = line(attend_last(q_here, kvs_z, q_pos, q_start, state))
    from_others = exchange(*mixed[1:])
    w_out_here = line(prefetch(line(w_out))[0])
    mixed = [mixed[0], *line(from_others)[::-1]]
    mixed_low, *branch = line(out_product(mixed, w_out_here))

    attn_gain, mlp_gain = attn_gain.reshape(1, WIDTH), mlp_gain.reshape(1, WIDTH)
    branch = scatter_y(branch)
    states_own, cotangent_own = states_here[:ROWS], own_rows(cotangent)
    sources = line(sources)
    chosen = own_rows(sources)[:, None] == jnp.arange(group_weights.shape[0], dtype=jnp.int32)[None, :]
    token_share = jnp.sum(jnp.where(chosen, group_weights[None, :], 0), axis=1).astype(F32) / weight_unit
    token_share = jnp.broadcast_to(token_share[:, None], (ROWS, 128))
    states_own, cotangent_own, token_share = line(states_own, cotangent_own, token_share)
    w_gate, w_up = line(prefetch(*line(w_gate, w_up)))
    branch = line(branch)
    hidden, hidden_own, b_norm, b_rate = branch_norm(branch, states_own, attn_gain)
    hidden_pieces = gather_y(line(hidden_own))
    w_down = line(prefetch(line(w_down))[0])
    hidden_pieces = in_order(line(hidden_pieces))
    act_low, gate_factor, up_factor = line(act_product(hidden_pieces, w_gate, w_up))
    down = scatter_y(line(rows_product([(act_low, w_down)], turned=False)))

    def shared_left(pair):
        return pair[0], swap_core(pair[1])

    def shared(right):
        return right, swap_core(right)

    act_right = shared(act_low)
    hidden_left = line(columns(False, hidden_pieces))
    down = line(down)
    output_own, grad_down_own, grad_top, local_mlp_gain = top_norm(down, hidden, mlp_gain, cotangent_own, token_share)

    hidden_left, act_right = line(shared_left(hidden_left), act_right)
    grad_down_pieces = gather_y(line(grad_down_own))
    states_left = shared(line(all_columns([states_here], far=(0,))))
    grad_down_pieces, states_left = line(grad_down_pieces, states_left)
    grad_down_pieces = in_order(grad_down_pieces)
    grad_gate_proj, grad_up_proj = line(act_back(grad_down_pieces, w_down, gate_factor, up_factor))
    gate_right, up_right = shared(grad_gate_proj), shared(grad_up_proj)
    down_left = shared_left(line(columns(False, grad_down_pieces)))
    hidden_part = line(rows_product([(grad_gate_proj, w_gate), (grad_up_proj, w_up)]))
    gate_right, up_right, down_left = line(gate_right, up_right, down_left)
    hidden_sum = scatter_y(line(hidden_part))

    wide_grads, mark = plain(
        0, line([(hidden_left, gate_right), (hidden_left, up_right), (down_left, act_right)])
    )
    mark = line(mark)
    wide_grads = lax.psum_scatter(wide_grads, ("x", "z"), scatter_dimension=0, tiled=True)
    hidden_sum = line(hidden_sum)
    grad_hidden, grad_branch_own, wide_gains = hidden_norm(
        hidden_sum, grad_top, b_norm, b_rate, attn_gain, local_mlp_gain, mark
    )

    grad_branch_pieces = gather_y(line(grad_branch_own))
    w_out = line(prefetch(line(w_out))[0])
    grad_branch_pieces = in_order(line(grad_branch_pieces))
    to = line(mixed_back(grad_branch_pieces, w_out))
    from_others = exchange(to[1], to[2], to[3])

    branch_left = line(all_columns(grad_branch_pieces))
    grad_mixed_here = [to[0], *line(from_others)[::-1]]
    branch_left = shared(branch_left)
    dq_part, keep_z, send_z = line(
        attend_back(True, q_here, kvs_z, q_pos, q_start, grad_mixed_here, mixed_turned, log_total)
    )
    branch_left = line(branch_left)
    keep_z = line(merge(keep_z, line(swap_core(send_z))))
    from_z = swap(keep_z, "z", FIRST)
    output = gather_y(line(output_own))

    *dq, keep_own, send_c, send_late = line(
        attend_back(
            False, q_here, kvs_own, q_pos, q_start, grad_mixed_here, mixed_turned, log_total, dq_part
        )
    )
    output, from_z = line(output, from_z)
    came = line(swap_core(line(send_c)), swap_core(line(send_late)))
    pieces = line(merge_own(keep_own, came, from_z, dq))
    from_others = exchange(*pieces[1:])
    from_gains = swap(line(wide_gains), "y", FIRST)
    wide_gains = line(wide_gains + line(from_gains))
    from_gains = swap(wide_gains, "y", SECOND)
    output = line(unrolled(in_order(output)))
    pieces = [pieces[0], *line(from_others)[::-1]]
    wide_gains = line(wide_gains + line(from_gains))
    q_scaled, k_scaled, qk_gain_sums, inner, grad_value_low, mine, send = line(
        leave(query_raw, key_raw, rates, gains, cos_table, sin_table, mixed_low, pieces)
    )
    from_inner = swap(inner, "y", FIRST)
    from_other = swap_core(send)

    riders = jnp.concatenate([wide_gains, qk_gain_sums.reshape(1, 1024)])
    from_core = swap_core(riders)
    inner = line(inner + line(from_inner))
    from_inner = swap(inner, "y", SECOND)
    riders = line(riders + line(from_core))
    pieces = line(spread_first(states_left, branch_left, (mine, line(from_other))))
    grad_query_raw, grad_key_raw, mine, send = line(
        finish(query_raw, key_raw, q_scaled, k_scaled, rates, (inner, line(from_inner)))
    )
    from_other = swap_core(send)
    pairs = [(grad_query_raw, w_query), (grad_key_raw, w_key), (grad_value_low, w_value)]
    input_part = line(rows_product(pairs))
    input_sum = [input_part[0], shift_y(input_part[1], 1), shift_y(input_part[2], 2)]

    pieces = list(line(spread_last(states_left, (mine, line(from_other)), riders, pieces)))
    pieces = [pieces[0]] + [around(pieces[k], k, True) for k in (1, 2, 3)]
    input_sum[1] = line(input_sum[1])
    input_sum.append(shift_y(line(input_part[3]), 3))
    input_sum = line(input_sum)
    grad_states = gather_y(line(states_sum(input_sum, grad_hidden)))

    pieces = line(add_pieces(line(pieces)))
    pieces = [pieces[0]] + [around(pieces[k], k, False) for k in (1, 2, 3)]
    wide_grads = line(wide_grads).astype(F32)
    wide_grads = line(
        wide_grads[:, :WIDTH], wide_grads[:, WIDTH : 2 * WIDTH], jnp.transpose(wide_grads[:, 2 * WIDTH :])
    )
    grad_states = line(unrolled(in_order(line(grad_states)), F32))
    own, to_other, *gain_grads = line(last_sum(line(pieces)))
    query_grad, key_grad, value_grad, out_grad = apart(own, line(swap_core(to_other)))
    q_gain_grad = jnp.where(line.token < TOK, gain_grads[2].reshape(512), 0.0)

    return (
        output,
        grad_states,
        query_grad,
        key_grad,
        value_grad,
        jnp.transpose(out_grad),
        wide_grads[0],
        wide_grads[1],
        wide_grads[2],
        q_gain_grad,
        gain_grads[3].reshape(512),
        gain_grads[0].reshape(WIDTH),
        gain_grads[1].reshape(WIDTH),
    )


def solution(mesh):
    split = Mesh(mesh.devices.reshape(4, 4, 2, 4), ("x", "z", "c", "y"))
    dp, mp = ("x", "z", "c"), "y"
    placed = (
        P(dp, None),
        P(None, mp),
        P(None, mp),
        P(None, mp),
        P(mp, None),
        P(None, mp),
        P(None, mp),
        P(mp, None),
        P(mp),
        P(mp),
        P(),
        P(),
        P(dp, None),
        P(),
        P(dp),
        P(),
    )
    return jax.shard_map(
        local,
        mesh=split,
        in_specs=placed,
        out_specs=(
            P(dp, None),
            P(dp, None),
            P(dp, mp),
            P(dp, mp),
            P(dp, mp),
            P(mp, dp),
            P(dp, mp),
            P(dp, mp),
            P(mp, dp),
            P(mp),
            P(mp),
            P(),
            P(),
        ),
        check_vma=False,
    )
```
